256 devices in a mesh: px: 8 (over z), py: 32 (over y, x, core).
Axes of the slice: x: 4, y: 4, z: 8, core: 2. Of those that a mesh axis runs over, the one named last changes fastest.
Arguments:
- current_state: float32 [5, 125, 262144], P(None, None, ('px', 'py')), may hold values from -6 to 6
- state_old: float32 [5, 125, 262144], P(None, None, ('px', 'py')), may hold values from -6 to 6
- jacobian: float32 [262144], P(('px', 'py')), may hold values from 0.5 to 2
- volume_operator_list: float32 [3, 125, 125], replicated, may hold values from -0.3125 to 0.3125
- flux_jacobian_list: float32 [3, 5, 5], replicated, may hold values from -2.5 to 2.5
- penalty: float32 [5], replicated, may hold values from 0.5 to 2
- cut_owner: int32 [10240, 1], P(('px', 'py')), may hold values from 0 to 31; in each aligned block of 40 rows (0 to 39, 40 to 79, ...) at most 2 rows name the same one
- cut_element: int32 [10240], P(('px', 'py')), may hold values from 0 to 1023
- cut_mass: float32 [10240, 125, 125], P(('px', 'py')), may hold values from -0.5 to 0.5
- cut_operator: float32 [10240, 125, 125], P(('px', 'py')), may hold values from -0.5 to 0.5
- body_holder_index: int32 [48], P('px'), may hold values from 0 to 31
- body_points: float32 [1536, 3, 128], P(('px', 'py')), may hold values from -1 to 1
- body_normals: float32 [1536, 3, 128], P(('px', 'py')), may hold values from -6 to 6
- body_weights: float32 [1536, 128], P(('px', 'py')), may hold values from 0.01 to 0.1
- covered: int32 [1536, 16], P(('px', 'py')), may hold values from 0 to 1023
Outputs:
- residual: float32 [5, 125, 262144], P(None, None, ('px', 'py'))
The draws below stay inside these ranges and needn't reach their ends.
Inputs may be any that keep to these rules, and one draw needn't show every extreme that they name: `cut_owner`: among the 40 rows of one device no owner is named by more than 2 rows, a bound that some block reaches. Owners are py indices within the same slab. `cut_element`: several cut blocks may belong to one element; their terms add. `body_holder_index`: only the slot of the owning device is read for each body. `covered`: an element may be listed more than once; its terms add.
All inputs are finite; a program needn't handle non-finite values.
Results may differ from the reference program's by a relative error of at most 0.0001.
Values sent between devices are 32-bit elements; how exact they have to be, the bound alone decides.
A program may use at most 128 MiB of HBM per device.

```python
import math
import jax
import jax.numpy as jnp
import numpy as np
from jax import lax

DEGREE = 4
MODES = 125
FACE = 25
NVAR = 5
ELEM_DEV = 1024
LAYERS = 8
COLS = 128
ELEMS = 262144
CUT_DEV = 40
CUTS = 10240
CAP = 2
BODIES = 6
OWNERS = 48
BODY_SLOTS = 1536
QPTS = 128
COVERED = 16
N_PX = 8
N_PY = 32


def plant(entries, own_key, smallest, largest):
    longest = entries.shape.index(max(entries.shape))
    spots = []
    for shift in (0, 1):
        where = [jax.random.randint(jax.random.fold_in(own_key, axis), (), 0, length) for axis, length in enumerate(entries.shape)]
        where[longest] = (where[longest] + shift) % entries.shape[longest]
        spots.append(tuple(where))
    return entries.at[spots[0]].set(smallest).at[spots[1]].set(largest)


def level_of(stream_key, dims, split, low, top_value):
    loudness = 1.0
    for dim, shards_of in split:
        heights = jax.random.uniform(jax.random.fold_in(jax.random.fold_in(stream_key, 6), dim), (shards_of,), jnp.float32, low / len(split), top_value / len(split))
        loudness = loudness * jnp.repeat(jnp.exp(heights), dims[dim] // shards_of).reshape((-1,) + (1,) * (len(dims) - 1 - dim))
    return loudness


def shared_out(stream_key, own, number, rows, amount, top, limit, slope):
    ranking = jax.random.permutation(stream_key, amount)
    packed, usual = load_shares(amount, rows * top, limit, slope, True), load_shares(amount, rows * top, limit, slope, False)
    places = jnp.arange(amount)

    def named(sizes, offset_by):
        used = int((sizes > 0).sum())
        fixed = max(1, used // 4)
        moved = fixed + (places - fixed + offset_by * (used - fixed)) % max(1, amount - fixed)
        return jnp.zeros((amount,), jnp.int32).at[ranking[jnp.where(places < fixed, places, moved)]].set(jnp.asarray(sizes, jnp.int32))

    sizes = jnp.where(number % 4 == 0, named(packed, number // 4), named(usual, number - number // 4 - 1))
    mixed = jax.random.permutation(jax.random.fold_in(own, 3), amount)
    giver, receiver = mixed[0:amount // 2 * 2:2], mixed[1:amount // 2 * 2:2]
    room = jnp.minimum(sizes[giver] - 1, limit - sizes[receiver]) // 2
    room = jnp.where((giver == ranking[0]) | (receiver == ranking[0]) | (sizes[receiver] == 0), 0, jnp.maximum(room, 0))
    moved = jax.random.randint(jax.random.fold_in(own, 4), (amount // 2,), 0, 1 << 20) % (room + 1)
    sizes = sizes.at[giver].add(-moved).at[receiver].add(moved)
    items = jnp.searchsorted(jnp.cumsum(sizes), jnp.arange(rows * top), side="right").astype(jnp.int32)
    listing = items.reshape(top, rows).T
    listing = listing[jax.random.permutation(jax.random.fold_in(own, 1), rows)]
    offset_by = jax.random.randint(jax.random.fold_in(own, 2), (rows, 1), 0, top)
    return jnp.take_along_axis(listing, (jnp.arange(top)[None, :] + offset_by) % top, axis=1)


def load_shares(count, total, reach, skew, full):
    weights = [(1 << 20) // math.isqrt(grade ** skew) + 1 for grade in range(1, count + 1)]
    largest = reach if full else min(reach, max(-(-total // count), total * weights[0] // sum(weights)))
    least = 1 if total - largest >= count - 1 else 0
    counts, spare = [largest] + [least] * (count - 1), total - largest - least * (count - 1)
    while spare > 0:
        movable = [i for i in range(1, count) if counts[i] < largest] or [i for i in range(1, count) if counts[i] < reach]
        whole, budget = sum([weights[i] for i in movable]), spare
        for i in movable:
            addition = min(reach - counts[i], max(1, budget * weights[i] // whole), spare)
            counts[i] = counts[i] + addition
            spare = spare - addition
    return np.array(counts)


def centred(key, dims, scale, most, shards=(), held_as=jnp.bfloat16):
    level = level_of(key, dims, shards, -0.22, 0.18) if shards else 1.0
    array = jax.random.normal(key, dims, jnp.float32) * scale * level
    return jnp.minimum(jnp.maximum(array, -most), most).astype(held_as)


def setup_inputs(seed: int = 0) -> dict:
    splits = jax.random.split(jax.random.key(seed), 16)
    current_state = centred(splits[0], (NVAR, MODES, ELEMS), 1.0, 6.0, ((2, 256),), jnp.float32)
    state_old = centred(splits[1], (NVAR, MODES, ELEMS), 1.0, 6.0, ((2, 256),), jnp.float32)
    jacobian = jnp.clip(jnp.exp(math.log(2.0) - 1.3862944 * jax.random.uniform(splits[2], (ELEMS,), jnp.float32) ** level_of(splits[2], (ELEMS,), ((0, 256),), -0.2, 0.2)), 0.5, 2.0)
    volume_operator_list = centred(splits[3], (3, MODES, MODES), (3 * MODES) ** -0.5, 0.3125, (), jnp.float32)
    flux_jacobian_list = centred(splits[4], (3, NVAR, NVAR), NVAR ** -0.5, 2.5, (), jnp.float32)
    penalty = jnp.clip(jnp.exp(jax.random.uniform(splits[5], (NVAR,), jnp.float32, math.log(0.5), math.log(2.0))), 0.5, 2.0)
    cut_owner_keys = jax.random.split(jax.random.fold_in(splits[6], 1), CUTS // CUT_DEV)
    cut_owner_turns = jax.random.permutation(jax.random.fold_in(splits[6], 3), CUTS // CUT_DEV)
    cut_owner = jax.vmap(lambda own, number: shared_out(jax.random.fold_in(splits[6], 2), own, number, CUT_DEV, N_PY, 1, CAP, 2))(cut_owner_keys, cut_owner_turns).reshape((CUTS, 1))
    cut_element = plant(jax.random.randint(splits[7], (CUTS,), 0, ELEM_DEV), jax.random.fold_in(splits[7], 1), 0, ELEM_DEV - 1).astype(jnp.int32)
    cut_mass = centred(splits[8], (CUTS, MODES, MODES), MODES ** -0.5, 0.5, ((0, 256),), jnp.float32)
    cut_operator = centred(splits[9], (CUTS, MODES, MODES), MODES ** -0.5, 0.5, ((0, 256),), jnp.float32)
    body_holder_index = plant(jax.random.randint(splits[10], (OWNERS,), 0, N_PY), jax.random.fold_in(splits[10], 1), 0, N_PY - 1).astype(jnp.int32)
    body_points = jnp.clip(jax.random.uniform(splits[11], (BODY_SLOTS, 3, QPTS), jnp.float32, -1.0, 1.0) * level_of(splits[11], (BODY_SLOTS, 3, QPTS), ((0, 256),), -0.4, 0.0), -1.0, 1.0)
    body_normals = centred(splits[12], (BODY_SLOTS, 3, QPTS), 1.0, 6.0, ((0, 256),), jnp.float32)
    body_weights = jnp.clip(jnp.exp(math.log(0.1) - 2.3025851 * jax.random.uniform(splits[13], (BODY_SLOTS, QPTS), jnp.float32) ** level_of(splits[13], (BODY_SLOTS, QPTS), ((0, 256),), -0.2, 0.2)), 0.01, 0.1)
    covered = plant(jax.random.randint(splits[14], (BODY_SLOTS, COVERED), 0, ELEM_DEV), jax.random.fold_in(splits[14], 1), 0, ELEM_DEV - 1).astype(jnp.int32)
    return dict(current_state=current_state, state_old=state_old, jacobian=jacobian, volume_operator_list=volume_operator_list, flux_jacobian_list=flux_jacobian_list, penalty=penalty, cut_owner=cut_owner, cut_element=cut_element, cut_mass=cut_mass, cut_operator=cut_operator, body_holder_index=body_holder_index, body_points=body_points, body_normals=body_normals, body_weights=body_weights, covered=covered)


TOP_PRECISION = lax.Precision.HIGHEST


def mode_weights():
    degree_one = DEGREE + 1
    mode_index = jnp.arange(degree_one ** 3, dtype=jnp.int32)
    degree_x = (mode_index // (degree_one * degree_one)).astype(jnp.float32)
    degree_y = ((mode_index // degree_one) % degree_one).astype(jnp.float32)
    degree_z = (mode_index % degree_one).astype(jnp.float32)
    return 8.0 / ((2.0 * degree_x + 1.0) * (2.0 * degree_y + 1.0) * (2.0 * degree_z + 1.0))


def legendre_table(coords):
    poly_table = [jnp.ones_like(coords), coords]
    for degree_now in range(1, DEGREE):
        poly_table.append(((2.0 * degree_now + 1.0) * coords * poly_table[degree_now] - degree_now * poly_table[degree_now - 1]) / (degree_now + 1.0))
    return jnp.stack(poly_table[:DEGREE + 1], axis=0)


def basis_rows(points):
    along_x = legendre_table(points[..., 0, :])
    along_y = legendre_table(points[..., 1, :])
    along_z = legendre_table(points[..., 2, :])
    basis_vals = along_x[:, None, None] * along_y[None, :, None] * along_z[None, None, :]
    leading = points.shape[:-2]
    basis_vals = basis_vals.reshape(((DEGREE + 1) ** 3,) + leading + (points.shape[-1],))
    return jnp.moveaxis(basis_vals, 0, -2)


def to_lines(traces):
    shaped = traces.reshape(NVAR, FACE, N_PX, N_PY, LAYERS, COLS).transpose(0, 1, 3, 2, 4, 5)
    return shaped.reshape(NVAR, FACE, N_PY, N_PX * LAYERS, COLS)


def from_lines(traces):
    shaped = traces.reshape(NVAR, FACE, N_PY, N_PX, LAYERS, COLS).transpose(0, 1, 3, 2, 4, 5)
    return shaped.reshape(NVAR, FACE, ELEMS)


def reference(current_state, state_old, jacobian, volume_operator_list, flux_jacobian_list, penalty, cut_owner, cut_element, cut_mass, cut_operator, body_holder_index, body_points, body_normals, body_weights, covered):
    degree_one = DEGREE + 1
    change = current_state - state_old
    residual = mode_weights()[None, :, None] * jacobian[None, None, :] * change
    for space_direction in range(3):
        blended_state = jnp.einsum("jr,rti->jti", flux_jacobian_list[space_direction], current_state, precision=TOP_PRECISION)
        residual = residual - jnp.einsum("fz,jzx->jfx", volume_operator_list[space_direction], blended_state, precision=TOP_PRECISION)

    split_modes = current_state.reshape(NVAR, degree_one, FACE, ELEMS)
    parity = jnp.where(jnp.arange(degree_one, dtype=jnp.int32) % 2 == 0, 1.0, -1.0).astype(jnp.float32)
    upper_line = to_lines(jnp.sum(split_modes, axis=1))
    lower_line = to_lines(jnp.sum(split_modes * parity[None, :, None, None], axis=1))
    zero_layer = jnp.zeros_like(upper_line[:, :, :, :1])
    from_above = jnp.concatenate([lower_line[:, :, :, 1:], zero_layer], axis=3)
    from_below = jnp.concatenate([zero_layer, upper_line[:, :, :, :-1]], axis=3)
    jump_top = from_lines(from_above - upper_line)
    jump_bottom = from_lines(from_below - lower_line)
    face_term = penalty[:, None, None, None] * (jump_top[:, None] + parity[None, :, None, None] * jump_bottom[:, None])
    residual = residual - face_term.reshape(NVAR, MODES, ELEMS)

    slab_of = jnp.arange(CUTS, dtype=jnp.int32) // (CUT_DEV * N_PY)
    target = ((slab_of * N_PY + cut_owner[:, 0].astype(jnp.int32)) * ELEM_DEV + cut_element.astype(jnp.int32)).astype(jnp.int32)
    cut_terms = jnp.einsum("cmn,vnc->vmc", cut_mass, change[:, :, target], precision=TOP_PRECISION) - jnp.einsum("cmn,vnc->vmc", cut_operator, current_state[:, :, target], precision=TOP_PRECISION)
    residual = residual.at[:, :, target].add(cut_terms)

    owners = body_holder_index.reshape(N_PX, BODIES).astype(jnp.int32)
    points_grid = body_points.reshape(N_PX, N_PY, BODIES, 3, QPTS)
    normal_grid = body_normals.reshape(N_PX, N_PY, BODIES, 3, QPTS)
    weight_grid = body_weights.reshape(N_PX, N_PY, BODIES, QPTS)
    covered_grid = covered.reshape(N_PX, N_PY, BODIES, COVERED).astype(jnp.int32)
    slab_ids = jnp.arange(N_PX, dtype=jnp.int32)
    device_base = (slab_ids[:, None] * N_PY + jnp.arange(N_PY, dtype=jnp.int32)[None, :]) * ELEM_DEV
    for body_index in range(BODIES):
        owner_ids = owners[:, body_index]
        points = points_grid[slab_ids, owner_ids, body_index]
        normals = normal_grid[slab_ids, owner_ids, body_index]
        weights = weight_grid[slab_ids, owner_ids, body_index]
        basis_now = basis_rows(points)
        targets = (device_base[:, :, None] + covered_grid[:, :, body_index, :]).astype(jnp.int32)
        gathered = current_state[:, :, targets]
        surf_trace = jnp.einsum("smq,vmspo->vqspo", basis_now, gathered, precision=TOP_PRECISION)
        normal_x = jnp.transpose(normals[:, 0, :])[:, :, None, None]
        normal_y = jnp.transpose(normals[:, 1, :])[:, :, None, None]
        normal_z = jnp.transpose(normals[:, 2, :])[:, :, None, None]
        speed = normal_x * surf_trace[1] + normal_y * surf_trace[2] + normal_z * surf_trace[3]
        body_wall_flux = jnp.stack([speed + 0.5 * surf_trace[0], normal_x * surf_trace[4], normal_y * surf_trace[4], normal_z * surf_trace[4], 1.4 * speed], axis=0)
        weighted = body_wall_flux * jnp.transpose(weights)[None, :, :, None, None]
        lifted = jnp.einsum("smq,vqspo->vmspo", basis_now, weighted, precision=TOP_PRECISION)
        residual = residual.at[:, :, targets].add(-lifted)
    return residual
```

```python
import functools

import jax
import jax.numpy as jnp
from jax import lax
from jax.experimental import pallas as pl
from jax.experimental.pallas import tpu as pltpu
from jax.sharding import PartitionSpec as P

F32 = jnp.float32
BF16 = jnp.bfloat16
MESH = pl.DeviceIdType.MESH
NVAR = 5
MODES = 125
PAD = 128
ELEM = 1024
PEERS = 32
CUTS = 40
CPAD = 48
SLOTS = 64
BODIES = 6
COVER = 16
TERMS = SLOTS + BODIES * COVER
WIDTH = NVAR * PAD
MBLOCK = 16


def split(value):
    high = value.astype(BF16)
    low = (value - high.astype(F32)).astype(BF16)
    return high, low


def dot(left, right):
    return jnp.dot(left, right, preferred_element_type=F32)


def dot_nt(left, right):
    return lax.dot_general(left, right, (((1,), (1,)), ((), ())), preferred_element_type=F32)


def iota(shape, dim):
    return lax.broadcasted_iota(jnp.int32, shape, dim)


def divmod_const(index, by):
    exact = index.astype(F32)
    whole = jnp.floor((exact + 0.5) * (1.0 / by))
    return whole, exact - whole * by


def parity_of(whole):
    return 1.0 - 2.0 * (whole - 2.0 * jnp.floor(whole * 0.5))


def pad_rows(value):
    zero = jnp.zeros((PAD - value.shape[0], value.shape[1]), value.dtype)
    return jnp.concatenate([value, zero], axis=0)


def pad_lanes(value):
    zero = jnp.zeros((value.shape[0], PAD - value.shape[1]), value.dtype)
    return jnp.concatenate([value, zero], axis=1)


def to_column(row, rows, lanes):
    spread = jnp.broadcast_to(row, (rows, lanes))
    pick = iota((rows, lanes), 0) == iota((rows, lanes), 1)
    return jnp.sum(jnp.where(pick, spread, 0), axis=1, keepdims=True)


def kernel(
    state_hbm,
    old_hbm,
    mass_hbm,
    oper_hbm,
    jac,
    vol,
    flux,
    penalty,
    owner,
    elem,
    holder,
    points,
    normals,
    weights,
    covered,
    out_hbm,
    st,
    so,
    mats,
    uhl,
    chl,
    vpad,
    mhh,
    mlo,
    trx,
    part,
    cuth,
    cutl,
    ids_row,
    ids_all,
    onehot,
    p2send,
    p2recv,
    p3send,
    p3recv,
    gbody,
    xh,
    xl,
    tmode,
    bown,
    bgot1,
    bsum1,
    bgot2,
    bsum2,
    bgot3,
    basis,
    tbody,
    load_sem,
    out_sem,
    rim_send,
    rim_recv,
    id_send,
    id_recv,
    p2_send,
    p2_recv,
    p3_send,
    p3_recv,
    b_send,
    b_recv,
):
    me = lax.axis_index("py")
    pz = lax.axis_index("px")
    npx = lax.axis_size("px")

    load_state = pltpu.make_async_copy(state_hbm, st, load_sem.at[0])
    load_old = pltpu.make_async_copy(old_hbm, so, load_sem.at[1])
    load_mass = pltpu.make_async_copy(mass_hbm, mats.at[0], load_sem.at[2])
    load_oper = pltpu.make_async_copy(oper_hbm, mats.at[1], load_sem.at[3])
    load_state.start()
    load_old.start()
    load_mass.start()
    load_oper.start()

    barrier = pltpu.get_barrier_semaphore()
    above = lax.rem(pz + 1, npx)
    below = lax.rem(pz + npx - 1, npx)

    def greet(r, carry):
        pl.semaphore_signal(
            barrier, inc=1, device_id={"py": lax.rem(me + r, PEERS)}, device_id_type=MESH
        )
        return carry

    lax.fori_loop(1, PEERS, greet, 0)
    for neighbour in (above, below):
        pl.semaphore_signal(barrier, inc=1, device_id={"px": neighbour}, device_id_type=MESH)

    own_row = jnp.broadcast_to(owner[...], (CUTS, CUTS))
    own_col = to_column(owner[...], CUTS, CUTS)
    elem_col = to_column(elem[...], CUTS, CUTS)
    same = own_row == own_col
    row_c, lane_c = iota((CUTS, CUTS), 0), iota((CUTS, CUTS), 1)
    pos_col = jnp.sum(jnp.where(same & (lane_c < row_c), 1, 0), axis=1, keepdims=True)
    pos_row = jnp.sum(jnp.where(same & (row_c < lane_c), 1, 0), axis=0, keepdims=True)
    slot_col = pos_col * PEERS + own_col
    slot_row = pos_row * PEERS + owner[...]
    placed = jnp.where(slot_col == iota((CUTS, PAD), 1), elem_col + 1, 0)
    ids_row[...] = jnp.sum(placed, axis=0, keepdims=True) - 1

    bown[...] = jnp.zeros_like(bown)
    body_row = iota((BODIES, 128), 0)
    held = jnp.zeros((BODIES, 128), jnp.int32)
    for b in range(BODIES):
        held = jnp.where(body_row == b, jnp.where(holder[b] == me, 1, 0), held)
    held = held == 1
    for d in range(3):
        bown[d, 0:BODIES, :] = jnp.where(held, points[:, d, :], 0.0)
        bown[3 + d, 0:BODIES, :] = jnp.where(held, normals[:, d, :], 0.0)
    bown[6, 0:BODIES, :] = jnp.where(held, weights[...], 0.0)

    pl.semaphore_wait(barrier, PEERS + 1)

    def id_copy(r):
        return pltpu.make_async_remote_copy(
            src_ref=ids_row,
            dst_ref=ids_all.at[pl.ds(me, 1), :],
            send_sem=id_send.at[r],
            recv_sem=id_recv,
            device_id={"py": lax.rem(me + r, PEERS)},
            device_id_type=MESH,
        )

    def id_start(r, carry):
        id_copy(r).start()
        return carry

    lax.fori_loop(1, PEERS, id_start, 0)
    pltpu.make_async_copy(ids_row, ids_all.at[pl.ds(me, 1), :], id_recv).start()

    core = lax.rem(me, 2)
    px_in = lax.rem(me // 2, 4)
    py_in = me // 8
    sibling = me + 1 - 2 * core
    body1 = pltpu.make_async_remote_copy(
        src_ref=bown,
        dst_ref=bgot1,
        send_sem=b_send.at[0],
        recv_sem=b_recv.at[0],
        device_id={"py": sibling},
        device_id_type=MESH,
    )
    body1.start()

    vpad[...] = jnp.zeros_like(vpad)
    for d in range(3):
        vpad[d, 0:MODES, 0:MODES] = vol[d]
    ri, rf = divmod_const(iota((PAD, PAD), 0), 25)
    ci, cf = divmod_const(iota((PAD, PAD), 1), 25)
    inside = (ri < 5.0) & (ci < 5.0)
    own_face = jnp.where(inside & (rf == cf), 1.0 + parity_of(ri) * parity_of(ci), 0.0)

    def build(v, carry):
        rows = pl.ds(pl.multiple_of(v * PAD, PAD), PAD)
        for w in range(NVAR):
            block = jnp.where(v == w, penalty[v], 0.0) * own_face
            for d in range(3):
                block = block - flux[v, d, w] * vpad[d]
            high, low = split(block)
            mhh[rows, w * PAD : (w + 1) * PAD] = high
            mhh[rows, WIDTH + w * PAD : WIDTH + (w + 1) * PAD] = high
            mlo[rows, w * PAD : (w + 1) * PAD] = low
        return carry

    lax.fori_loop(0, NVAR, build, 0)

    ti, tf = divmod_const(iota((64, PAD), 1), 25)
    tr_row = iota((64, PAD), 0)
    tr_lower = tr_row >= 32
    tr_f = jnp.where(tr_lower, tr_row - 32, tr_row).astype(F32)
    trace_op = jnp.where(
        (tf == tr_f) & (ti < 5.0), jnp.where(tr_lower, parity_of(ti), 1.0), 0.0
    ).astype(BF16)
    l64 = lax.rem(iota((PAD, PAD), 1), 64)
    l32 = lax.rem(iota((PAD, PAD), 1), 32)
    expand_op = jnp.where(
        (rf == l32.astype(F32)) & (ri < 5.0), jnp.where(l64 < 32, parity_of(ri), 1.0), 0.0
    ).astype(BF16)

    load_state.wait()
    load_old.wait()

    def split_state(j, carry):
        cols = pl.ds(pl.multiple_of(j * 256, 256), 256)
        tcols = pl.ds(pl.multiple_of(j * 256 + 128, 128), 256)
        for v in range(NVAR):
            rows = pl.ds(v * PAD, PAD)
            u = st[v, :, cols]
            high, low = split(pad_rows(u))
            uhl[0, rows, cols] = high
            uhl[1, rows, cols] = low
            trx[v, :, tcols] = dot(trace_op, high) + dot(trace_op, low)
            high, low = split(pad_rows(u - so[v, :, cols]))
            chl[0, rows, cols] = high
            chl[1, rows, cols] = low
        return carry

    lax.fori_loop(0, 4, split_state, 0)

    rim_down = pltpu.make_async_remote_copy(
        src_ref=trx.at[:, 32:64, 128:256],
        dst_ref=trx.at[:, 32:64, 1152:1280],
        send_sem=rim_send.at[0],
        recv_sem=rim_recv.at[0],
        device_id={"px": below},
        device_id_type=MESH,
    )
    rim_up = pltpu.make_async_remote_copy(
        src_ref=trx.at[:, 0:32, 1024:1152],
        dst_ref=trx.at[:, 0:32, 0:128],
        send_sem=rim_send.at[1],
        recv_sem=rim_recv.at[1],
        device_id={"px": above},
        device_id_type=MESH,
    )
    rim_down.start()
    rim_up.start()

    body1.wait_recv()
    bsum1[...] = bown[...] + bgot1[...]
    body2 = []
    for r in range(1, 4):
        body2.append(
            pltpu.make_async_remote_copy(
                src_ref=bsum1,
                dst_ref=bgot2.at[r - 1],
                send_sem=b_send.at[r],
                recv_sem=b_recv.at[r],
                device_id={"py": py_in * 8 + lax.rem(px_in + r, 4) * 2 + core},
                device_id_type=MESH,
            )
        )
        body2[-1].start()

    pltpu.make_async_copy(ids_all, ids_all, id_recv).wait()
    asked = ids_all[...]
    lane = iota((PEERS, 128), 1)
    elem_lane = iota((PEERS, ELEM), 1)
    for k in range(2):
        wanted = jnp.sum(jnp.where(lane == me + k * PEERS, asked, 0), axis=1, keepdims=True)
        onehot[k * PEERS : (k + 1) * PEERS, :] = jnp.where(wanted == elem_lane, 1.0, 0.0).astype(BF16)
    cover_lane = iota((COVER, ELEM), 1)
    for b in range(BODIES):
        wanted = to_column(covered[b : b + 1, :], COVER, COVER)
        start = SLOTS + b * COVER
        onehot[start : start + COVER, :] = jnp.where(wanted == cover_lane, 1.0, 0.0).astype(BF16)

    state_high = dot_nt(onehot[...], uhl[0])
    state_low = dot_nt(onehot[...], uhl[1])
    state_cols = state_high + state_low
    change_cols = dot_nt(onehot[0:SLOTS, :], chl[0]) + dot_nt(onehot[0:SLOTS, :], chl[1])
    for k in range(2):
        rows = slice(k * PEERS, (k + 1) * PEERS)
        for v in range(NVAR):
            lanes = slice(v * PAD, (v + 1) * PAD)
            p2send[k * 10 + v] = change_cols[rows, lanes]
            p2send[k * 10 + 5 + v] = state_cols[rows, lanes]
    for v in range(NVAR):
        gbody[v] = state_cols[SLOTS:, v * PAD : (v + 1) * PAD]

    def p2_copy(r):
        peer = lax.rem(me + r, PEERS)
        return pltpu.make_async_remote_copy(
            src_ref=p2send.at[:, pl.ds(peer, 1), :],
            dst_ref=p2recv.at[:, pl.ds(me, 1), :],
            send_sem=p2_send.at[r],
            recv_sem=p2_recv,
            device_id={"py": peer},
            device_id_type=MESH,
        )

    def p2_start(r, carry):
        p2_copy(r).start()
        return carry

    lax.fori_loop(1, PEERS, p2_start, 0)
    pltpu.make_async_copy(
        p2send.at[:, pl.ds(me, 1), :], p2recv.at[:, pl.ds(me, 1), :], p2_recv
    ).start()

    for copy in body2:
        copy.wait_recv()
    bsum2[...] = bsum1[...] + bgot2[0] + bgot2[1] + bgot2[2]
    body3 = []
    for r in range(1, 4):
        body3.append(
            pltpu.make_async_remote_copy(
                src_ref=bsum2,
                dst_ref=bgot3.at[r - 1],
                send_sem=b_send.at[3 + r],
                recv_sem=b_recv.at[3 + r],
                device_id={"py": lax.rem(py_in + r, 4) * 8 + px_in * 2 + core},
                device_id_type=MESH,
            )
        )
        body3[-1].start()

    rim_down.wait_recv()
    rim_up.wait_recv()
    rim = trx[:, 32:64, 1152:1280]
    trx[:, 32:64, 1152:1280] = jnp.where(pz == npx - 1, 0.0, rim)
    rim = trx[:, 0:32, 0:128]
    trx[:, 0:32, 0:128] = jnp.where(pz == 0, 0.0, rim)

    mi, mrest = divmod_const(iota((MODES, 256), 0), 25)
    mj = jnp.floor((mrest + 0.5) * 0.2)
    mk = mrest - mj * 5.0
    mode_weight = 8.0 / ((2.0 * mi + 1.0) * (2.0 * mj + 1.0) * (2.0 * mk + 1.0))

    def volume(j, carry):
        base = pl.multiple_of(j * 256, 256)
        cols = pl.ds(base, 256)
        acc = dot(mhh[...], uhl[:, :, cols].reshape(2 * WIDTH, 256)) + dot(
            mlo[...], uhl[0, :, cols]
        )
        scale = mode_weight * jac[:, cols]
        for v in range(NVAR):
            near = jnp.concatenate(
                [trx[v, 0:32, cols], trx[v, 32:64, pl.ds(pl.multiple_of(base + 256, 256), 256)]],
                axis=0,
            )
            high, low = split(near)
            faces = dot(expand_op, jnp.concatenate([high, low], axis=0))
            change = st[v, :, cols] - so[v, :, cols]
            part[v, :, cols] = (
                acc[v * PAD : v * PAD + MODES] + scale * change - penalty[v] * faces[0:MODES]
            )
        return carry

    lax.fori_loop(0, 4, volume, 0)

    load_mass.wait()
    load_oper.wait()

    def split_cut(i, carry):
        rows = pl.ds(pl.multiple_of(i * (8 * CUTS), 8 * CUTS), 8 * CUTS)
        for t in range(2):
            high, low = split(pad_lanes(mats[t, pl.ds(i * 8, 8)].reshape(8 * CUTS, MODES)))
            cuth[rows, t * PAD : (t + 1) * PAD] = high
            cutl[rows, t * PAD : (t + 1) * PAD] = low
        return carry

    lax.fori_loop(0, MODES // 8, split_cut, 0)
    whole = MODES // 8 * 8
    for t in range(2):
        tail = pad_lanes(mats[t, whole:MODES].reshape((MODES - whole) * CUTS, MODES))
        zero = jnp.zeros(((PAD - MODES) * CUTS, PAD), F32)
        high, low = split(jnp.concatenate([tail, zero], axis=0))
        cuth[whole * CUTS :, t * PAD : (t + 1) * PAD] = high
        cutl[whole * CUTS :, t * PAD : (t + 1) * PAD] = low

    pltpu.make_async_copy(p2recv, p2recv, p2_recv).wait()
    xh[...] = jnp.zeros_like(xh)
    xl[...] = jnp.zeros_like(xl)
    take = jnp.where(slot_col == iota((CUTS, SLOTS), 1), 1.0, 0.0)
    take = jnp.concatenate([take, jnp.zeros((CPAD - CUTS, SLOTS), F32)], axis=0).astype(BF16)
    for t in range(2):
        for v in range(NVAR):
            got = jnp.concatenate([p2recv[t * 5 + v], p2recv[10 + t * 5 + v]], axis=0)
            high, low = split(-got if t else got)
            rows, lanes = slice(v * CPAD, (v + 1) * CPAD), slice(t * PAD, (t + 1) * PAD)
            xh[rows, lanes] = dot(take, high).astype(BF16)
            xl[rows, lanes] = dot(take, low).astype(BF16)

    _, block_lane = divmod_const(iota((CUTS, 256), 1), CPAD)
    diagonal = jnp.where(block_lane == iota((CUTS, 256), 0).astype(F32), 1.0, 0.0)

    def products(i, carry):
        rows = pl.ds(pl.multiple_of(i * (MBLOCK * CUTS), MBLOCK * CUTS), MBLOCK * CUTS)
        high, low = cuth[rows, :], cutl[rows, :]
        all_pairs = dot_nt(high, xh[...]) + dot_nt(low, xh[...]) + dot_nt(high, xl[...])
        kept = all_pairs.reshape(MBLOCK, CUTS, 256) * diagonal[None]
        tmode[pl.ds(pl.multiple_of(i * MBLOCK, MBLOCK), MBLOCK), :] = jnp.sum(kept, axis=1)
        return carry

    lax.fori_loop(0, PAD // MBLOCK, products, 0)

    spread_row, spread_lane = divmod_const(iota((CUTS, 256), 1), CPAD)
    spread = jnp.where(spread_lane == iota((CUTS, 256), 0).astype(F32), 1.0, 0.0)
    slots_f = jnp.sum(spread * slot_col.astype(F32), axis=0, keepdims=True)
    lane_v, lane_in = divmod_const(iota((1, 256), 1), CPAD)
    target = jnp.where((lane_in < CUTS) & (lane_v < NVAR), lane_v * SLOTS + slots_f, -1.0)
    place = jnp.where(
        target == iota((NVAR * SLOTS, 256), 0).astype(F32), 1.0, 0.0
    ).astype(BF16)
    high, low = split(tmode[...])
    slotted = dot_nt(place, high) + dot_nt(place, low)
    p3send[...] = slotted.reshape(2 * NVAR, PEERS, PAD)

    def p3_copy(r):
        peer = lax.rem(me + r, PEERS)
        return pltpu.make_async_remote_copy(
            src_ref=p3send.at[:, pl.ds(peer, 1), :],
            dst_ref=p3recv.at[:, pl.ds(me, 1), :],
            send_sem=p3_send.at[r],
            recv_sem=p3_recv,
            device_id={"py": peer},
            device_id_type=MESH,
        )

    def p3_start(r, carry):
        p3_copy(r).start()
        return carry

    lax.fori_loop(1, PEERS, p3_start, 0)
    pltpu.make_async_copy(
        p3send.at[:, pl.ds(me, 1), :], p3recv.at[:, pl.ds(me, 1), :], p3_recv
    ).start()

    for copy in body3:
        copy.wait_recv()
    bodies = bsum2[...] + bgot3[0] + bgot3[1] + bgot3[2]
    tables = []
    for d in range(3):
        x = bodies[d]
        table = [jnp.ones_like(x), x]
        for n in range(1, 4):
            table.append(((2.0 * n + 1.0) * x * table[n] - n * table[n - 1]) / (n + 1.0))
        tables.append(table)
    for i in range(5):
        for j in range(5):
            pair = tables[0][i] * tables[1][j]
            for k in range(5):
                basis[(i * 5 + j) * 5 + k] = pair * tables[2][k]
    for m in range(MODES, PAD):
        basis[m] = jnp.zeros((8, 128), F32)
    for b in range(BODIES):
        rows = slice(b * COVER, (b + 1) * COVER)
        bh, bl = split(basis[:, b, :])
        gh, gl = split(gbody[:, rows, :].reshape(NVAR * COVER, PAD))
        trace = (dot(gh, bh) + dot(gl, bh) + dot(gh, bl)).reshape(NVAR, COVER, 128)
        nx, ny, nz = bodies[3, b : b + 1], bodies[4, b : b + 1], bodies[5, b : b + 1]
        weight = bodies[6, b : b + 1]
        speed = nx * trace[1] + ny * trace[2] + nz * trace[3]
        wall = jnp.concatenate(
            [
                (speed + 0.5 * trace[0]) * weight,
                nx * trace[4] * weight,
                ny * trace[4] * weight,
                nz * trace[4] * weight,
                1.4 * speed * weight,
            ],
            axis=0,
        )
        wh, wl = split(wall)
        lifted = dot_nt(wh, bh) + dot_nt(wl, bh) + dot_nt(wh, bl)
        tbody[:, rows, :] = -lifted.reshape(NVAR, COVER, PAD)

    pltpu.make_async_copy(p3recv, p3recv, p3_recv).wait()
    stores = []
    for v in range(NVAR):
        terms = jnp.concatenate([p3recv[2 * v], p3recv[2 * v + 1], tbody[v]], axis=0)
        high, low = split(terms.T)
        added = dot(high, onehot[...]) + dot(low, onehot[...])
        part[v] = part[v] + added[0:MODES]
        stores.append(pltpu.make_async_copy(part.at[v], out_hbm.at[v], out_sem.at[v]))
        stores[-1].start()

    def finish(r, carry):
        id_copy(r).wait_send()
        p2_copy(r).wait_send()
        p3_copy(r).wait_send()
        return carry

    lax.fori_loop(1, PEERS, finish, 0)
    body1.wait_send()
    for copy in body2 + body3:
        copy.wait_send()
    rim_down.wait_send()
    rim_up.wait_send()
    for copy in stores:
        copy.wait()


def local(
    current_state,
    state_old,
    jacobian,
    volume_operator_list,
    flux_jacobian_list,
    penalty,
    cut_owner,
    cut_element,
    cut_mass,
    cut_operator,
    body_holder_index,
    body_points,
    body_normals,
    body_weights,
    covered,
):
    hbm = pl.BlockSpec(memory_space=pl.ANY)
    vmem = pl.BlockSpec(memory_space=pltpu.VMEM)
    smem = pl.BlockSpec(memory_space=pltpu.SMEM)
    dma = pltpu.SemaphoreType.DMA
    return pl.pallas_call(
        kernel,
        out_shape=jax.ShapeDtypeStruct((NVAR, MODES, ELEM), F32),
        in_specs=[hbm] * 4 + [vmem, vmem, smem, smem, vmem, vmem, smem] + [vmem] * 4,
        out_specs=hbm,
        scratch_shapes=[
            pltpu.VMEM((NVAR, MODES, ELEM), F32),
            pltpu.VMEM((NVAR, MODES, ELEM), F32),
            pltpu.VMEM((2, MODES, CUTS, MODES), F32),
            pltpu.VMEM((2, WIDTH, ELEM), BF16),
            pltpu.VMEM((2, WIDTH, ELEM), BF16),
            pltpu.VMEM((3, PAD, PAD), F32),
            pltpu.VMEM((WIDTH, 2 * WIDTH), BF16),
            pltpu.VMEM((WIDTH, WIDTH), BF16),
            pltpu.VMEM((NVAR, 64, ELEM + 256), F32),
            pltpu.VMEM((NVAR, MODES, ELEM), F32),
            pltpu.VMEM((PAD * CUTS, 256), BF16),
            pltpu.VMEM((PAD * CUTS, 256), BF16),
            pltpu.VMEM((1, 128), jnp.int32),
            pltpu.VMEM((PEERS, 128), jnp.int32),
            pltpu.VMEM((TERMS, ELEM), BF16),
            pltpu.VMEM((4 * NVAR, PEERS, PAD), F32),
            pltpu.VMEM((4 * NVAR, PEERS, PAD), F32),
            pltpu.VMEM((2 * NVAR, PEERS, PAD), F32),
            pltpu.VMEM((2 * NVAR, PEERS, PAD), F32),
            pltpu.VMEM((NVAR, BODIES * COVER, PAD), F32),
            pltpu.VMEM((256, 256), BF16),
            pltpu.VMEM((256, 256), BF16),
            pltpu.VMEM((PAD, 256), F32),
            pltpu.VMEM((7, 8, 128), F32),
            pltpu.VMEM((7, 8, 128), F32),
            pltpu.VMEM((7, 8, 128), F32),
            pltpu.VMEM((3, 7, 8, 128), F32),
            pltpu.VMEM((7, 8, 128), F32),
            pltpu.VMEM((3, 7, 8, 128), F32),
            pltpu.VMEM((PAD, 8, 128), F32),
            pltpu.VMEM((NVAR, BODIES * COVER, PAD), F32),
            dma((4,)),
            dma((NVAR,)),
            dma((2,)),
            dma((2,)),
            dma((PEERS,)),
            dma,
            dma((PEERS,)),
            dma,
            dma((PEERS,)),
            dma,
            dma((7,)),
            dma((7,)),
        ],
        compiler_params=pltpu.CompilerParams(
            collective_id=0, has_side_effects=True, vmem_limit_bytes=56 * 1024 * 1024
        ),
        name="residual_step",
    )(
        current_state,
        state_old,
        cut_mass.transpose(1, 0, 2),
        cut_operator.transpose(1, 0, 2),
        jacobian.reshape(1, ELEM),
        volume_operator_list,
        flux_jacobian_list.transpose(1, 0, 2),
        penalty,
        cut_owner.reshape(1, CUTS),
        cut_element.reshape(1, CUTS),
        body_holder_index,
        body_points,
        body_normals,
        body_weights,
        covered,
    )


def solution(mesh):
    in_specs = (
        P(None, None, ("px", "py")),
        P(None, None, ("px", "py")),
        P(("px", "py")),
        P(),
        P(),
        P(),
        P(("px", "py"), None),
        P(("px", "py")),
        P(("px", "py"), None, None),
        P(("px", "py"), None, None),
        P("px"),
        P(("px", "py"), None, None),
        P(("px", "py"), None, None),
        P(("px", "py"), None),
        P(("px", "py"), None),
    )
    out_specs = P(None, None, ("px", "py"))
    return jax.shard_map(local, mesh=mesh, in_specs=in_specs, out_specs=out_specs, check_vma=False)
```

```python
import functools

import jax
import jax.numpy as jnp
from jax import lax
from jax.experimental import pallas as pl
from jax.experimental.pallas import tpu as pltpu
from jax.sharding import PartitionSpec as P

F32 = jnp.float32
BF16 = jnp.bfloat16
MESH = pl.DeviceIdType.MESH
NVAR = 5
MODES = 125
PAD = 128
ELEM = 1024
PEERS = 32
CUTS = 40
CPAD = 48
SLOTS = 64
BODIES = 6
COVER = 16
TERMS = SLOTS + BODIES * COVER
WIDTH = NVAR * PAD
MBLOCK = 16


def split(value):
    high = value.astype(BF16)
    low = (value - high.astype(F32)).astype(BF16)
    return high, low


def dot(left, right):
    return jnp.dot(left, right, preferred_element_type=F32)


def dot_nt(left, right):
    return lax.dot_general(left, right, (((1,), (1,)), ((), ())), preferred_element_type=F32)


def iota(shape, dim):
    return lax.broadcasted_iota(jnp.int32, shape, dim)


def divmod_const(index, by):
    exact = index.astype(F32)
    whole = jnp.floor((exact + 0.5) * (1.0 / by))
    return whole, exact - whole * by


def parity_of(whole):
    return 1.0 - 2.0 * (whole - 2.0 * jnp.floor(whole * 0.5))


def pad_rows(value):
    zero = jnp.zeros((PAD - value.shape[0], value.shape[1]), value.dtype)
    return jnp.concatenate([value, zero], axis=0)


def pad_lanes(value):
    zero = jnp.zeros((value.shape[0], PAD - value.shape[1]), value.dtype)
    return jnp.concatenate([value, zero], axis=1)


def to_column(row, rows, lanes):
    spread = jnp.broadcast_to(row, (rows, lanes))
    pick = iota((rows, lanes), 0) == iota((rows, lanes), 1)
    return jnp.sum(jnp.where(pick, spread, 0), axis=1, keepdims=True)


def kernel(
    state_hbm,
    old_hbm,
    mass_hbm,
    oper_hbm,
    jac_hbm,
    vol_hbm,
    flux_hbm,
    penalty_hbm,
    owner_hbm,
    elem_hbm,
    holder_hbm,
    points_hbm,
    normals_hbm,
    weights_hbm,
    covered_hbm,
    part,
    returned,
    asked_rows,
    jac,
    vol,
    flux,
    penalty,
    owner,
    elem,
    holder,
    points,
    normals,
    weights,
    covered,
    st,
    so,
    mats,
    uhl,
    chl,
    vpad,
    mhh,
    mlo,
    trx,
    cuth,
    cutl,
    ids_row,
    ids_all,
    onehot,
    place,
    p2send,
    p2recv,
    p3send,
    p3recv,
    gbody,
    xh,
    xl,
    tmode,
    bown,
    bgot1,
    bsum1,
    bgot2,
    bsum2,
    bgot3,
    basis,
    tbody,
    load_sem,
    small_sem,
    rim_send,
    rim_recv,
    id_send,
    id_recv,
    p2_send,
    p2_recv,
    p3_send,
    p3_recv,
    b_send,
    b_recv,
):
    me = lax.axis_index("py")
    pz = lax.axis_index("px")
    npx = lax.axis_size("px")

    barrier = pltpu.get_barrier_semaphore()
    above = lax.rem(pz + 1, npx)
    below = lax.rem(pz + npx - 1, npx)

    def greet(r, carry):
        pl.semaphore_signal(
            barrier, inc=1, device_id={"py": lax.rem(me + r, PEERS)}, device_id_type=MESH
        )
        return carry

    lax.fori_loop(1, PEERS, greet, 0)
    for neighbour in (above, below):
        pl.semaphore_signal(barrier, inc=1, device_id={"px": neighbour}, device_id_type=MESH)

    load_state = pltpu.make_async_copy(state_hbm, st, load_sem.at[0])
    load_old = pltpu.make_async_copy(old_hbm, so, load_sem.at[1])
    load_mass = pltpu.make_async_copy(mass_hbm, mats.at[0], load_sem.at[2])
    load_oper = pltpu.make_async_copy(oper_hbm, mats.at[1], load_sem.at[3])
    pairs = (
        (owner_hbm, owner),
        (elem_hbm, elem),
        (covered_hbm, covered),
        (holder_hbm, holder),
        (points_hbm, points),
        (normals_hbm, normals),
        (weights_hbm, weights),
        (penalty_hbm, penalty),
        (flux_hbm, flux),
        (vol_hbm, vol),
        (jac_hbm, jac),
    )
    smalls = [
        pltpu.make_async_copy(source, target, small_sem.at[i])
        for i, (source, target) in enumerate(pairs)
    ]
    for copy in smalls:
        copy.start()
    for copy in smalls:
        copy.wait()
    load_state.start()
    load_old.start()

    own_row = jnp.broadcast_to(owner[...], (CUTS, CUTS))
    own_col = to_column(owner[...], CUTS, CUTS)
    elem_col = to_column(elem[...], CUTS, CUTS)
    same = own_row == own_col
    row_c, lane_c = iota((CUTS, CUTS), 0), iota((CUTS, CUTS), 1)
    pos_col = jnp.sum(jnp.where(same & (lane_c < row_c), 1, 0), axis=1, keepdims=True)
    pos_row = jnp.sum(jnp.where(same & (row_c < lane_c), 1, 0), axis=0, keepdims=True)
    slot_col = pos_col * PEERS + own_col
    slot_row = pos_row * PEERS + owner[...]
    placed = jnp.where(slot_col == iota((CUTS, PAD), 1), elem_col + 1, 0)
    ids_row[...] = jnp.sum(placed, axis=0, keepdims=True) - 1

    _, spread_lane = divmod_const(iota((CUTS, 256), 1), CPAD)
    spread = jnp.where(spread_lane == iota((CUTS, 256), 0).astype(F32), 1.0, 0.0)
    slots_f = jnp.sum(spread * slot_col.astype(F32), axis=0, keepdims=True)
    lane_v, lane_in = divmod_const(iota((1, 256), 1), CPAD)
    target = jnp.where((lane_in < CUTS) & (lane_v < NVAR), lane_v * SLOTS + slots_f, -1.0)
    place[...] = jnp.where(
        target == iota((NVAR * SLOTS, 256), 0).astype(F32), 1.0, 0.0
    ).astype(BF16)

    cover_lane = iota((COVER, ELEM), 1)
    for b in range(BODIES):
        wanted = to_column(covered[b : b + 1, :], COVER, COVER)
        start = SLOTS + b * COVER
        onehot[start : start + COVER, :] = jnp.where(wanted == cover_lane, 1.0, 0.0).astype(BF16)

    bown[...] = jnp.zeros_like(bown)
    body_row = iota((BODIES, 128), 0)
    held = jnp.zeros((BODIES, 128), jnp.int32)
    for b in range(BODIES):
        held = jnp.where(body_row == b, jnp.where(holder[b] == me, 1, 0), held)
    held = held == 1
    for d in range(3):
        bown[d, 0:BODIES, :] = jnp.where(held, points[:, d, :], 0.0)
        bown[3 + d, 0:BODIES, :] = jnp.where(held, normals[:, d, :], 0.0)
    bown[6, 0:BODIES, :] = jnp.where(held, weights[...], 0.0)

    ri, rf = divmod_const(iota((PAD, PAD), 0), 25)
    ti, tf = divmod_const(iota((64, PAD), 1), 25)
    tr_row = iota((64, PAD), 0)
    tr_lower = tr_row >= 32
    tr_f = jnp.where(tr_lower, tr_row - 32, tr_row).astype(F32)
    trace_op = jnp.where(
        (tf == tr_f) & (ti < 5.0), jnp.where(tr_lower, parity_of(ti), 1.0), 0.0
    ).astype(BF16)
    l64 = lax.rem(iota((PAD, PAD), 1), 64)
    l32 = lax.rem(iota((PAD, PAD), 1), 32)
    expand_op = jnp.where(
        (rf == l32.astype(F32)) & (ri < 5.0), jnp.where(l64 < 32, parity_of(ri), 1.0), 0.0
    ).astype(BF16)

    vpad[...] = jnp.zeros_like(vpad)
    for d in range(3):
        vpad[d, 0:MODES, 0:MODES] = vol[d]
    ci, cf = divmod_const(iota((PAD, PAD), 1), 25)
    inside = (ri < 5.0) & (ci < 5.0)
    own_face = jnp.where(inside & (rf == cf), 1.0 + parity_of(ri) * parity_of(ci), 0.0)

    def build(v, carry):
        rows = pl.ds(pl.multiple_of(v * PAD, PAD), PAD)
        for w in range(NVAR):
            block = jnp.where(v == w, penalty[v], 0.0) * own_face
            for d in range(3):
                block = block - flux[v, d, w] * vpad[d]
            high, low = split(block)
            mhh[rows, w * PAD : (w + 1) * PAD] = high
            mhh[rows, WIDTH + w * PAD : WIDTH + (w + 1) * PAD] = high
            mlo[rows, w * PAD : (w + 1) * PAD] = low
        return carry

    lax.fori_loop(0, NVAR, build, 0)

    pl.semaphore_wait(barrier, PEERS + 1)

    def id_copy(r):
        return pltpu.make_async_remote_copy(
            src_ref=ids_row,
            dst_ref=ids_all.at[pl.ds(me, 1), :],
            send_sem=id_send.at[r],
            recv_sem=id_recv,
            device_id={"py": lax.rem(me + r, PEERS)},
            device_id_type=MESH,
        )

    def id_start(r, carry):
        id_copy(r).start()
        return carry

    lax.fori_loop(1, PEERS, id_start, 0)
    pltpu.make_async_copy(ids_row, ids_all.at[pl.ds(me, 1), :], id_recv).start()

    core = lax.rem(me, 2)
    px_in = lax.rem(me // 2, 4)
    py_in = me // 8
    sibling = me + 1 - 2 * core
    body1 = pltpu.make_async_remote_copy(
        src_ref=bown,
        dst_ref=bgot1,
        send_sem=b_send.at[0],
        recv_sem=b_recv.at[0],
        device_id={"py": sibling},
        device_id_type=MESH,
    )
    body1.start()

    load_state.wait()
    load_old.wait()
    load_mass.start()
    load_oper.start()

    def split_state(j, carry):
        cols = pl.ds(pl.multiple_of(j * 256, 256), 256)
        tcols = pl.ds(pl.multiple_of(j * 256 + 128, 128), 256)
        for v in range(NVAR):
            rows = pl.ds(v * PAD, PAD)
            u = st[v, :, cols]
            high, low = split(pad_rows(u))
            uhl[0, rows, cols] = high
            uhl[1, rows, cols] = low
            trx[v, :, tcols] = dot(trace_op, high) + dot(trace_op, low)
            high, low = split(pad_rows(u - so[v, :, cols]))
            chl[0, rows, cols] = high
            chl[1, rows, cols] = low
        return carry

    lax.fori_loop(0, 4, split_state, 0)
    rim_down = pltpu.make_async_remote_copy(
        src_ref=trx.at[:, 32:64, 128:256],
        dst_ref=trx.at[:, 32:64, 1152:1280],
        send_sem=rim_send.at[0],
        recv_sem=rim_recv.at[0],
        device_id={"px": below},
        device_id_type=MESH,
    )
    rim_up = pltpu.make_async_remote_copy(
        src_ref=trx.at[:, 0:32, 1024:1152],
        dst_ref=trx.at[:, 0:32, 0:128],
        send_sem=rim_send.at[1],
        recv_sem=rim_recv.at[1],
        device_id={"px": above},
        device_id_type=MESH,
    )
    rim_down.start()
    rim_up.start()

    body1.wait_recv()
    bsum1[...] = bown[...] + bgot1[...]
    body2 = []
    for r in range(1, 4):
        body2.append(
            pltpu.make_async_remote_copy(
                src_ref=bsum1,
                dst_ref=bgot2.at[r - 1],
                send_sem=b_send.at[r],
                recv_sem=b_recv.at[r],
                device_id={"py": py_in * 8 + lax.rem(px_in + r, 4) * 2 + core},
                device_id_type=MESH,
            )
        )
        body2[-1].start()

    load_mass.wait()
    load_oper.wait()

    def split_cut(i, carry):
        rows = pl.ds(pl.multiple_of(i * (8 * CUTS), 8 * CUTS), 8 * CUTS)
        for t in range(2):
            high, low = split(pad_lanes(mats[t, pl.ds(i * 8, 8)].reshape(8 * CUTS, MODES)))
            cuth[rows, t * PAD : (t + 1) * PAD] = high
            cutl[rows, t * PAD : (t + 1) * PAD] = low
        return carry

    lax.fori_loop(0, MODES // 8, split_cut, 0)
    whole = MODES // 8 * 8
    for t in range(2):
        tail = pad_lanes(mats[t, whole:MODES].reshape((MODES - whole) * CUTS, MODES))
        zero = jnp.zeros(((PAD - MODES) * CUTS, PAD), F32)
        high, low = split(jnp.concatenate([tail, zero], axis=0))
        cuth[whole * CUTS :, t * PAD : (t + 1) * PAD] = high
        cutl[whole * CUTS :, t * PAD : (t + 1) * PAD] = low

    pltpu.make_async_copy(ids_all, ids_all, id_recv).wait()
    asked = ids_all[...]
    lane = iota((PEERS, 128), 1)
    elem_lane = iota((PEERS, ELEM), 1)
    for k in range(2):
        wanted = jnp.sum(jnp.where(lane == me + k * PEERS, asked, 0), axis=1, keepdims=True)
        rows = slice(k * PEERS, (k + 1) * PEERS)
        onehot[rows, :] = jnp.where(wanted == elem_lane, 1.0, 0.0).astype(BF16)
    state_high = dot_nt(onehot[...], uhl[0])
    state_low = dot_nt(onehot[...], uhl[1])
    state_cols = state_high + state_low
    change_cols = dot_nt(onehot[0:SLOTS, :], chl[0]) + dot_nt(onehot[0:SLOTS, :], chl[1])
    for k in range(2):
        rows = slice(k * PEERS, (k + 1) * PEERS)
        for v in range(NVAR):
            lanes = slice(v * PAD, (v + 1) * PAD)
            p2send[k * 10 + v] = change_cols[rows, lanes]
            p2send[k * 10 + 5 + v] = state_cols[rows, lanes]
    for v in range(NVAR):
        gbody[v] = state_cols[SLOTS:, v * PAD : (v + 1) * PAD]

    def p2_copy(r):
        peer = lax.rem(me + r, PEERS)
        return pltpu.make_async_remote_copy(
            src_ref=p2send.at[:, pl.ds(peer, 1), :],
            dst_ref=p2recv.at[:, pl.ds(me, 1), :],
            send_sem=p2_send.at[r],
            recv_sem=p2_recv,
            device_id={"py": peer},
            device_id_type=MESH,
        )

    def p2_start(r, carry):
        p2_copy(r).start()
        return carry

    lax.fori_loop(1, PEERS, p2_start, 0)
    pltpu.make_async_copy(
        p2send.at[:, pl.ds(me, 1), :], p2recv.at[:, pl.ds(me, 1), :], p2_recv
    ).start()

    for copy in body2:
        copy.wait_recv()
    bsum2[...] = bsum1[...] + bgot2[0] + bgot2[1] + bgot2[2]
    body3 = []
    for r in range(1, 4):
        body3.append(
            pltpu.make_async_remote_copy(
                src_ref=bsum2,
                dst_ref=bgot3.at[r - 1],
                send_sem=b_send.at[3 + r],
                recv_sem=b_recv.at[3 + r],
                device_id={"py": lax.rem(py_in + r, 4) * 8 + px_in * 2 + core},
                device_id_type=MESH,
            )
        )
        body3[-1].start()

    rim_down.wait_recv()
    rim_up.wait_recv()
    rim = trx[:, 32:64, 1152:1280]
    trx[:, 32:64, 1152:1280] = jnp.where(pz == npx - 1, 0.0, rim)
    rim = trx[:, 0:32, 0:128]
    trx[:, 0:32, 0:128] = jnp.where(pz == 0, 0.0, rim)

    mi, mrest = divmod_const(iota((MODES, 256), 0), 25)
    mj = jnp.floor((mrest + 0.5) * 0.2)
    mk = mrest - mj * 5.0
    mode_weight = 8.0 / ((2.0 * mi + 1.0) * (2.0 * mj + 1.0) * (2.0 * mk + 1.0))

    def volume(j, carry):
        base = pl.multiple_of(j * 256, 256)
        cols = pl.ds(base, 256)
        acc = dot(mhh[...], uhl[:, :, cols].reshape(2 * WIDTH, 256)) + dot(
            mlo[...], uhl[0, :, cols]
        )
        scale = mode_weight * jac[:, cols]
        for v in range(NVAR):
            near = jnp.concatenate(
                [trx[v, 0:32, cols], trx[v, 32:64, pl.ds(pl.multiple_of(base + 256, 256), 256)]],
                axis=0,
            )
            high, low = split(near)
            faces = dot(expand_op, jnp.concatenate([high, low], axis=0))
            change = st[v, :, cols] - so[v, :, cols]
            part[v, :, cols] = (
                acc[v * PAD : v * PAD + MODES] + scale * change - penalty[v] * faces[0:MODES]
            )
        return carry

    lax.fori_loop(0, 4, volume, 0)

    for copy in body3:
        copy.wait_recv()
    bodies = bsum2[...] + bgot3[0] + bgot3[1] + bgot3[2]
    tables = []
    for d in range(3):
        x = bodies[d]
        table = [jnp.ones_like(x), x]
        for n in range(1, 4):
            table.append(((2.0 * n + 1.0) * x * table[n] - n * table[n - 1]) / (n + 1.0))
        tables.append(table)
    for i in range(5):
        for j in range(5):
            pair = tables[0][i] * tables[1][j]
            for k in range(5):
                basis[(i * 5 + j) * 5 + k] = pair * tables[2][k]
    for m in range(MODES, PAD):
        basis[m] = jnp.zeros((8, 128), F32)
    for b in range(BODIES):
        rows = slice(b * COVER, (b + 1) * COVER)
        bh, bl = split(basis[:, b, :])
        gh, gl = split(gbody[:, rows, :].reshape(NVAR * COVER, PAD))
        trace = (dot(gh, bh) + dot(gl, bh) + dot(gh, bl)).reshape(NVAR, COVER, 128)
        nx, ny, nz = bodies[3, b : b + 1], bodies[4, b : b + 1], bodies[5, b : b + 1]
        weight = bodies[6, b : b + 1]
        speed = nx * trace[1] + ny * trace[2] + nz * trace[3]
        wall = jnp.concatenate(
            [
                (speed + 0.5 * trace[0]) * weight,
                nx * trace[4] * weight,
                ny * trace[4] * weight,
                nz * trace[4] * weight,
                1.4 * speed * weight,
            ],
            axis=0,
        )
        wh, wl = split(wall)
        lifted = dot_nt(wh, bh) + dot_nt(wl, bh) + dot_nt(wh, bl)
        tbody[:, rows, :] = -lifted.reshape(NVAR, COVER, PAD)

    pltpu.make_async_copy(p2recv, p2recv, p2_recv).wait()
    xh[...] = jnp.zeros_like(xh)
    xl[...] = jnp.zeros_like(xl)
    take = jnp.where(slot_col == iota((CUTS, SLOTS), 1), 1.0, 0.0)
    take = jnp.concatenate([take, jnp.zeros((CPAD - CUTS, SLOTS), F32)], axis=0).astype(BF16)
    for t in range(2):
        for v in range(NVAR):
            got = jnp.concatenate([p2recv[t * 5 + v], p2recv[10 + t * 5 + v]], axis=0)
            high, low = split(-got if t else got)
            rows, lanes = slice(v * CPAD, (v + 1) * CPAD), slice(t * PAD, (t + 1) * PAD)
            xh[rows, lanes] = dot(take, high).astype(BF16)
            xl[rows, lanes] = dot(take, low).astype(BF16)

    _, block_lane = divmod_const(iota((CUTS, 256), 1), CPAD)
    diagonal = jnp.where(block_lane == iota((CUTS, 256), 0).astype(F32), 1.0, 0.0)

    def products(i, carry):
        rows = pl.ds(pl.multiple_of(i * (MBLOCK * CUTS), MBLOCK * CUTS), MBLOCK * CUTS)
        high, low = cuth[rows, :], cutl[rows, :]
        all_pairs = dot_nt(high, xh[...]) + dot_nt(low, xh[...]) + dot_nt(high, xl[...])
        kept = all_pairs.reshape(MBLOCK, CUTS, 256) * diagonal[None]
        tmode[pl.ds(pl.multiple_of(i * MBLOCK, MBLOCK), MBLOCK), :] = jnp.sum(kept, axis=1)
        return carry

    lax.fori_loop(0, PAD // MBLOCK, products, 0)

    high, low = split(tmode[...])
    slotted = dot_nt(place[...], high) + dot_nt(place[...], low)
    p3send[...] = slotted.reshape(2 * NVAR, PEERS, PAD)

    def p3_copy(r):
        peer = lax.rem(me + r, PEERS)
        return pltpu.make_async_remote_copy(
            src_ref=p3send.at[:, pl.ds(peer, 1), :],
            dst_ref=p3recv.at[:, pl.ds(me, 1), :],
            send_sem=p3_send.at[r],
            recv_sem=p3_recv,
            device_id={"py": peer},
            device_id_type=MESH,
        )

    def p3_start(r, carry):
        p3_copy(r).start()
        return carry

    lax.fori_loop(1, PEERS, p3_start, 0)
    pltpu.make_async_copy(
        p3send.at[:, pl.ds(me, 1), :], p3recv.at[:, pl.ds(me, 1), :], p3_recv
    ).start()

    for v in range(NVAR):
        high, low = split(tbody[v].T)
        cover = onehot[SLOTS:, :]
        added = dot(high, cover) + dot(low, cover)
        part[v] = part[v] + added[0:MODES]

    asked_rows[...] = onehot[0:SLOTS, :]
    pltpu.make_async_copy(p3recv, p3recv, p3_recv).wait()
    returned[...] = p3recv[...]

    def finish(r, carry):
        id_copy(r).wait_send()
        p2_copy(r).wait_send()
        p3_copy(r).wait_send()
        return carry

    lax.fori_loop(1, PEERS, finish, 0)
    body1.wait_send()
    for copy in body2 + body3:
        copy.wait_send()
    rim_down.wait_send()
    rim_up.wait_send()


def add_cut_terms(part, got, asked_rows, out_hbm, total, out_sem):
    stores = []
    for v in range(NVAR):
        terms = jnp.concatenate([got[2 * v], got[2 * v + 1]], axis=0)
        high, low = split(terms.T)
        added = dot(high, asked_rows[...]) + dot(low, asked_rows[...])
        total[v] = part[v] + added[0:MODES]
        stores.append(pltpu.make_async_copy(total.at[v], out_hbm.at[v], out_sem.at[v]))
        stores[-1].start()
    for copy in stores:
        copy.wait()


def local(
    current_state,
    state_old,
    jacobian,
    volume_operator_list,
    flux_jacobian_list,
    penalty,
    cut_owner,
    cut_element,
    cut_mass,
    cut_operator,
    body_holder_index,
    body_points,
    body_normals,
    body_weights,
    covered,
):
    hbm = pl.BlockSpec(memory_space=pl.ANY)
    dma = pltpu.SemaphoreType.DMA
    vmem = pl.BlockSpec(memory_space=pltpu.VMEM)
    operands = (
        current_state,
        state_old,
        cut_mass.transpose(1, 0, 2),
        cut_operator.transpose(1, 0, 2),
        jacobian.reshape(1, ELEM),
        volume_operator_list,
        flux_jacobian_list.transpose(1, 0, 2),
        penalty,
        cut_owner.reshape(1, CUTS),
        cut_element.reshape(1, CUTS),
        body_holder_index,
        body_points,
        body_normals,
        body_weights,
        covered,
    )
    partial = pl.pallas_call(
        kernel,
        out_shape=(
            pltpu.VMEM((NVAR, MODES, ELEM), F32),
            pltpu.VMEM((2 * NVAR, PEERS, PAD), F32),
            pltpu.VMEM((SLOTS, ELEM), BF16),
        ),
        in_specs=[hbm] * 15,
        out_specs=(vmem, vmem, vmem),
        scratch_shapes=[
            pltpu.VMEM((1, ELEM), F32),
            pltpu.VMEM((3, MODES, MODES), F32),
            pltpu.SMEM((NVAR, 3, NVAR), F32),
            pltpu.SMEM((NVAR,), F32),
            pltpu.VMEM((1, CUTS), jnp.int32),
            pltpu.VMEM((1, CUTS), jnp.int32),
            pltpu.SMEM((BODIES,), jnp.int32),
            pltpu.VMEM((BODIES, 3, 128), F32),
            pltpu.VMEM((BODIES, 3, 128), F32),
            pltpu.VMEM((BODIES, 128), F32),
            pltpu.VMEM((BODIES, COVER), jnp.int32),
            pltpu.VMEM((NVAR, MODES, ELEM), F32),
            pltpu.VMEM((NVAR, MODES, ELEM), F32),
            pltpu.VMEM((2, MODES, CUTS, MODES), F32),
            pltpu.VMEM((2, WIDTH, ELEM), BF16),
            pltpu.VMEM((2, WIDTH, ELEM), BF16),
            pltpu.VMEM((3, PAD, PAD), F32),
            pltpu.VMEM((WIDTH, 2 * WIDTH), BF16),
            pltpu.VMEM((WIDTH, WIDTH), BF16),
            pltpu.VMEM((NVAR, 64, ELEM + 256), F32),
            pltpu.VMEM((PAD * CUTS, 256), BF16),
            pltpu.VMEM((PAD * CUTS, 256), BF16),
            pltpu.VMEM((1, 128), jnp.int32),
            pltpu.VMEM((PEERS, 128), jnp.int32),
            pltpu.VMEM((TERMS, ELEM), BF16),
            pltpu.VMEM((NVAR * SLOTS, 256), BF16),
            pltpu.VMEM((4 * NVAR, PEERS, PAD), F32),
            pltpu.VMEM((4 * NVAR, PEERS, PAD), F32),
            pltpu.VMEM((2 * NVAR, PEERS, PAD), F32),
            pltpu.VMEM((2 * NVAR, PEERS, PAD), F32),
            pltpu.VMEM((NVAR, BODIES * COVER, PAD), F32),
            pltpu.VMEM((256, 256), BF16),
            pltpu.VMEM((256, 256), BF16),
            pltpu.VMEM((PAD, 256), F32),
            pltpu.VMEM((7, 8, 128), F32),
            pltpu.VMEM((7, 8, 128), F32),
            pltpu.VMEM((7, 8, 128), F32),
            pltpu.VMEM((3, 7, 8, 128), F32),
            pltpu.VMEM((7, 8, 128), F32),
            pltpu.VMEM((3, 7, 8, 128), F32),
            pltpu.VMEM((PAD, 8, 128), F32),
            pltpu.VMEM((NVAR, BODIES * COVER, PAD), F32),
            dma((4,)),
            dma((11,)),
            dma((2,)),
            dma((2,)),
            dma((PEERS,)),
            dma,
            dma((PEERS,)),
            dma,
            dma((PEERS,)),
            dma,
            dma((7,)),
            dma((7,)),
        ],
        compiler_params=pltpu.CompilerParams(
            collective_id=0, has_side_effects=True, vmem_limit_bytes=44 * 1024 * 1024
        ),
        name="residual_step",
    )(
        *(pltpu.with_memory_space_constraint(x, pltpu.HBM) for x in operands)
    )
    return pl.pallas_call(
        add_cut_terms,
        out_shape=jax.ShapeDtypeStruct((NVAR, MODES, ELEM), F32),
        in_specs=[vmem] * 3,
        out_specs=hbm,
        scratch_shapes=[pltpu.VMEM((NVAR, MODES, ELEM), F32), dma((NVAR,))],
        compiler_params=pltpu.CompilerParams(vmem_limit_bytes=16 * 1024 * 1024),
        name="add_cut_terms",
    )(*partial)


def solution(mesh):
    in_specs = (
        P(None, None, ("px", "py")),
        P(None, None, ("px", "py")),
        P(("px", "py")),
        P(),
        P(),
        P(),
        P(("px", "py"), None),
        P(("px", "py")),
        P(("px", "py"), None, None),
        P(("px", "py"), None, None),
        P("px"),
        P(("px", "py"), None, None),
        P(("px", "py"), None, None),
        P(("px", "py"), None),
        P(("px", "py"), None),
    )
    out_specs = P(None, None, ("px", "py"))
    return jax.shard_map(local, mesh=mesh, in_specs=in_specs, out_specs=out_specs, check_vma=False)
```

```python
import functools

import jax
import jax.numpy as jnp
from jax import lax
from jax.experimental import pallas as pl
from jax.experimental.pallas import tpu as pltpu
from jax.sharding import PartitionSpec as P

F32 = jnp.float32
BF16 = jnp.bfloat16
MESH = pl.DeviceIdType.MESH
NVAR = 5
MODES = 125
PAD = 128
ELEM = 1024
PEERS = 32
CUTS = 40
CPAD = 48
SLOTS = 64
BODIES = 6
COVER = 16
TERMS = SLOTS + BODIES * COVER
WIDTH = NVAR * PAD
MBLOCK = 64


def split(value):
    high = value.astype(BF16)
    low = (value - high.astype(F32)).astype(BF16)
    return high, low


def dot(left, right):
    return jnp.dot(left, right, preferred_element_type=F32)


def dot_nt(left, right):
    return lax.dot_general(left, right, (((1,), (1,)), ((), ())), preferred_element_type=F32)


def iota(shape, dim):
    return lax.broadcasted_iota(jnp.int32, shape, dim)


def divmod_const(index, by):
    exact = index.astype(F32)
    whole = jnp.floor((exact + 0.5) * (1.0 / by))
    return whole, exact - whole * by


def parity_of(whole):
    return 1.0 - 2.0 * (whole - 2.0 * jnp.floor(whole * 0.5))


def pad_rows(value):
    zero = jnp.zeros((PAD - value.shape[0], value.shape[1]), value.dtype)
    return jnp.concatenate([value, zero], axis=0)


def pad_lanes(value):
    zero = jnp.zeros((value.shape[0], PAD - value.shape[1]), value.dtype)
    return jnp.concatenate([value, zero], axis=1)


def to_column(row, rows, lanes):
    spread = jnp.broadcast_to(row, (rows, lanes))
    pick = iota((rows, lanes), 0) == iota((rows, lanes), 1)
    return jnp.sum(jnp.where(pick, spread, 0), axis=1, keepdims=True)


def kernel(
    state_hbm,
    old_hbm,
    mass_hbm,
    oper_hbm,
    jac_hbm,
    vol_hbm,
    flux_hbm,
    penalty_hbm,
    owner_hbm,
    elem_hbm,
    holder_hbm,
    points_hbm,
    normals_hbm,
    weights_hbm,
    covered_hbm,
    part,
    returned,
    asked_rows,
    jac,
    vol,
    flux,
    penalty,
    owner,
    elem,
    holder,
    points,
    normals,
    weights,
    covered,
    st,
    so,
    mats,
    uhl,
    chl,
    vpad,
    mhh,
    mlo,
    trx,
    cuth,
    cutl,
    ids_row,
    ids_all,
    onehot,
    place,
    p2send,
    p2recv,
    p3send,
    p3recv,
    gbody,
    xh,
    xl,
    tmode,
    bown,
    bgot1,
    bsum1,
    bgot2,
    bsum2,
    bgot3,
    basis,
    tbody,
    load_sem,
    small_sem,
    rim_send,
    rim_recv,
    id_send,
    id_recv,
    p2_send,
    p2_recv,
    p3_send,
    p3_recv,
    b_send,
    b_recv,
):
    me = lax.axis_index("py")
    pz = lax.axis_index("px")
    npx = lax.axis_size("px")

    barrier = pltpu.get_barrier_semaphore()
    above = lax.rem(pz + 1, npx)
    below = lax.rem(pz + npx - 1, npx)

    def greet(r, carry):
        pl.semaphore_signal(
            barrier, inc=1, device_id={"py": lax.rem(me + r, PEERS)}, device_id_type=MESH
        )
        return carry

    lax.fori_loop(1, PEERS, greet, 0)
    for neighbour in (above, below):
        pl.semaphore_signal(barrier, inc=1, device_id={"px": neighbour}, device_id_type=MESH)

    load_state = pltpu.make_async_copy(state_hbm, st, load_sem.at[0])
    load_old = pltpu.make_async_copy(old_hbm, so, load_sem.at[1])
    load_mass = pltpu.make_async_copy(mass_hbm, mats.at[0], load_sem.at[2])
    load_oper = pltpu.make_async_copy(oper_hbm, mats.at[1], load_sem.at[3])
    pairs = (
        (owner_hbm, owner),
        (elem_hbm, elem),
        (covered_hbm, covered),
        (holder_hbm, holder),
        (points_hbm, points),
        (normals_hbm, normals),
        (weights_hbm, weights),
        (penalty_hbm, penalty),
        (flux_hbm, flux),
        (vol_hbm, vol),
        (jac_hbm, jac),
    )
    smalls = [
        pltpu.make_async_copy(source, target, small_sem.at[i])
        for i, (source, target) in enumerate(pairs)
    ]
    for copy in smalls:
        copy.start()
    for copy in smalls:
        copy.wait()
    load_state.start()
    load_old.start()

    own_row = jnp.broadcast_to(owner[...], (CUTS, CUTS))
    own_col = to_column(owner[...], CUTS, CUTS)
    elem_col = to_column(elem[...], CUTS, CUTS)
    same = own_row == own_col
    row_c, lane_c = iota((CUTS, CUTS), 0), iota((CUTS, CUTS), 1)
    pos_col = jnp.sum(jnp.where(same & (lane_c < row_c), 1, 0), axis=1, keepdims=True)
    pos_row = jnp.sum(jnp.where(same & (row_c < lane_c), 1, 0), axis=0, keepdims=True)
    slot_col = pos_col * PEERS + own_col
    slot_row = pos_row * PEERS + owner[...]
    placed = jnp.where(slot_col == iota((CUTS, PAD), 1), elem_col + 1, 0)
    ids_row[...] = jnp.sum(placed, axis=0, keepdims=True) - 1

    _, spread_lane = divmod_const(iota((CUTS, 256), 1), CPAD)
    spread = jnp.where(spread_lane == iota((CUTS, 256), 0).astype(F32), 1.0, 0.0)
    slots_f = jnp.sum(spread * slot_col.astype(F32), axis=0, keepdims=True)
    lane_v, lane_in = divmod_const(iota((1, 256), 1), CPAD)
    target = jnp.where((lane_in < CUTS) & (lane_v < NVAR), lane_v * SLOTS + slots_f, -1.0)
    place[...] = jnp.where(
        target == iota((NVAR * SLOTS, 256), 0).astype(F32), 1.0, 0.0
    ).astype(BF16)

    cover_lane = iota((COVER, ELEM), 1)
    for b in range(BODIES):
        wanted = to_column(covered[b : b + 1, :], COVER, COVER)
        start = SLOTS + b * COVER
        onehot[start : start + COVER, :] = jnp.where(wanted == cover_lane, 1.0, 0.0).astype(BF16)

    bown[...] = jnp.zeros_like(bown)
    body_row = iota((BODIES, 128), 0)
    held = jnp.zeros((BODIES, 128), jnp.int32)
    for b in range(BODIES):
        held = jnp.where(body_row == b, jnp.where(holder[b] == me, 1, 0), held)
    held = held == 1
    for d in range(3):
        bown[d, 0:BODIES, :] = jnp.where(held, points[:, d, :], 0.0)
        bown[3 + d, 0:BODIES, :] = jnp.where(held, normals[:, d, :], 0.0)
    bown[6, 0:BODIES, :] = jnp.where(held, weights[...], 0.0)

    ri, rf = divmod_const(iota((PAD, PAD), 0), 25)
    ti, tf = divmod_const(iota((64, PAD), 1), 25)
    tr_row = iota((64, PAD), 0)
    tr_lower = tr_row >= 32
    tr_f = jnp.where(tr_lower, tr_row - 32, tr_row).astype(F32)
    trace_op = jnp.where(
        (tf == tr_f) & (ti < 5.0), jnp.where(tr_lower, parity_of(ti), 1.0), 0.0
    ).astype(BF16)
    l64 = lax.rem(iota((PAD, PAD), 1), 64)
    l32 = lax.rem(iota((PAD, PAD), 1), 32)
    expand_op = jnp.where(
        (rf == l32.astype(F32)) & (ri < 5.0), jnp.where(l64 < 32, parity_of(ri), 1.0), 0.0
    ).astype(BF16)

    vpad[...] = jnp.zeros_like(vpad)
    for d in range(3):
        vpad[d, 0:MODES, 0:MODES] = vol[d]
    ci, cf = divmod_const(iota((PAD, PAD), 1), 25)
    inside = (ri < 5.0) & (ci < 5.0)
    own_face = jnp.where(inside & (rf == cf), 1.0 + parity_of(ri) * parity_of(ci), 0.0)

    def build(v, carry):
        rows = pl.ds(pl.multiple_of(v * PAD, PAD), PAD)
        for w in range(NVAR):
            block = jnp.where(v == w, penalty[v], 0.0) * own_face
            for d in range(3):
                block = block - flux[v, d, w] * vpad[d]
            high, low = split(block)
            mhh[rows, w * PAD : (w + 1) * PAD] = high
            mhh[rows, WIDTH + w * PAD : WIDTH + (w + 1) * PAD] = high
            mlo[rows, w * PAD : (w + 1) * PAD] = low
        return carry

    lax.fori_loop(0, NVAR, build, 0)

    pl.semaphore_wait(barrier, PEERS + 1)

    def id_copy(r):
        return pltpu.make_async_remote_copy(
            src_ref=ids_row,
            dst_ref=ids_all.at[pl.ds(me, 1), :],
            send_sem=id_send.at[r],
            recv_sem=id_recv,
            device_id={"py": lax.rem(me + r, PEERS)},
            device_id_type=MESH,
        )

    def id_start(r, carry):
        id_copy(r).start()
        return carry

    lax.fori_loop(1, PEERS, id_start, 0)
    pltpu.make_async_copy(ids_row, ids_all.at[pl.ds(me, 1), :], id_recv).start()

    core = lax.rem(me, 2)
    px_in = lax.rem(me // 2, 4)
    py_in = me // 8
    sibling = me + 1 - 2 * core
    body1 = pltpu.make_async_remote_copy(
        src_ref=bown,
        dst_ref=bgot1,
        send_sem=b_send.at[0],
        recv_sem=b_recv.at[0],
        device_id={"py": sibling},
        device_id_type=MESH,
    )
    body1.start()

    load_state.wait()
    load_old.wait()
    load_mass.start()
    load_oper.start()

    def split_state(j, carry):
        cols = pl.ds(pl.multiple_of(j * 256, 256), 256)
        tcols = pl.ds(pl.multiple_of(j * 256 + 128, 128), 256)
        for v in range(NVAR):
            rows = pl.ds(v * PAD, PAD)
            u = st[v, :, cols]
            high, low = split(pad_rows(u))
            uhl[0, rows, cols] = high
            uhl[1, rows, cols] = low
            trx[v, :, tcols] = dot(trace_op, high) + dot(trace_op, low)
            high, low = split(pad_rows(u - so[v, :, cols]))
            chl[0, rows, cols] = high
            chl[1, rows, cols] = low
        return carry

    lax.fori_loop(0, 4, split_state, 0)
    rim_down = pltpu.make_async_remote_copy(
        src_ref=trx.at[:, 32:64, 128:256],
        dst_ref=trx.at[:, 32:64, 1152:1280],
        send_sem=rim_send.at[0],
        recv_sem=rim_recv.at[0],
        device_id={"px": below},
        device_id_type=MESH,
    )
    rim_up = pltpu.make_async_remote_copy(
        src_ref=trx.at[:, 0:32, 1024:1152],
        dst_ref=trx.at[:, 0:32, 0:128],
        send_sem=rim_send.at[1],
        recv_sem=rim_recv.at[1],
        device_id={"px": above},
        device_id_type=MESH,
    )
    rim_down.start()
    rim_up.start()

    body1.wait_recv()
    bsum1[...] = bown[...] + bgot1[...]
    body2 = []
    for r in range(1, 4):
        body2.append(
            pltpu.make_async_remote_copy(
                src_ref=bsum1,
                dst_ref=bgot2.at[r - 1],
                send_sem=b_send.at[r],
                recv_sem=b_recv.at[r],
                device_id={"py": py_in * 8 + lax.rem(px_in + r, 4) * 2 + core},
                device_id_type=MESH,
            )
        )
        body2[-1].start()

    load_mass.wait()
    load_oper.wait()

    def split_cut(i, carry):
        rows = pl.ds(pl.multiple_of(i * (8 * CUTS), 8 * CUTS), 8 * CUTS)
        for t in range(2):
            high, low = split(pad_lanes(mats[t, pl.ds(i * 8, 8)].reshape(8 * CUTS, MODES)))
            cuth[rows, t * PAD : (t + 1) * PAD] = high
            cutl[rows, t * PAD : (t + 1) * PAD] = low
        return carry

    lax.fori_loop(0, MODES // 8, split_cut, 0)
    whole = MODES // 8 * 8
    for t in range(2):
        tail = pad_lanes(mats[t, whole:MODES].reshape((MODES - whole) * CUTS, MODES))
        zero = jnp.zeros(((PAD - MODES) * CUTS, PAD), F32)
        high, low = split(jnp.concatenate([tail, zero], axis=0))
        cuth[whole * CUTS :, t * PAD : (t + 1) * PAD] = high
        cutl[whole * CUTS :, t * PAD : (t + 1) * PAD] = low

    pltpu.make_async_copy(ids_all, ids_all, id_recv).wait()
    asked = ids_all[...]
    lane = iota((PEERS, 128), 1)
    elem_lane = iota((PEERS, ELEM), 1)
    for k in range(2):
        wanted = jnp.sum(jnp.where(lane == me + k * PEERS, asked, 0), axis=1, keepdims=True)
        rows = slice(k * PEERS, (k + 1) * PEERS)
        onehot[rows, :] = jnp.where(wanted == elem_lane, 1.0, 0.0).astype(BF16)
    state_high = dot_nt(onehot[...], uhl[0])
    state_low = dot_nt(onehot[...], uhl[1])
    state_cols = state_high + state_low
    change_cols = dot_nt(onehot[0:SLOTS, :], chl[0]) + dot_nt(onehot[0:SLOTS, :], chl[1])
    for k in range(2):
        rows = slice(k * PEERS, (k + 1) * PEERS)
        for v in range(NVAR):
            lanes = slice(v * PAD, (v + 1) * PAD)
            p2send[k * 10 + v] = change_cols[rows, lanes]
            p2send[k * 10 + 5 + v] = state_cols[rows, lanes]
    for v in range(NVAR):
        gbody[v] = state_cols[SLOTS:, v * PAD : (v + 1) * PAD]

    def p2_copy(r):
        peer = lax.rem(me + r, PEERS)
        return pltpu.make_async_remote_copy(
            src_ref=p2send.at[:, pl.ds(peer, 1), :],
            dst_ref=p2recv.at[:, pl.ds(me, 1), :],
            send_sem=p2_send.at[r],
            recv_sem=p2_recv,
            device_id={"py": peer},
            device_id_type=MESH,
        )

    def p2_start(r, carry):
        p2_copy(r).start()
        return carry

    lax.fori_loop(1, PEERS, p2_start, 0)
    pltpu.make_async_copy(
        p2send.at[:, pl.ds(me, 1), :], p2recv.at[:, pl.ds(me, 1), :], p2_recv
    ).start()

    for copy in body2:
        copy.wait_recv()
    bsum2[...] = bsum1[...] + bgot2[0] + bgot2[1] + bgot2[2]
    body3 = []
    for r in range(1, 4):
        body3.append(
            pltpu.make_async_remote_copy(
                src_ref=bsum2,
                dst_ref=bgot3.at[r - 1],
                send_sem=b_send.at[3 + r],
                recv_sem=b_recv.at[3 + r],
                device_id={"py": lax.rem(py_in + r, 4) * 8 + px_in * 2 + core},
                device_id_type=MESH,
            )
        )
        body3[-1].start()

    rim_down.wait_recv()
    rim_up.wait_recv()
    rim = trx[:, 32:64, 1152:1280]
    trx[:, 32:64, 1152:1280] = jnp.where(pz == npx - 1, 0.0, rim)
    rim = trx[:, 0:32, 0:128]
    trx[:, 0:32, 0:128] = jnp.where(pz == 0, 0.0, rim)

    mi, mrest = divmod_const(iota((MODES, 256), 0), 25)
    mj = jnp.floor((mrest + 0.5) * 0.2)
    mk = mrest - mj * 5.0
    mode_weight = 8.0 / ((2.0 * mi + 1.0) * (2.0 * mj + 1.0) * (2.0 * mk + 1.0))

    def volume(j, carry):
        base = pl.multiple_of(j * 256, 256)
        cols = pl.ds(base, 256)
        acc = dot(mhh[...], uhl[:, :, cols].reshape(2 * WIDTH, 256)) + dot(
            mlo[...], uhl[0, :, cols]
        )
        scale = mode_weight * jac[:, cols]
        for v in range(NVAR):
            near = jnp.concatenate(
                [trx[v, 0:32, cols], trx[v, 32:64, pl.ds(pl.multiple_of(base + 256, 256), 256)]],
                axis=0,
            )
            high, low = split(near)
            faces = dot(expand_op, jnp.concatenate([high, low], axis=0))
            change = st[v, :, cols] - so[v, :, cols]
            part[v, :, cols] = (
                acc[v * PAD : v * PAD + MODES] + scale * change - penalty[v] * faces[0:MODES]
            )
        return carry

    lax.fori_loop(0, 4, volume, 0)

    pltpu.make_async_copy(p2recv, p2recv, p2_recv).wait()
    xh[...] = jnp.zeros_like(xh)
    xl[...] = jnp.zeros_like(xl)
    take = jnp.where(slot_col == iota((CUTS, SLOTS), 1), 1.0, 0.0)
    take = jnp.concatenate([take, jnp.zeros((CPAD - CUTS, SLOTS), F32)], axis=0).astype(BF16)
    for t in range(2):
        for v in range(NVAR):
            got = jnp.concatenate([p2recv[t * 5 + v], p2recv[10 + t * 5 + v]], axis=0)
            high, low = split(-got if t else got)
            rows, lanes = slice(v * CPAD, (v + 1) * CPAD), slice(t * PAD, (t + 1) * PAD)
            xh[rows, lanes] = dot(take, high).astype(BF16)
            xl[rows, lanes] = dot(take, low).astype(BF16)

    _, block_lane = divmod_const(iota((CUTS, 256), 1), CPAD)
    diagonal = jnp.where(block_lane == iota((CUTS, 256), 0).astype(F32), 1.0, 0.0)

    for i in range(PAD // MBLOCK):
        rows = slice(i * MBLOCK * CUTS, (i + 1) * MBLOCK * CUTS)
        high, low = cuth[rows, :], cutl[rows, :]
        all_pairs = dot_nt(high, xh[...]) + (dot_nt(low, xh[...]) + dot_nt(high, xl[...]))
        kept = all_pairs.reshape(MBLOCK, CUTS, 256) * diagonal[None]
        tmode[i * MBLOCK : (i + 1) * MBLOCK, :] = jnp.sum(kept, axis=1)

    high, low = split(tmode[...])
    slotted = dot_nt(place[...], high) + dot_nt(place[...], low)
    p3send[...] = slotted.reshape(2 * NVAR, PEERS, PAD)

    def p3_copy(r):
        peer = lax.rem(me + r, PEERS)
        return pltpu.make_async_remote_copy(
            src_ref=p3send.at[:, pl.ds(peer, 1), :],
            dst_ref=p3recv.at[:, pl.ds(me, 1), :],
            send_sem=p3_send.at[r],
            recv_sem=p3_recv,
            device_id={"py": peer},
            device_id_type=MESH,
        )

    def p3_start(r, carry):
        p3_copy(r).start()
        return carry

    lax.fori_loop(1, PEERS, p3_start, 0)
    pltpu.make_async_copy(
        p3send.at[:, pl.ds(me, 1), :], p3recv.at[:, pl.ds(me, 1), :], p3_recv
    ).start()

    for copy in body3:
        copy.wait_recv()
    bodies = bsum2[...] + bgot3[0] + bgot3[1] + bgot3[2]
    tables = []
    for d in range(3):
        x = bodies[d]
        table = [jnp.ones_like(x), x]
        for n in range(1, 4):
            table.append(((2.0 * n + 1.0) * x * table[n] - n * table[n - 1]) / (n + 1.0))
        tables.append(table)
    for i in range(5):
        for j in range(5):
            pair = tables[0][i] * tables[1][j]
            for k in range(5):
                basis[(i * 5 + j) * 5 + k] = pair * tables[2][k]
    for m in range(MODES, PAD):
        basis[m] = jnp.zeros((8, 128), F32)
    for b in range(BODIES):
        rows = slice(b * COVER, (b + 1) * COVER)
        bh, bl = split(basis[:, b, :])
        gh, gl = split(gbody[:, rows, :].reshape(NVAR * COVER, PAD))
        trace = (dot(gh, bh) + dot(gl, bh) + dot(gh, bl)).reshape(NVAR, COVER, 128)
        nx, ny, nz = bodies[3, b : b + 1], bodies[4, b : b + 1], bodies[5, b : b + 1]
        weight = bodies[6, b : b + 1]
        speed = nx * trace[1] + ny * trace[2] + nz * trace[3]
        wall = jnp.concatenate(
            [
                (speed + 0.5 * trace[0]) * weight,
                nx * trace[4] * weight,
                ny * trace[4] * weight,
                nz * trace[4] * weight,
                1.4 * speed * weight,
            ],
            axis=0,
        )
        wh, wl = split(wall)
        lifted = dot_nt(wh, bh) + dot_nt(wl, bh) + dot_nt(wh, bl)
        tbody[:, rows, :] = -lifted.reshape(NVAR, COVER, PAD)

    for v in range(NVAR):
        high, low = split(tbody[v].T)
        cover = onehot[SLOTS:, :]
        added = dot(high, cover) + dot(low, cover)
        part[v] = part[v] + added[0:MODES]

    def left_before(r, carry):
        id_copy(r).wait_send()
        p2_copy(r).wait_send()
        return carry

    lax.fori_loop(1, PEERS, left_before, 0)
    body1.wait_send()
    for copy in body2 + body3:
        copy.wait_send()
    rim_down.wait_send()
    rim_up.wait_send()
    asked_rows[...] = onehot[0:SLOTS, :]

    pltpu.make_async_copy(p3recv, p3recv, p3_recv).wait()
    returned[...] = p3recv[...]

    def left(r, carry):
        p3_copy(r).wait_send()
        return carry

    lax.fori_loop(1, PEERS, left, 0)


def add_cut_terms(part, got, asked_rows, out_hbm, total, out_sem):
    rows = jnp.concatenate([asked_rows[...], asked_rows[...]], axis=0)
    stores = []
    for v in range(NVAR):
        terms = jnp.concatenate([got[2 * v], got[2 * v + 1]], axis=0)
        added = dot(jnp.concatenate(split(terms.T), axis=1), rows)
        total[v] = part[v] + added[0:MODES]
        stores.append(pltpu.make_async_copy(total.at[v], out_hbm.at[v], out_sem.at[v]))
        stores[-1].start()
    for copy in stores:
        copy.wait()


def local(
    current_state,
    state_old,
    jacobian,
    volume_operator_list,
    flux_jacobian_list,
    penalty,
    cut_owner,
    cut_element,
    cut_mass,
    cut_operator,
    body_holder_index,
    body_points,
    body_normals,
    body_weights,
    covered,
):
    hbm = pl.BlockSpec(memory_space=pl.ANY)
    dma = pltpu.SemaphoreType.DMA
    vmem = pl.BlockSpec(memory_space=pltpu.VMEM)
    operands = (
        current_state,
        state_old,
        cut_mass.transpose(1, 0, 2),
        cut_operator.transpose(1, 0, 2),
        jacobian.reshape(1, ELEM),
        volume_operator_list,
        flux_jacobian_list.transpose(1, 0, 2),
        penalty,
        cut_owner.reshape(1, CUTS),
        cut_element.reshape(1, CUTS),
        body_holder_index,
        body_points,
        body_normals,
        body_weights,
        covered,
    )
    partial = pl.pallas_call(
        kernel,
        out_shape=(
            pltpu.VMEM((NVAR, MODES, ELEM), F32),
            pltpu.VMEM((2 * NVAR, PEERS, PAD), F32),
            pltpu.VMEM((SLOTS, ELEM), BF16),
        ),
        in_specs=[hbm] * 15,
        out_specs=(vmem, vmem, vmem),
        scratch_shapes=[
            pltpu.VMEM((1, ELEM), F32),
            pltpu.VMEM((3, MODES, MODES), F32),
            pltpu.SMEM((NVAR, 3, NVAR), F32),
            pltpu.SMEM((NVAR,), F32),
            pltpu.VMEM((1, CUTS), jnp.int32),
            pltpu.VMEM((1, CUTS), jnp.int32),
            pltpu.SMEM((BODIES,), jnp.int32),
            pltpu.VMEM((BODIES, 3, 128), F32),
            pltpu.VMEM((BODIES, 3, 128), F32),
            pltpu.VMEM((BODIES, 128), F32),
            pltpu.VMEM((BODIES, COVER), jnp.int32),
            pltpu.VMEM((NVAR, MODES, ELEM), F32),
            pltpu.VMEM((NVAR, MODES, ELEM), F32),
            pltpu.VMEM((2, MODES, CUTS, MODES), F32),
            pltpu.VMEM((2, WIDTH, ELEM), BF16),
            pltpu.VMEM((2, WIDTH, ELEM), BF16),
            pltpu.VMEM((3, PAD, PAD), F32),
            pltpu.VMEM((WIDTH, 2 * WIDTH), BF16),
            pltpu.VMEM((WIDTH, WIDTH), BF16),
            pltpu.VMEM((NVAR, 64, ELEM + 256), F32),
            pltpu.VMEM((PAD * CUTS, 256), BF16),
            pltpu.VMEM((PAD * CUTS, 256), BF16),
            pltpu.VMEM((1, 128), jnp.int32),
            pltpu.VMEM((PEERS, 128), jnp.int32),
            pltpu.VMEM((TERMS, ELEM), BF16),
            pltpu.VMEM((NVAR * SLOTS, 256), BF16),
            pltpu.VMEM((4 * NVAR, PEERS, PAD), F32),
            pltpu.VMEM((4 * NVAR, PEERS, PAD), F32),
            pltpu.VMEM((2 * NVAR, PEERS, PAD), F32),
            pltpu.VMEM((2 * NVAR, PEERS, PAD), F32),
            pltpu.VMEM((NVAR, BODIES * COVER, PAD), F32),
            pltpu.VMEM((256, 256), BF16),
            pltpu.VMEM((256, 256), BF16),
            pltpu.VMEM((PAD, 256), F32),
            pltpu.VMEM((7, 8, 128), F32),
            pltpu.VMEM((7, 8, 128), F32),
            pltpu.VMEM((7, 8, 128), F32),
            pltpu.VMEM((3, 7, 8, 128), F32),
            pltpu.VMEM((7, 8, 128), F32),
            pltpu.VMEM((3, 7, 8, 128), F32),
            pltpu.VMEM((PAD, 8, 128), F32),
            pltpu.VMEM((NVAR, BODIES * COVER, PAD), F32),
            dma((4,)),
            dma((11,)),
            dma((2,)),
            dma((2,)),
            dma((PEERS,)),
            dma,
            dma((PEERS,)),
            dma,
            dma((PEERS,)),
            dma,
            dma((7,)),
            dma((7,)),
        ],
        compiler_params=pltpu.CompilerParams(
            collective_id=0, has_side_effects=True, vmem_limit_bytes=44 * 1024 * 1024
        ),
        name="residual_step",
    )(
        *(pltpu.with_memory_space_constraint(x, pltpu.HBM) for x in operands)
    )
    return pl.pallas_call(
        add_cut_terms,
        out_shape=jax.ShapeDtypeStruct((NVAR, MODES, ELEM), F32),
        in_specs=[vmem] * 3,
        out_specs=hbm,
        scratch_shapes=[pltpu.VMEM((NVAR, MODES, ELEM), F32), dma((NVAR,))],
        compiler_params=pltpu.CompilerParams(vmem_limit_bytes=16 * 1024 * 1024),
        name="add_cut_terms",
    )(*partial)


def solution(mesh):
    in_specs = (
        P(None, None, ("px", "py")),
        P(None, None, ("px", "py")),
        P(("px", "py")),
        P(),
        P(),
        P(),
        P(("px", "py"), None),
        P(("px", "py")),
        P(("px", "py"), None, None),
        P(("px", "py"), None, None),
        P("px"),
        P(("px", "py"), None, None),
        P(("px", "py"), None, None),
        P(("px", "py"), None),
        P(("px", "py"), None),
    )
    out_specs = P(None, None, ("px", "py"))
    return jax.shard_map(local, mesh=mesh, in_specs=in_specs, out_specs=out_specs, check_vma=False)
```

```python
import functools

import jax
import jax.numpy as jnp
from jax import lax
from jax.experimental import pallas as pl
from jax.experimental.pallas import tpu as pltpu
from jax.sharding import PartitionSpec as P

F32 = jnp.float32
BF16 = jnp.bfloat16
MESH = pl.DeviceIdType.MESH
NVAR = 5
MODES = 125
PAD = 128
ELEM = 1024
PEERS = 32
CUTS = 40
CPAD = 48
SLOTS = 64
BODIES = 6
COVER = 16
TERMS = SLOTS + BODIES * COVER
WIDTH = NVAR * PAD
MBLOCK = 64


def split(value):
    high = value.astype(BF16)
    low = (value - high.astype(F32)).astype(BF16)
    return high, low


def dot(left, right):
    return jnp.dot(left, right, preferred_element_type=F32)


def dot_nt(left, right):
    return lax.dot_general(left, right, (((1,), (1,)), ((), ())), preferred_element_type=F32)


def iota(shape, dim):
    return lax.broadcasted_iota(jnp.int32, shape, dim)


def divmod_const(index, by):
    exact = index.astype(F32)
    whole = jnp.floor((exact + 0.5) * (1.0 / by))
    return whole, exact - whole * by


def parity_of(whole):
    return 1.0 - 2.0 * (whole - 2.0 * jnp.floor(whole * 0.5))


def pad_rows(value):
    zero = jnp.zeros((PAD - value.shape[0], value.shape[1]), value.dtype)
    return jnp.concatenate([value, zero], axis=0)


def pad_lanes(value):
    zero = jnp.zeros((value.shape[0], PAD - value.shape[1]), value.dtype)
    return jnp.concatenate([value, zero], axis=1)


def to_column(row, rows, lanes):
    spread = jnp.broadcast_to(row, (rows, lanes))
    pick = iota((rows, lanes), 0) == iota((rows, lanes), 1)
    return jnp.sum(jnp.where(pick, spread, 0), axis=1, keepdims=True)


def kernel(
    state_hbm,
    old_hbm,
    mass_hbm,
    oper_hbm,
    jac_hbm,
    vol_hbm,
    flux_hbm,
    penalty_hbm,
    owner_hbm,
    elem_hbm,
    holder_hbm,
    points_hbm,
    normals_hbm,
    weights_hbm,
    covered_hbm,
    part,
    returned,
    asked_rows,
    jac,
    vol,
    flux,
    penalty,
    owner,
    elem,
    holder,
    points,
    normals,
    weights,
    covered,
    st,
    so,
    mats,
    uhl,
    chl,
    vpad,
    mhh,
    mlo,
    trx,
    cuth,
    cutl,
    ids_row,
    ids_all,
    onehot,
    place,
    p2send,
    p2recv,
    p3send,
    p3recv,
    gbody,
    xh,
    xl,
    tmode,
    bown,
    bgot1,
    bsum1,
    bgot2,
    bsum2,
    bgot3,
    basis,
    tbody,
    load_sem,
    small_sem,
    rim_send,
    rim_recv,
    id_send,
    id_recv,
    p2_send,
    p2_recv,
    p3_send,
    p3_recv,
    b_send,
    b_recv,
):
    me = lax.axis_index("py")
    pz = lax.axis_index("px")
    npx = lax.axis_size("px")

    barrier = pltpu.get_barrier_semaphore()
    above = lax.rem(pz + 1, npx)
    below = lax.rem(pz + npx - 1, npx)

    def greet(r, carry):
        pl.semaphore_signal(
            barrier, inc=1, device_id={"py": lax.rem(me + r, PEERS)}, device_id_type=MESH
        )
        return carry

    lax.fori_loop(1, PEERS, greet, 0)
    has_above = pz < npx - 1
    has_below = pz > 0

    @pl.when(has_above)
    def _():
        pl.semaphore_signal(barrier, inc=1, device_id={"px": above}, device_id_type=MESH)

    @pl.when(has_below)
    def _():
        pl.semaphore_signal(barrier, inc=1, device_id={"px": below}, device_id_type=MESH)


    load_state = pltpu.make_async_copy(state_hbm, st, load_sem.at[0])
    load_old = pltpu.make_async_copy(old_hbm, so, load_sem.at[1])
    load_mass = pltpu.make_async_copy(mass_hbm, mats.at[0], load_sem.at[2])
    load_oper = pltpu.make_async_copy(oper_hbm, mats.at[1], load_sem.at[3])
    pairs = (
        (owner_hbm, owner),
        (elem_hbm, elem),
        (covered_hbm, covered),
        (holder_hbm, holder),
        (points_hbm, points),
        (normals_hbm, normals),
        (weights_hbm, weights),
        (penalty_hbm, penalty),
        (flux_hbm, flux),
        (vol_hbm, vol),
        (jac_hbm, jac),
    )
    smalls = [
        pltpu.make_async_copy(source, target, small_sem.at[i])
        for i, (source, target) in enumerate(pairs)
    ]
    for copy in smalls:
        copy.start()
    for copy in smalls:
        copy.wait()
    load_state.start()
    load_old.start()

    own_row = jnp.broadcast_to(owner[...], (CUTS, CUTS))
    own_col = to_column(owner[...], CUTS, CUTS)
    elem_col = to_column(elem[...], CUTS, CUTS)
    same = own_row == own_col
    row_c, lane_c = iota((CUTS, CUTS), 0), iota((CUTS, CUTS), 1)
    pos_col = jnp.sum(jnp.where(same & (lane_c < row_c), 1, 0), axis=1, keepdims=True)
    pos_row = jnp.sum(jnp.where(same & (row_c < lane_c), 1, 0), axis=0, keepdims=True)
    slot_col = pos_col * PEERS + own_col
    slot_row = pos_row * PEERS + owner[...]
    placed = jnp.where(slot_col == iota((CUTS, PAD), 1), elem_col + 1, 0)
    ids_row[...] = jnp.sum(placed, axis=0, keepdims=True) - 1

    _, spread_lane = divmod_const(iota((CUTS, 256), 1), CPAD)
    spread = jnp.where(spread_lane == iota((CUTS, 256), 0).astype(F32), 1.0, 0.0)
    slots_f = jnp.sum(spread * slot_col.astype(F32), axis=0, keepdims=True)
    lane_v, lane_in = divmod_const(iota((1, 256), 1), CPAD)
    target = jnp.where((lane_in < CUTS) & (lane_v < NVAR), lane_v * SLOTS + slots_f, -1.0)
    place[...] = jnp.where(
        target == iota((NVAR * SLOTS, 256), 0).astype(F32), 1.0, 0.0
    ).astype(BF16)

    cover_lane = iota((COVER, ELEM), 1)
    for b in range(BODIES):
        wanted = to_column(covered[b : b + 1, :], COVER, COVER)
        start = SLOTS + b * COVER
        onehot[start : start + COVER, :] = jnp.where(wanted == cover_lane, 1.0, 0.0).astype(BF16)

    bown[...] = jnp.zeros_like(bown)
    body_row = iota((BODIES, 128), 0)
    held = jnp.zeros((BODIES, 128), jnp.int32)
    for b in range(BODIES):
        held = jnp.where(body_row == b, jnp.where(holder[b] == me, 1, 0), held)
    held = held == 1
    for d in range(3):
        bown[d, 0:BODIES, :] = jnp.where(held, points[:, d, :], 0.0)
        bown[3 + d, 0:BODIES, :] = jnp.where(held, normals[:, d, :], 0.0)
    bown[6, 0:BODIES, :] = jnp.where(held, weights[...], 0.0)

    ri, rf = divmod_const(iota((PAD, PAD), 0), 25)
    ti, tf = divmod_const(iota((64, PAD), 1), 25)
    tr_row = iota((64, PAD), 0)
    tr_lower = tr_row >= 32
    tr_f = jnp.where(tr_lower, tr_row - 32, tr_row).astype(F32)
    trace_op = jnp.where(
        (tf == tr_f) & (ti < 5.0), jnp.where(tr_lower, parity_of(ti), 1.0), 0.0
    ).astype(BF16)
    l64 = lax.rem(iota((PAD, PAD), 1), 64)
    l32 = lax.rem(iota((PAD, PAD), 1), 32)
    expand_op = jnp.where(
        (rf == l32.astype(F32)) & (ri < 5.0), jnp.where(l64 < 32, parity_of(ri), 1.0), 0.0
    ).astype(BF16)

    vpad[...] = jnp.zeros_like(vpad)
    for d in range(3):
        vpad[d, 0:MODES, 0:MODES] = vol[d]
    ci, cf = divmod_const(iota((PAD, PAD), 1), 25)
    inside = (ri < 5.0) & (ci < 5.0)
    own_face = jnp.where(inside & (rf == cf), 1.0 + parity_of(ri) * parity_of(ci), 0.0)

    def build(v, carry):
        rows = pl.ds(pl.multiple_of(v * PAD, PAD), PAD)
        for w in range(NVAR):
            block = jnp.where(v == w, penalty[v], 0.0) * own_face
            for d in range(3):
                block = block - flux[v, d, w] * vpad[d]
            high, low = split(block)
            mhh[rows, w * PAD : (w + 1) * PAD] = high
            mhh[rows, WIDTH + w * PAD : WIDTH + (w + 1) * PAD] = high
            mlo[rows, w * PAD : (w + 1) * PAD] = low
        return carry

    lax.fori_loop(0, NVAR, build, 0)

    nearby = jnp.where(has_above, 1, 0) + jnp.where(has_below, 1, 0)
    pl.semaphore_wait(barrier, PEERS - 1 + nearby)

    def id_copy(r):
        return pltpu.make_async_remote_copy(
            src_ref=ids_row,
            dst_ref=ids_all.at[pl.ds(me, 1), :],
            send_sem=id_send.at[r],
            recv_sem=id_recv,
            device_id={"py": lax.rem(me + r, PEERS)},
            device_id_type=MESH,
        )

    def id_start(r, carry):
        id_copy(r).start()
        return carry

    lax.fori_loop(1, PEERS, id_start, 0)
    pltpu.make_async_copy(ids_row, ids_all.at[pl.ds(me, 1), :], id_recv).start()

    core = lax.rem(me, 2)
    px_in = lax.rem(me // 2, 4)
    py_in = me // 8
    sibling = me + 1 - 2 * core
    body1 = pltpu.make_async_remote_copy(
        src_ref=bown,
        dst_ref=bgot1,
        send_sem=b_send.at[0],
        recv_sem=b_recv.at[0],
        device_id={"py": sibling},
        device_id_type=MESH,
    )
    body1.start()

    load_state.wait()
    load_old.wait()
    load_mass.start()
    load_oper.start()

    def split_state(j, carry):
        cols = pl.ds(pl.multiple_of(j * 256, 256), 256)
        tcols = pl.ds(pl.multiple_of(j * 256 + 128, 128), 256)
        for v in range(NVAR):
            rows = pl.ds(v * PAD, PAD)
            u = st[v, :, cols]
            high, low = split(pad_rows(u))
            uhl[0, rows, cols] = high
            uhl[1, rows, cols] = low
            trx[v, :, tcols] = dot(trace_op, high) + dot(trace_op, low)
            high, low = split(pad_rows(u - so[v, :, cols]))
            chl[0, rows, cols] = high
            chl[1, rows, cols] = low
        return carry

    lax.fori_loop(0, 4, split_state, 0)
    rim_down = pltpu.make_async_remote_copy(
        src_ref=trx.at[:, 32:64, 128:256],
        dst_ref=trx.at[:, 32:64, 1152:1280],
        send_sem=rim_send.at[0],
        recv_sem=rim_recv.at[0],
        device_id={"px": below},
        device_id_type=MESH,
    )
    rim_up = pltpu.make_async_remote_copy(
        src_ref=trx.at[:, 0:32, 1024:1152],
        dst_ref=trx.at[:, 0:32, 0:128],
        send_sem=rim_send.at[1],
        recv_sem=rim_recv.at[1],
        device_id={"px": above},
        device_id_type=MESH,
    )

    @pl.when(has_below)
    def _():
        rim_down.start()

    @pl.when(has_above)
    def _():
        rim_up.start()


    body1.wait_recv()
    bsum1[...] = bown[...] + bgot1[...]
    body2 = []
    for r in range(1, 4):
        body2.append(
            pltpu.make_async_remote_copy(
                src_ref=bsum1,
                dst_ref=bgot2.at[r - 1],
                send_sem=b_send.at[r],
                recv_sem=b_recv.at[r],
                device_id={"py": py_in * 8 + lax.rem(px_in + r, 4) * 2 + core},
                device_id_type=MESH,
            )
        )
        body2[-1].start()

    load_mass.wait()
    load_oper.wait()

    def split_cut(i, carry):
        rows = pl.ds(pl.multiple_of(i * (8 * CUTS), 8 * CUTS), 8 * CUTS)
        for t in range(2):
            high, low = split(pad_lanes(mats[t, pl.ds(i * 8, 8)].reshape(8 * CUTS, MODES)))
            cuth[rows, t * PAD : (t + 1) * PAD] = high
            cutl[rows, t * PAD : (t + 1) * PAD] = low
        return carry

    lax.fori_loop(0, MODES // 8, split_cut, 0)
    whole = MODES // 8 * 8
    for t in range(2):
        tail = pad_lanes(mats[t, whole:MODES].reshape((MODES - whole) * CUTS, MODES))
        zero = jnp.zeros(((PAD - MODES) * CUTS, PAD), F32)
        high, low = split(jnp.concatenate([tail, zero], axis=0))
        cuth[whole * CUTS :, t * PAD : (t + 1) * PAD] = high
        cutl[whole * CUTS :, t * PAD : (t + 1) * PAD] = low

    pltpu.make_async_copy(ids_all, ids_all, id_recv).wait()
    asked = ids_all[...]
    lane = iota((PEERS, 128), 1)
    elem_lane = iota((PEERS, ELEM), 1)
    for k in range(2):
        wanted = jnp.sum(jnp.where(lane == me + k * PEERS, asked, 0), axis=1, keepdims=True)
        rows = slice(k * PEERS, (k + 1) * PEERS)
        onehot[rows, :] = jnp.where(wanted == elem_lane, 1.0, 0.0).astype(BF16)
    state_high = dot_nt(onehot[...], uhl[0])
    state_low = dot_nt(onehot[...], uhl[1])
    state_cols = state_high + state_low
    change_cols = dot_nt(onehot[0:SLOTS, :], chl[0]) + dot_nt(onehot[0:SLOTS, :], chl[1])
    for k in range(2):
        rows = slice(k * PEERS, (k + 1) * PEERS)
        for v in range(NVAR):
            lanes = slice(v * PAD, (v + 1) * PAD)
            p2send[k * 10 + v] = change_cols[rows, lanes]
            p2send[k * 10 + 5 + v] = state_cols[rows, lanes]
    for v in range(NVAR):
        gbody[v] = state_cols[SLOTS:, v * PAD : (v + 1) * PAD]

    def p2_copy(r):
        peer = lax.rem(me + r, PEERS)
        return pltpu.make_async_remote_copy(
            src_ref=p2send.at[:, pl.ds(peer, 1), :],
            dst_ref=p2recv.at[:, pl.ds(me, 1), :],
            send_sem=p2_send.at[r],
            recv_sem=p2_recv,
            device_id={"py": peer},
            device_id_type=MESH,
        )

    def p2_start(r, carry):
        p2_copy(r).start()
        return carry

    lax.fori_loop(1, PEERS, p2_start, 0)
    pltpu.make_async_copy(
        p2send.at[:, pl.ds(me, 1), :], p2recv.at[:, pl.ds(me, 1), :], p2_recv
    ).start()

    for copy in body2:
        copy.wait_recv()
    bsum2[...] = bsum1[...] + bgot2[0] + bgot2[1] + bgot2[2]
    body3 = []
    for r in range(1, 4):
        body3.append(
            pltpu.make_async_remote_copy(
                src_ref=bsum2,
                dst_ref=bgot3.at[r - 1],
                send_sem=b_send.at[3 + r],
                recv_sem=b_recv.at[3 + r],
                device_id={"py": lax.rem(py_in + r, 4) * 8 + px_in * 2 + core},
                device_id_type=MESH,
            )
        )
        body3[-1].start()

    @pl.when(has_above)
    def _():
        rim_down.wait_recv()

    @pl.when(jnp.logical_not(has_above))
    def _():
        trx[:, 32:64, 1152:1280] = jnp.zeros((NVAR, 32, 128), F32)

    @pl.when(has_below)
    def _():
        rim_up.wait_recv()

    @pl.when(jnp.logical_not(has_below))
    def _():
        trx[:, 0:32, 0:128] = jnp.zeros((NVAR, 32, 128), F32)

    mi, mrest = divmod_const(iota((MODES, 256), 0), 25)
    mj = jnp.floor((mrest + 0.5) * 0.2)
    mk = mrest - mj * 5.0
    mode_weight = 8.0 / ((2.0 * mi + 1.0) * (2.0 * mj + 1.0) * (2.0 * mk + 1.0))

    def volume(j, carry):
        base = pl.multiple_of(j * 256, 256)
        cols = pl.ds(base, 256)
        acc = dot(mhh[...], uhl[:, :, cols].reshape(2 * WIDTH, 256)) + dot(
            mlo[...], uhl[0, :, cols]
        )
        scale = mode_weight * jac[:, cols]
        for v in range(NVAR):
            near = jnp.concatenate(
                [trx[v, 0:32, cols], trx[v, 32:64, pl.ds(pl.multiple_of(base + 256, 256), 256)]],
                axis=0,
            )
            high, low = split(near)
            faces = dot(expand_op, jnp.concatenate([high, low], axis=0))
            change = st[v, :, cols] - so[v, :, cols]
            part[v, :, cols] = (
                acc[v * PAD : v * PAD + MODES] + scale * change - penalty[v] * faces[0:MODES]
            )
        return carry

    lax.fori_loop(0, 4, volume, 0)

    pltpu.make_async_copy(p2recv, p2recv, p2_recv).wait()
    xh[...] = jnp.zeros_like(xh)
    xl[...] = jnp.zeros_like(xl)
    take = jnp.where(slot_col == iota((CUTS, SLOTS), 1), 1.0, 0.0)
    take = jnp.concatenate([take, jnp.zeros((CPAD - CUTS, SLOTS), F32)], axis=0).astype(BF16)
    for t in range(2):
        for v in range(NVAR):
            got = jnp.concatenate([p2recv[t * 5 + v], p2recv[10 + t * 5 + v]], axis=0)
            high, low = split(-got if t else got)
            rows, lanes = slice(v * CPAD, (v + 1) * CPAD), slice(t * PAD, (t + 1) * PAD)
            xh[rows, lanes] = dot(take, high).astype(BF16)
            xl[rows, lanes] = dot(take, low).astype(BF16)

    _, block_lane = divmod_const(iota((CUTS, 256), 1), CPAD)
    diagonal = jnp.where(block_lane == iota((CUTS, 256), 0).astype(F32), 1.0, 0.0)

    for i in range(PAD // MBLOCK):
        rows = slice(i * MBLOCK * CUTS, (i + 1) * MBLOCK * CUTS)
        high, low = cuth[rows, :], cutl[rows, :]
        all_pairs = dot_nt(high, xh[...]) + (dot_nt(low, xh[...]) + dot_nt(high, xl[...]))
        kept = all_pairs.reshape(MBLOCK, CUTS, 256) * diagonal[None]
        tmode[i * MBLOCK : (i + 1) * MBLOCK, :] = jnp.sum(kept, axis=1)

    high, low = split(tmode[...])
    slotted = dot_nt(place[...], high) + dot_nt(place[...], low)
    p3send[...] = slotted.reshape(2 * NVAR, PEERS, PAD)

    def p3_copy(r):
        peer = lax.rem(me + r, PEERS)
        return pltpu.make_async_remote_copy(
            src_ref=p3send.at[:, pl.ds(peer, 1), :],
            dst_ref=p3recv.at[:, pl.ds(me, 1), :],
            send_sem=p3_send.at[r],
            recv_sem=p3_recv,
            device_id={"py": peer},
            device_id_type=MESH,
        )

    def p3_start(r, carry):
        p3_copy(r).start()
        return carry

    lax.fori_loop(1, PEERS, p3_start, 0)
    pltpu.make_async_copy(
        p3send.at[:, pl.ds(me, 1), :], p3recv.at[:, pl.ds(me, 1), :], p3_recv
    ).start()

    for copy in body3:
        copy.wait_recv()
    bodies = bsum2[...] + bgot3[0] + bgot3[1] + bgot3[2]
    tables = []
    for d in range(3):
        x = bodies[d]
        table = [jnp.ones_like(x), x]
        for n in range(1, 4):
            table.append(((2.0 * n + 1.0) * x * table[n] - n * table[n - 1]) / (n + 1.0))
        tables.append(table)
    for i in range(5):
        for j in range(5):
            pair = tables[0][i] * tables[1][j]
            for k in range(5):
                basis[(i * 5 + j) * 5 + k] = pair * tables[2][k]
    for m in range(MODES, PAD):
        basis[m] = jnp.zeros((8, 128), F32)
    for b in range(BODIES):
        rows = slice(b * COVER, (b + 1) * COVER)
        bh, bl = split(basis[:, b, :])
        gh, gl = split(gbody[:, rows, :].reshape(NVAR * COVER, PAD))
        trace = (dot(gh, bh) + dot(gl, bh) + dot(gh, bl)).reshape(NVAR, COVER, 128)
        nx, ny, nz = bodies[3, b : b + 1], bodies[4, b : b + 1], bodies[5, b : b + 1]
        weight = bodies[6, b : b + 1]
        speed = nx * trace[1] + ny * trace[2] + nz * trace[3]
        wall = jnp.concatenate(
            [
                (speed + 0.5 * trace[0]) * weight,
                nx * trace[4] * weight,
                ny * trace[4] * weight,
                nz * trace[4] * weight,
                1.4 * speed * weight,
            ],
            axis=0,
        )
        wh, wl = split(wall)
        lifted = dot_nt(wh, bh) + dot_nt(wl, bh) + dot_nt(wh, bl)
        tbody[:, rows, :] = -lifted.reshape(NVAR, COVER, PAD)

    for v in range(NVAR):
        high, low = split(tbody[v].T)
        cover = onehot[SLOTS:, :]
        added = dot(high, cover) + dot(low, cover)
        part[v] = part[v] + added[0:MODES]

    def left_before(r, carry):
        id_copy(r).wait_send()
        p2_copy(r).wait_send()
        return carry

    lax.fori_loop(1, PEERS, left_before, 0)
    body1.wait_send()
    for copy in body2 + body3:
        copy.wait_send()

    @pl.when(has_below)
    def _():
        rim_down.wait_send()

    @pl.when(has_above)
    def _():
        rim_up.wait_send()

    asked_rows[...] = onehot[0:SLOTS, :]

    pltpu.make_async_copy(p3recv, p3recv, p3_recv).wait()
    returned[...] = p3recv[...]

    def left(r, carry):
        p3_copy(r).wait_send()
        return carry

    lax.fori_loop(1, PEERS, left, 0)


def add_cut_terms(part, got, asked_rows, out_hbm, total, out_sem):
    rows = jnp.concatenate([asked_rows[...], asked_rows[...]], axis=0)
    stores = []
    for v in range(NVAR):
        terms = jnp.concatenate([got[2 * v], got[2 * v + 1]], axis=0)
        added = dot(jnp.concatenate(split(terms.T), axis=1), rows)
        total[v] = part[v] + added[0:MODES]
        stores.append(pltpu.make_async_copy(total.at[v], out_hbm.at[v], out_sem.at[v]))
        stores[-1].start()
    for copy in stores:
        copy.wait()


def local(
    current_state,
    state_old,
    jacobian,
    volume_operator_list,
    flux_jacobian_list,
    penalty,
    cut_owner,
    cut_element,
    cut_mass,
    cut_operator,
    body_holder_index,
    body_points,
    body_normals,
    body_weights,
    covered,
):
    hbm = pl.BlockSpec(memory_space=pl.ANY)
    dma = pltpu.SemaphoreType.DMA
    vmem = pl.BlockSpec(memory_space=pltpu.VMEM)
    operands = (
        current_state,
        state_old,
        cut_mass.transpose(1, 0, 2),
        cut_operator.transpose(1, 0, 2),
        jacobian.reshape(1, ELEM),
        volume_operator_list,
        flux_jacobian_list.transpose(1, 0, 2),
        penalty,
        cut_owner.reshape(1, CUTS),
        cut_element.reshape(1, CUTS),
        body_holder_index,
        body_points,
        body_normals,
        body_weights,
        covered,
    )
    partial = pl.pallas_call(
        kernel,
        out_shape=(
            pltpu.VMEM((NVAR, MODES, ELEM), F32),
            pltpu.VMEM((2 * NVAR, PEERS, PAD), F32),
            pltpu.VMEM((SLOTS, ELEM), BF16),
        ),
        in_specs=[hbm] * 15,
        out_specs=(vmem, vmem, vmem),
        scratch_shapes=[
            pltpu.VMEM((1, ELEM), F32),
            pltpu.VMEM((3, MODES, MODES), F32),
            pltpu.SMEM((NVAR, 3, NVAR), F32),
            pltpu.SMEM((NVAR,), F32),
            pltpu.VMEM((1, CUTS), jnp.int32),
            pltpu.VMEM((1, CUTS), jnp.int32),
            pltpu.SMEM((BODIES,), jnp.int32),
            pltpu.VMEM((BODIES, 3, 128), F32),
            pltpu.VMEM((BODIES, 3, 128), F32),
            pltpu.VMEM((BODIES, 128), F32),
            pltpu.VMEM((BODIES, COVER), jnp.int32),
            pltpu.VMEM((NVAR, MODES, ELEM), F32),
            pltpu.VMEM((NVAR, MODES, ELEM), F32),
            pltpu.VMEM((2, MODES, CUTS, MODES), F32),
            pltpu.VMEM((2, WIDTH, ELEM), BF16),
            pltpu.VMEM((2, WIDTH, ELEM), BF16),
            pltpu.VMEM((3, PAD, PAD), F32),
            pltpu.VMEM((WIDTH, 2 * WIDTH), BF16),
            pltpu.VMEM((WIDTH, WIDTH), BF16),
            pltpu.VMEM((NVAR, 64, ELEM + 256), F32),
            pltpu.VMEM((PAD * CUTS, 256), BF16),
            pltpu.VMEM((PAD * CUTS, 256), BF16),
            pltpu.VMEM((1, 128), jnp.int32),
            pltpu.VMEM((PEERS, 128), jnp.int32),
            pltpu.VMEM((TERMS, ELEM), BF16),
            pltpu.VMEM((NVAR * SLOTS, 256), BF16),
            pltpu.VMEM((4 * NVAR, PEERS, PAD), F32),
            pltpu.VMEM((4 * NVAR, PEERS, PAD), F32),
            pltpu.VMEM((2 * NVAR, PEERS, PAD), F32),
            pltpu.VMEM((2 * NVAR, PEERS, PAD), F32),
            pltpu.VMEM((NVAR, BODIES * COVER, PAD), F32),
            pltpu.VMEM((256, 256), BF16),
            pltpu.VMEM((256, 256), BF16),
            pltpu.VMEM((PAD, 256), F32),
            pltpu.VMEM((7, 8, 128), F32),
            pltpu.VMEM((7, 8, 128), F32),
            pltpu.VMEM((7, 8, 128), F32),
            pltpu.VMEM((3, 7, 8, 128), F32),
            pltpu.VMEM((7, 8, 128), F32),
            pltpu.VMEM((3, 7, 8, 128), F32),
            pltpu.VMEM((PAD, 8, 128), F32),
            pltpu.VMEM((NVAR, BODIES * COVER, PAD), F32),
            dma((4,)),
            dma((11,)),
            dma((2,)),
            dma((2,)),
            dma((PEERS,)),
            dma,
            dma((PEERS,)),
            dma,
            dma((PEERS,)),
            dma,
            dma((7,)),
            dma((7,)),
        ],
        compiler_params=pltpu.CompilerParams(
            collective_id=0, has_side_effects=True, vmem_limit_bytes=44 * 1024 * 1024
        ),
        name="residual_step",
    )(
        *(pltpu.with_memory_space_constraint(x, pltpu.HBM) for x in operands)
    )
    return pl.pallas_call(
        add_cut_terms,
        out_shape=jax.ShapeDtypeStruct((NVAR, MODES, ELEM), F32),
        in_specs=[vmem] * 3,
        out_specs=hbm,
        scratch_shapes=[pltpu.VMEM((NVAR, MODES, ELEM), F32), dma((NVAR,))],
        compiler_params=pltpu.CompilerParams(vmem_limit_bytes=16 * 1024 * 1024),
        name="add_cut_terms",
    )(*partial)


def solution(mesh):
    in_specs = (
        P(None, None, ("px", "py")),
        P(None, None, ("px", "py")),
        P(("px", "py")),
        P(),
        P(),
        P(),
        P(("px", "py"), None),
        P(("px", "py")),
        P(("px", "py"), None, None),
        P(("px", "py"), None, None),
        P("px"),
        P(("px", "py"), None, None),
        P(("px", "py"), None, None),
        P(("px", "py"), None),
        P(("px", "py"), None),
    )
    out_specs = P(None, None, ("px", "py"))
    return jax.shard_map(local, mesh=mesh, in_specs=in_specs, out_specs=out_specs, check_vma=False)
```

```python
import functools

import jax
import jax.numpy as jnp
from jax import lax
from jax.experimental import pallas as pl
from jax.experimental.pallas import tpu as pltpu
from jax.sharding import PartitionSpec as P

F32 = jnp.float32
BF16 = jnp.bfloat16
MESH = pl.DeviceIdType.MESH
NVAR = 5
MODES = 125
PAD = 128
ELEM = 1024
PEERS = 32
CUTS = 40
CPAD = 48
SLOTS = 64
BODIES = 6
COVER = 16
TERMS = SLOTS + BODIES * COVER
WIDTH = NVAR * PAD
MBLOCK = 64


def split(value):
    high = value.astype(BF16)
    low = (value - high.astype(F32)).astype(BF16)
    return high, low


def dot(left, right):
    return jnp.dot(left, right, preferred_element_type=F32)


def dot_nt(left, right):
    return lax.dot_general(left, right, (((1,), (1,)), ((), ())), preferred_element_type=F32)


def iota(shape, dim):
    return lax.broadcasted_iota(jnp.int32, shape, dim)


def divmod_const(index, by):
    exact = index.astype(F32)
    whole = jnp.floor((exact + 0.5) * (1.0 / by))
    return whole, exact - whole * by


def parity_of(whole):
    return 1.0 - 2.0 * (whole - 2.0 * jnp.floor(whole * 0.5))


def pad_rows(value):
    zero = jnp.zeros((PAD - value.shape[0], value.shape[1]), value.dtype)
    return jnp.concatenate([value, zero], axis=0)


def pad_lanes(value):
    zero = jnp.zeros((value.shape[0], PAD - value.shape[1]), value.dtype)
    return jnp.concatenate([value, zero], axis=1)


def to_column(row, rows, lanes):
    spread = jnp.broadcast_to(row, (rows, lanes))
    pick = iota((rows, lanes), 0) == iota((rows, lanes), 1)
    return jnp.sum(jnp.where(pick, spread, 0), axis=1, keepdims=True)


def kernel(
    state_hbm,
    old_hbm,
    mass_hbm,
    oper_hbm,
    jac_hbm,
    vol_hbm,
    flux_hbm,
    penalty_hbm,
    owner_hbm,
    elem_hbm,
    holder_hbm,
    points_hbm,
    normals_hbm,
    weights_hbm,
    covered_hbm,
    part,
    returned,
    asked_rows,
    jac,
    vol,
    flux,
    penalty,
    owner,
    elem,
    holder,
    points,
    normals,
    weights,
    covered,
    st,
    so,
    mats,
    uhl,
    across,
    vpad,
    mhh,
    mlo,
    trx,
    cuth,
    cutl,
    ids_row,
    ids_all,
    onehot,
    place,
    p2send,
    p2recv,
    p3send,
    p3recv,
    gbody,
    xh,
    xl,
    tmode,
    bown,
    bgot1,
    bsum1,
    bgot2,
    bsum2,
    bgot3,
    basis,
    tbody,
    load_sem,
    small_sem,
    rim_send,
    rim_recv,
    id_send,
    id_recv,
    p2_send,
    p2_recv,
    p3_send,
    p3_recv,
    b_send,
    b_recv,
):
    me = lax.axis_index("py")
    pz = lax.axis_index("px")
    npx = lax.axis_size("px")

    barrier = pltpu.get_barrier_semaphore()
    above = lax.rem(pz + 1, npx)
    below = lax.rem(pz + npx - 1, npx)

    def greet(r, carry):
        pl.semaphore_signal(
            barrier, inc=1, device_id={"py": lax.rem(me + r, PEERS)}, device_id_type=MESH
        )
        return carry

    lax.fori_loop(1, PEERS, greet, 0)
    has_above = pz < npx - 1
    has_below = pz > 0

    @pl.when(has_above)
    def _():
        pl.semaphore_signal(barrier, inc=1, device_id={"px": above}, device_id_type=MESH)

    @pl.when(has_below)
    def _():
        pl.semaphore_signal(barrier, inc=1, device_id={"px": below}, device_id_type=MESH)


    load_state = pltpu.make_async_copy(state_hbm, st, load_sem.at[0])
    load_old = pltpu.make_async_copy(old_hbm, so, load_sem.at[1])
    load_mass = pltpu.make_async_copy(mass_hbm, mats.at[0], load_sem.at[2])
    load_oper = pltpu.make_async_copy(oper_hbm, mats.at[1], load_sem.at[3])
    pairs = (
        (owner_hbm, owner),
        (elem_hbm, elem),
        (covered_hbm, covered),
        (holder_hbm, holder),
        (points_hbm, points),
        (normals_hbm, normals),
        (weights_hbm, weights),
        (penalty_hbm, penalty),
        (flux_hbm, flux),
        (vol_hbm, vol),
        (jac_hbm, jac),
    )
    smalls = [
        pltpu.make_async_copy(source, target, small_sem.at[i])
        for i, (source, target) in enumerate(pairs)
    ]
    for copy in smalls:
        copy.start()
    for copy in smalls:
        copy.wait()
    load_state.start()
    load_old.start()

    own_row = jnp.broadcast_to(owner[...], (CUTS, CUTS))
    own_col = to_column(owner[...], CUTS, CUTS)
    elem_col = to_column(elem[...], CUTS, CUTS)
    same = own_row == own_col
    row_c, lane_c = iota((CUTS, CUTS), 0), iota((CUTS, CUTS), 1)
    pos_col = jnp.sum(jnp.where(same & (lane_c < row_c), 1, 0), axis=1, keepdims=True)
    pos_row = jnp.sum(jnp.where(same & (row_c < lane_c), 1, 0), axis=0, keepdims=True)
    slot_col = pos_col * PEERS + own_col
    slot_row = pos_row * PEERS + owner[...]
    placed = jnp.where(slot_col == iota((CUTS, PAD), 1), elem_col + 1, 0)
    ids_row[...] = jnp.sum(placed, axis=0, keepdims=True) - 1

    _, spread_lane = divmod_const(iota((CUTS, 256), 1), CPAD)
    spread = jnp.where(spread_lane == iota((CUTS, 256), 0).astype(F32), 1.0, 0.0)
    slots_f = jnp.sum(spread * slot_col.astype(F32), axis=0, keepdims=True)
    lane_v, lane_in = divmod_const(iota((1, 256), 1), CPAD)
    target = jnp.where((lane_in < CUTS) & (lane_v < NVAR), lane_v * SLOTS + slots_f, -1.0)
    place[...] = jnp.where(
        target == iota((NVAR * SLOTS, 256), 0).astype(F32), 1.0, 0.0
    ).astype(BF16)

    cover_lane = iota((COVER, ELEM), 1)
    for b in range(BODIES):
        wanted = to_column(covered[b : b + 1, :], COVER, COVER)
        start = SLOTS + b * COVER
        onehot[start : start + COVER, :] = jnp.where(wanted == cover_lane, 1.0, 0.0).astype(BF16)

    bown[...] = jnp.zeros_like(bown)
    body_row = iota((BODIES, 128), 0)
    held = jnp.zeros((BODIES, 128), jnp.int32)
    for b in range(BODIES):
        held = jnp.where(body_row == b, jnp.where(holder[b] == me, 1, 0), held)
    held = held == 1
    for d in range(3):
        bown[d, 0:BODIES, :] = jnp.where(held, points[:, d, :], 0.0)
        bown[3 + d, 0:BODIES, :] = jnp.where(held, normals[:, d, :], 0.0)
    bown[6, 0:BODIES, :] = jnp.where(held, weights[...], 0.0)

    ri, rf = divmod_const(iota((PAD, PAD), 0), 25)
    ti, tf = divmod_const(iota((64, PAD), 1), 25)
    tr_row = iota((64, PAD), 0)
    tr_lower = tr_row >= 32
    tr_f = jnp.where(tr_lower, tr_row - 32, tr_row).astype(F32)
    trace_op = jnp.where(
        (tf == tr_f) & (ti < 5.0), jnp.where(tr_lower, parity_of(ti), 1.0), 0.0
    ).astype(BF16)
    l64 = lax.rem(iota((PAD, PAD), 1), 64)
    l32 = lax.rem(iota((PAD, PAD), 1), 32)
    expand_op = jnp.where(
        (rf == l32.astype(F32)) & (ri < 5.0), jnp.where(l64 < 32, parity_of(ri), 1.0), 0.0
    ).astype(BF16)

    vpad[...] = jnp.zeros_like(vpad)
    for d in range(3):
        vpad[d, 0:MODES, 0:MODES] = vol[d]
    ci, cf = divmod_const(iota((PAD, PAD), 1), 25)
    inside = (ri < 5.0) & (ci < 5.0)
    own_face = jnp.where(inside & (rf == cf), 1.0 + parity_of(ri) * parity_of(ci), 0.0)

    def build(v, carry):
        rows = pl.ds(pl.multiple_of(v * PAD, PAD), PAD)
        for w in range(NVAR):
            block = jnp.where(v == w, penalty[v], 0.0) * own_face
            for d in range(3):
                block = block - flux[v, d, w] * vpad[d]
            high, low = split(block)
            mhh[rows, w * PAD : (w + 1) * PAD] = high
            mhh[rows, WIDTH + w * PAD : WIDTH + (w + 1) * PAD] = high
            mlo[rows, w * PAD : (w + 1) * PAD] = low
        return carry

    lax.fori_loop(0, NVAR, build, 0)

    nearby = jnp.where(has_above, 1, 0) + jnp.where(has_below, 1, 0)
    pl.semaphore_wait(barrier, PEERS - 1 + nearby)

    def id_copy(r):
        return pltpu.make_async_remote_copy(
            src_ref=ids_row,
            dst_ref=ids_all.at[pl.ds(me, 1), :],
            send_sem=id_send.at[r],
            recv_sem=id_recv,
            device_id={"py": lax.rem(me + r, PEERS)},
            device_id_type=MESH,
        )

    def id_start(r, carry):
        id_copy(r).start()
        return carry

    lax.fori_loop(1, PEERS, id_start, 0, unroll=True)
    pltpu.make_async_copy(ids_row, ids_all.at[pl.ds(me, 1), :], id_recv).start()

    core = lax.rem(me, 2)
    px_in = lax.rem(me // 2, 4)
    py_in = me // 8
    sibling = me + 1 - 2 * core
    body1 = pltpu.make_async_remote_copy(
        src_ref=bown,
        dst_ref=bgot1,
        send_sem=b_send.at[0],
        recv_sem=b_recv.at[0],
        device_id={"py": sibling},
        device_id_type=MESH,
    )
    body1.start()

    load_state.wait()
    load_old.wait()
    load_mass.start()
    load_oper.start()

    def split_state(j, carry):
        cols = pl.ds(pl.multiple_of(j * 256, 256), 256)
        tcols = pl.ds(pl.multiple_of(j * 256 + 128, 128), 256)
        for v in range(NVAR):
            rows = pl.ds(v * PAD, PAD)
            u = pad_rows(st[v, :, cols])
            high, low = split(u)
            uhl[0, rows, cols] = high
            uhl[1, rows, cols] = low
            trx[v, :, tcols] = dot(trace_op, high) + dot(trace_op, low)
            high, low = split(u.T)
            across[0, cols, rows] = high
            across[1, cols, rows] = low
            high, low = split((u - pad_rows(so[v, :, cols])).T)
            across[2, cols, rows] = high
            across[3, cols, rows] = low
        return carry

    lax.fori_loop(0, 4, split_state, 0)
    rim_down = pltpu.make_async_remote_copy(
        src_ref=trx.at[:, 32:64, 128:256],
        dst_ref=trx.at[:, 32:64, 1152:1280],
        send_sem=rim_send.at[0],
        recv_sem=rim_recv.at[0],
        device_id={"px": below},
        device_id_type=MESH,
    )
    rim_up = pltpu.make_async_remote_copy(
        src_ref=trx.at[:, 0:32, 1024:1152],
        dst_ref=trx.at[:, 0:32, 0:128],
        send_sem=rim_send.at[1],
        recv_sem=rim_recv.at[1],
        device_id={"px": above},
        device_id_type=MESH,
    )

    @pl.when(has_below)
    def _():
        rim_down.start()

    @pl.when(has_above)
    def _():
        rim_up.start()


    body1.wait_recv()
    bsum1[...] = bown[...] + bgot1[...]
    body2 = []
    for r in range(1, 4):
        body2.append(
            pltpu.make_async_remote_copy(
                src_ref=bsum1,
                dst_ref=bgot2.at[r - 1],
                send_sem=b_send.at[r],
                recv_sem=b_recv.at[r],
                device_id={"py": py_in * 8 + lax.rem(px_in + r, 4) * 2 + core},
                device_id_type=MESH,
            )
        )
        body2[-1].start()

    pltpu.make_async_copy(ids_all, ids_all, id_recv).wait()
    asked = ids_all[...]
    lane = iota((PEERS, 128), 1)
    elem_lane = iota((PEERS, ELEM), 1)
    for k in range(2):
        wanted = jnp.sum(jnp.where(lane == me + k * PEERS, asked, 0), axis=1, keepdims=True)
        rows = slice(k * PEERS, (k + 1) * PEERS)
        onehot[rows, :] = jnp.where(wanted == elem_lane, 1.0, 0.0).astype(BF16)
    state_high = dot(onehot[...], across[0])
    state_low = dot(onehot[...], across[1])
    state_cols = state_high + state_low
    asking = onehot[0:SLOTS, :]
    change_cols = dot(asking, across[2]) + dot(asking, across[3])
    for k in range(2):
        rows = slice(k * PEERS, (k + 1) * PEERS)
        for v in range(NVAR):
            lanes = slice(v * PAD, (v + 1) * PAD)
            p2send[k * 10 + v] = change_cols[rows, lanes]
            p2send[k * 10 + 5 + v] = state_cols[rows, lanes]
    for v in range(NVAR):
        gbody[v] = state_cols[SLOTS:, v * PAD : (v + 1) * PAD]

    def p2_copy(r):
        peer = lax.rem(me + r, PEERS)
        return pltpu.make_async_remote_copy(
            src_ref=p2send.at[:, pl.ds(peer, 1), :],
            dst_ref=p2recv.at[:, pl.ds(me, 1), :],
            send_sem=p2_send.at[r],
            recv_sem=p2_recv,
            device_id={"py": peer},
            device_id_type=MESH,
        )

    def p2_start(r, carry):
        p2_copy(r).start()
        return carry

    lax.fori_loop(1, PEERS, p2_start, 0, unroll=True)
    pltpu.make_async_copy(
        p2send.at[:, pl.ds(me, 1), :], p2recv.at[:, pl.ds(me, 1), :], p2_recv
    ).start()

    @pl.when(has_above)
    def _():
        rim_down.wait_recv()

    @pl.when(jnp.logical_not(has_above))
    def _():
        trx[:, 32:64, 1152:1280] = jnp.zeros((NVAR, 32, 128), F32)

    @pl.when(has_below)
    def _():
        rim_up.wait_recv()

    @pl.when(jnp.logical_not(has_below))
    def _():
        trx[:, 0:32, 0:128] = jnp.zeros((NVAR, 32, 128), F32)

    mi, mrest = divmod_const(iota((MODES, 256), 0), 25)
    mj = jnp.floor((mrest + 0.5) * 0.2)
    mk = mrest - mj * 5.0
    mode_weight = 8.0 / ((2.0 * mi + 1.0) * (2.0 * mj + 1.0) * (2.0 * mk + 1.0))

    def volume(j, carry):
        base = pl.multiple_of(j * 256, 256)
        cols = pl.ds(base, 256)
        acc = dot(mhh[...], uhl[:, :, cols].reshape(2 * WIDTH, 256)) + dot(
            mlo[...], uhl[0, :, cols]
        )
        scale = mode_weight * jac[:, cols]
        for v in range(NVAR):
            near = jnp.concatenate(
                [trx[v, 0:32, cols], trx[v, 32:64, pl.ds(pl.multiple_of(base + 256, 256), 256)]],
                axis=0,
            )
            high, low = split(near)
            faces = dot(expand_op, jnp.concatenate([high, low], axis=0))
            change = st[v, :, cols] - so[v, :, cols]
            part[v, :, cols] = (
                acc[v * PAD : v * PAD + MODES] + scale * change - penalty[v] * faces[0:MODES]
            )
        return carry

    lax.fori_loop(0, 4, volume, 0)

    for copy in body2:
        copy.wait_recv()
    bsum2[...] = bsum1[...] + bgot2[0] + bgot2[1] + bgot2[2]
    body3 = []
    for r in range(1, 4):
        body3.append(
            pltpu.make_async_remote_copy(
                src_ref=bsum2,
                dst_ref=bgot3.at[r - 1],
                send_sem=b_send.at[3 + r],
                recv_sem=b_recv.at[3 + r],
                device_id={"py": lax.rem(py_in + r, 4) * 8 + px_in * 2 + core},
                device_id_type=MESH,
            )
        )
        body3[-1].start()

    load_mass.wait()
    load_oper.wait()

    def split_cut(i, carry):
        rows = pl.ds(pl.multiple_of(i * (8 * CUTS), 8 * CUTS), 8 * CUTS)
        for t in range(2):
            high, low = split(pad_lanes(mats[t, pl.ds(i * 8, 8)].reshape(8 * CUTS, MODES)))
            cuth[rows, t * PAD : (t + 1) * PAD] = high
            cutl[rows, t * PAD : (t + 1) * PAD] = low
        return carry

    lax.fori_loop(0, MODES // 8, split_cut, 0)
    whole = MODES // 8 * 8
    for t in range(2):
        tail = pad_lanes(mats[t, whole:MODES].reshape((MODES - whole) * CUTS, MODES))
        zero = jnp.zeros(((PAD - MODES) * CUTS, PAD), F32)
        high, low = split(jnp.concatenate([tail, zero], axis=0))
        cuth[whole * CUTS :, t * PAD : (t + 1) * PAD] = high
        cutl[whole * CUTS :, t * PAD : (t + 1) * PAD] = low

    pltpu.make_async_copy(p2recv, p2recv, p2_recv).wait()
    xh[...] = jnp.zeros_like(xh)
    xl[...] = jnp.zeros_like(xl)
    take = jnp.where(slot_col == iota((CUTS, SLOTS), 1), 1.0, 0.0)
    take = jnp.concatenate([take, jnp.zeros((CPAD - CUTS, SLOTS), F32)], axis=0).astype(BF16)
    for t in range(2):
        for v in range(NVAR):
            got = jnp.concatenate([p2recv[t * 5 + v], p2recv[10 + t * 5 + v]], axis=0)
            high, low = split(-got if t else got)
            rows, lanes = slice(v * CPAD, (v + 1) * CPAD), slice(t * PAD, (t + 1) * PAD)
            xh[rows, lanes] = dot(take, high).astype(BF16)
            xl[rows, lanes] = dot(take, low).astype(BF16)

    _, block_lane = divmod_const(iota((CUTS, 256), 1), CPAD)
    diagonal = jnp.where(block_lane == iota((CUTS, 256), 0).astype(F32), 1.0, 0.0)

    for i in range(PAD // MBLOCK):
        rows = slice(i * MBLOCK * CUTS, (i + 1) * MBLOCK * CUTS)
        high, low = cuth[rows, :], cutl[rows, :]
        all_pairs = dot_nt(high, xh[...]) + (dot_nt(low, xh[...]) + dot_nt(high, xl[...]))
        kept = all_pairs.reshape(MBLOCK, CUTS, 256) * diagonal[None]
        tmode[i * MBLOCK : (i + 1) * MBLOCK, :] = jnp.sum(kept, axis=1)

    high, low = split(tmode[...])
    slotted = dot_nt(place[...], high) + dot_nt(place[...], low)
    p3send[...] = slotted.reshape(2 * NVAR, PEERS, PAD)

    def p3_copy(r):
        peer = lax.rem(me + r, PEERS)
        return pltpu.make_async_remote_copy(
            src_ref=p3send.at[:, pl.ds(peer, 1), :],
            dst_ref=p3recv.at[:, pl.ds(me, 1), :],
            send_sem=p3_send.at[r],
            recv_sem=p3_recv,
            device_id={"py": peer},
            device_id_type=MESH,
        )

    def p3_start(r, carry):
        p3_copy(r).start()
        return carry

    lax.fori_loop(1, PEERS, p3_start, 0, unroll=True)
    pltpu.make_async_copy(
        p3send.at[:, pl.ds(me, 1), :], p3recv.at[:, pl.ds(me, 1), :], p3_recv
    ).start()

    for copy in body3:
        copy.wait_recv()
    bodies = bsum2[...] + bgot3[0] + bgot3[1] + bgot3[2]
    tables = []
    for d in range(3):
        x = bodies[d]
        table = [jnp.ones_like(x), x]
        for n in range(1, 4):
            table.append(((2.0 * n + 1.0) * x * table[n] - n * table[n - 1]) / (n + 1.0))
        tables.append(table)
    for i in range(5):
        for j in range(5):
            pair = tables[0][i] * tables[1][j]
            for k in range(5):
                basis[(i * 5 + j) * 5 + k] = pair * tables[2][k]
    for m in range(MODES, PAD):
        basis[m] = jnp.zeros((8, 128), F32)
    for b in range(BODIES):
        rows = slice(b * COVER, (b + 1) * COVER)
        bh, bl = split(basis[:, b, :])
        gh, gl = split(gbody[:, rows, :].reshape(NVAR * COVER, PAD))
        trace = (dot(gh, bh) + dot(gl, bh) + dot(gh, bl)).reshape(NVAR, COVER, 128)
        nx, ny, nz = bodies[3, b : b + 1], bodies[4, b : b + 1], bodies[5, b : b + 1]
        weight = bodies[6, b : b + 1]
        speed = nx * trace[1] + ny * trace[2] + nz * trace[3]
        wall = jnp.concatenate(
            [
                (speed + 0.5 * trace[0]) * weight,
                nx * trace[4] * weight,
                ny * trace[4] * weight,
                nz * trace[4] * weight,
                1.4 * speed * weight,
            ],
            axis=0,
        )
        wh, wl = split(wall)
        lifted = dot_nt(wh, bh) + dot_nt(wl, bh) + dot_nt(wh, bl)
        tbody[:, rows, :] = -lifted.reshape(NVAR, COVER, PAD)

    for v in range(NVAR):
        high, low = split(tbody[v].T)
        cover = onehot[SLOTS:, :]
        added = dot(high, cover) + dot(low, cover)
        part[v] = part[v] + added[0:MODES]

    def left_before(r, carry):
        id_copy(r).wait_send()
        p2_copy(r).wait_send()
        return carry

    lax.fori_loop(1, PEERS, left_before, 0)
    body1.wait_send()
    for copy in body2 + body3:
        copy.wait_send()

    @pl.when(has_below)
    def _():
        rim_down.wait_send()

    @pl.when(has_above)
    def _():
        rim_up.wait_send()

    asked_rows[...] = onehot[0:SLOTS, :]

    pltpu.make_async_copy(p3recv, p3recv, p3_recv).wait()
    returned[...] = p3recv[...]

    def left(r, carry):
        p3_copy(r).wait_send()
        return carry

    lax.fori_loop(1, PEERS, left, 0)


def add_cut_terms(part, got, asked_rows, out_hbm, total, out_sem):
    rows = jnp.concatenate([asked_rows[...], asked_rows[...]], axis=0)
    stores = []
    for v in range(NVAR):
        terms = jnp.concatenate([got[2 * v], got[2 * v + 1]], axis=0)
        added = dot(jnp.concatenate(split(terms.T), axis=1), rows)
        total[v] = part[v] + added[0:MODES]
        stores.append(pltpu.make_async_copy(total.at[v], out_hbm.at[v], out_sem.at[v]))
        stores[-1].start()
    for copy in stores:
        copy.wait()


def local(
    current_state,
    state_old,
    jacobian,
    volume_operator_list,
    flux_jacobian_list,
    penalty,
    cut_owner,
    cut_element,
    cut_mass,
    cut_operator,
    body_holder_index,
    body_points,
    body_normals,
    body_weights,
    covered,
):
    hbm = pl.BlockSpec(memory_space=pl.ANY)
    dma = pltpu.SemaphoreType.DMA
    vmem = pl.BlockSpec(memory_space=pltpu.VMEM)
    operands = (
        current_state,
        state_old,
        cut_mass.transpose(1, 0, 2),
        cut_operator.transpose(1, 0, 2),
        jacobian.reshape(1, ELEM),
        volume_operator_list,
        flux_jacobian_list.transpose(1, 0, 2),
        penalty,
        cut_owner.reshape(1, CUTS),
        cut_element.reshape(1, CUTS),
        body_holder_index,
        body_points,
        body_normals,
        body_weights,
        covered,
    )
    partial = pl.pallas_call(
        kernel,
        out_shape=(
            pltpu.VMEM((NVAR, MODES, ELEM), F32),
            pltpu.VMEM((2 * NVAR, PEERS, PAD), F32),
            pltpu.VMEM((SLOTS, ELEM), BF16),
        ),
        in_specs=[hbm] * 15,
        out_specs=(vmem, vmem, vmem),
        scratch_shapes=[
            pltpu.VMEM((1, ELEM), F32),
            pltpu.VMEM((3, MODES, MODES), F32),
            pltpu.SMEM((NVAR, 3, NVAR), F32),
            pltpu.SMEM((NVAR,), F32),
            pltpu.VMEM((1, CUTS), jnp.int32),
            pltpu.VMEM((1, CUTS), jnp.int32),
            pltpu.SMEM((BODIES,), jnp.int32),
            pltpu.VMEM((BODIES, 3, 128), F32),
            pltpu.VMEM((BODIES, 3, 128), F32),
            pltpu.VMEM((BODIES, 128), F32),
            pltpu.VMEM((BODIES, COVER), jnp.int32),
            pltpu.VMEM((NVAR, MODES, ELEM), F32),
            pltpu.VMEM((NVAR, MODES, ELEM), F32),
            pltpu.VMEM((2, MODES, CUTS, MODES), F32),
            pltpu.VMEM((2, WIDTH, ELEM), BF16),
            pltpu.VMEM((4, ELEM, WIDTH), BF16),
            pltpu.VMEM((3, PAD, PAD), F32),
            pltpu.VMEM((WIDTH, 2 * WIDTH), BF16),
            pltpu.VMEM((WIDTH, WIDTH), BF16),
            pltpu.VMEM((NVAR, 64, ELEM + 256), F32),
            pltpu.VMEM((PAD * CUTS, 256), BF16),
            pltpu.VMEM((PAD * CUTS, 256), BF16),
            pltpu.VMEM((1, 128), jnp.int32),
            pltpu.VMEM((PEERS, 128), jnp.int32),
            pltpu.VMEM((TERMS, ELEM), BF16),
            pltpu.VMEM((NVAR * SLOTS, 256), BF16),
            pltpu.VMEM((4 * NVAR, PEERS, PAD), F32),
            pltpu.VMEM((4 * NVAR, PEERS, PAD), F32),
            pltpu.VMEM((2 * NVAR, PEERS, PAD), F32),
            pltpu.VMEM((2 * NVAR, PEERS, PAD), F32),
            pltpu.VMEM((NVAR, BODIES * COVER, PAD), F32),
            pltpu.VMEM((256, 256), BF16),
            pltpu.VMEM((256, 256), BF16),
            pltpu.VMEM((PAD, 256), F32),
            pltpu.VMEM((7, 8, 128), F32),
            pltpu.VMEM((7, 8, 128), F32),
            pltpu.VMEM((7, 8, 128), F32),
            pltpu.VMEM((3, 7, 8, 128), F32),
            pltpu.VMEM((7, 8, 128), F32),
            pltpu.VMEM((3, 7, 8, 128), F32),
            pltpu.VMEM((PAD, 8, 128), F32),
            pltpu.VMEM((NVAR, BODIES * COVER, PAD), F32),
            dma((4,)),
            dma((11,)),
            dma((2,)),
            dma((2,)),
            dma((PEERS,)),
            dma,
            dma((PEERS,)),
            dma,
            dma((PEERS,)),
            dma,
            dma((7,)),
            dma((7,)),
        ],
        compiler_params=pltpu.CompilerParams(
            collective_id=0, has_side_effects=True, vmem_limit_bytes=44 * 1024 * 1024
        ),
        name="residual_step",
    )(
        *(pltpu.with_memory_space_constraint(x, pltpu.HBM) for x in operands)
    )
    return pl.pallas_call(
        add_cut_terms,
        out_shape=jax.ShapeDtypeStruct((NVAR, MODES, ELEM), F32),
        in_specs=[vmem] * 3,
        out_specs=hbm,
        scratch_shapes=[pltpu.VMEM((NVAR, MODES, ELEM), F32), dma((NVAR,))],
        compiler_params=pltpu.CompilerParams(vmem_limit_bytes=16 * 1024 * 1024),
        name="add_cut_terms",
    )(*partial)


def solution(mesh):
    in_specs = (
        P(None, None, ("px", "py")),
        P(None, None, ("px", "py")),
        P(("px", "py")),
        P(),
        P(),
        P(),
        P(("px", "py"), None),
        P(("px", "py")),
        P(("px", "py"), None, None),
        P(("px", "py"), None, None),
        P("px"),
        P(("px", "py"), None, None),
        P(("px", "py"), None, None),
        P(("px", "py"), None),
        P(("px", "py"), None),
    )
    out_specs = P(None, None, ("px", "py"))
    return jax.shard_map(local, mesh=mesh, in_specs=in_specs, out_specs=out_specs, check_vma=False)
```

```python
import functools

import jax
import jax.numpy as jnp
from jax import lax
from jax.experimental import pallas as pl
from jax.experimental.pallas import tpu as pltpu
from jax.sharding import PartitionSpec as P

F32 = jnp.float32
BF16 = jnp.bfloat16
MESH = pl.DeviceIdType.MESH
NVAR = 5
MODES = 125
PAD = 128
ELEM = 1024
PEERS = 32
CUTS = 40
CPAD = 48
SLOTS = 64
BODIES = 6
COVER = 16
TERMS = SLOTS + BODIES * COVER
WIDTH = NVAR * PAD
MBLOCK = 64


def split(value):
    high = value.astype(BF16)
    low = (value - high.astype(F32)).astype(BF16)
    return high, low


def dot(left, right):
    return jnp.dot(left, right, preferred_element_type=F32)


def dot_nt(left, right):
    return lax.dot_general(left, right, (((1,), (1,)), ((), ())), preferred_element_type=F32)


def iota(shape, dim):
    return lax.broadcasted_iota(jnp.int32, shape, dim)


def divmod_const(index, by):
    exact = index.astype(F32)
    whole = jnp.floor((exact + 0.5) * (1.0 / by))
    return whole, exact - whole * by


def parity_of(whole):
    return 1.0 - 2.0 * (whole - 2.0 * jnp.floor(whole * 0.5))


def pad_rows(value):
    zero = jnp.zeros((PAD - value.shape[0], value.shape[1]), value.dtype)
    return jnp.concatenate([value, zero], axis=0)


def pad_lanes(value):
    zero = jnp.zeros((value.shape[0], PAD - value.shape[1]), value.dtype)
    return jnp.concatenate([value, zero], axis=1)


def to_column(row, rows, lanes):
    spread = jnp.broadcast_to(row, (rows, lanes))
    pick = iota((rows, lanes), 0) == iota((rows, lanes), 1)
    return jnp.sum(jnp.where(pick, spread, 0), axis=1, keepdims=True)


def kernel(
    state_hbm,
    old_hbm,
    mass_hbm,
    oper_hbm,
    jac_hbm,
    vol_hbm,
    flux_hbm,
    penalty_hbm,
    owner_hbm,
    elem_hbm,
    holder_hbm,
    points_hbm,
    normals_hbm,
    weights_hbm,
    covered_hbm,
    part,
    returned,
    asked_rows,
    jac,
    vol,
    flux,
    penalty,
    owner,
    elem,
    holder,
    points,
    normals,
    weights,
    covered,
    st,
    so,
    mats,
    uhl,
    across,
    vpad,
    mhh,
    mlo,
    trx,
    cuth,
    cutl,
    ids_row,
    ids_all,
    onehot,
    place,
    p2send,
    p2recv,
    p3send,
    p3recv,
    gbody,
    xh,
    xl,
    tmode,
    bown,
    bgot1,
    bsum1,
    bgot2,
    bsum2,
    bgot3,
    basis,
    tbody,
    load_sem,
    small_sem,
    rim_send,
    rim_recv,
    id_send,
    id_recv,
    p2_send,
    p2_recv,
    p3_send,
    p3_recv,
    b_send,
    b_recv,
):
    me = lax.axis_index("py")
    pz = lax.axis_index("px")
    npx = lax.axis_size("px")

    barrier = pltpu.get_barrier_semaphore()
    above = lax.rem(pz + 1, npx)
    below = lax.rem(pz + npx - 1, npx)

    def greet(r, carry):
        pl.semaphore_signal(
            barrier, inc=1, device_id={"py": lax.rem(me + r, PEERS)}, device_id_type=MESH
        )
        return carry

    lax.fori_loop(1, PEERS, greet, 0)
    has_above = pz < npx - 1
    has_below = pz > 0

    @pl.when(has_above)
    def _():
        pl.semaphore_signal(barrier, inc=1, device_id={"px": above}, device_id_type=MESH)

    @pl.when(has_below)
    def _():
        pl.semaphore_signal(barrier, inc=1, device_id={"px": below}, device_id_type=MESH)


    load_state = pltpu.make_async_copy(state_hbm, st, load_sem.at[0])
    load_old = pltpu.make_async_copy(old_hbm, so, load_sem.at[1])
    load_mass = pltpu.make_async_copy(mass_hbm, mats.at[0], load_sem.at[2])
    load_oper = pltpu.make_async_copy(oper_hbm, mats.at[1], load_sem.at[3])
    pairs = (
        (owner_hbm, owner),
        (elem_hbm, elem),
        (covered_hbm, covered),
        (holder_hbm, holder),
        (points_hbm, points),
        (normals_hbm, normals),
        (weights_hbm, weights),
        (penalty_hbm, penalty),
        (flux_hbm, flux),
        (vol_hbm, vol),
        (jac_hbm, jac),
    )
    smalls = [
        pltpu.make_async_copy(source, target, small_sem.at[i])
        for i, (source, target) in enumerate(pairs)
    ]
    for copy in smalls:
        copy.start()
    for copy in smalls:
        copy.wait()
    load_state.start()
    load_old.start()

    own_row = jnp.broadcast_to(owner[...], (CUTS, CUTS))
    own_col = to_column(owner[...], CUTS, CUTS)
    elem_col = to_column(elem[...], CUTS, CUTS)
    same = own_row == own_col
    row_c, lane_c = iota((CUTS, CUTS), 0), iota((CUTS, CUTS), 1)
    pos_col = jnp.sum(jnp.where(same & (lane_c < row_c), 1, 0), axis=1, keepdims=True)
    pos_row = jnp.sum(jnp.where(same & (row_c < lane_c), 1, 0), axis=0, keepdims=True)
    slot_col = pos_col * PEERS + own_col
    slot_row = pos_row * PEERS + owner[...]
    placed = jnp.where(slot_col == iota((CUTS, PAD), 1), elem_col + 1, 0)
    ids_row[...] = jnp.sum(placed, axis=0, keepdims=True) - 1

    _, spread_lane = divmod_const(iota((CUTS, 256), 1), CPAD)
    spread = jnp.where(spread_lane == iota((CUTS, 256), 0).astype(F32), 1.0, 0.0)
    slots_f = jnp.sum(spread * slot_col.astype(F32), axis=0, keepdims=True)
    lane_v, lane_in = divmod_const(iota((1, 256), 1), CPAD)
    target = jnp.where((lane_in < CUTS) & (lane_v < NVAR), lane_v * SLOTS + slots_f, -1.0)
    place[...] = jnp.where(
        target == iota((NVAR * SLOTS, 256), 0).astype(F32), 1.0, 0.0
    ).astype(BF16)

    cover_lane = iota((COVER, ELEM), 1)
    for b in range(BODIES):
        wanted = to_column(covered[b : b + 1, :], COVER, COVER)
        start = SLOTS + b * COVER
        onehot[start : start + COVER, :] = jnp.where(wanted == cover_lane, 1.0, 0.0).astype(BF16)

    bown[...] = jnp.zeros_like(bown)
    body_row = iota((BODIES, 128), 0)
    held = jnp.zeros((BODIES, 128), jnp.int32)
    for b in range(BODIES):
        held = jnp.where(body_row == b, jnp.where(holder[b] == me, 1, 0), held)
    held = held == 1
    for d in range(3):
        bown[d, 0:BODIES, :] = jnp.where(held, points[:, d, :], 0.0)
        bown[3 + d, 0:BODIES, :] = jnp.where(held, normals[:, d, :], 0.0)
    bown[6, 0:BODIES, :] = jnp.where(held, weights[...], 0.0)

    ri, rf = divmod_const(iota((PAD, PAD), 0), 25)
    ti, tf = divmod_const(iota((64, PAD), 1), 25)
    tr_row = iota((64, PAD), 0)
    tr_lower = tr_row >= 32
    tr_f = jnp.where(tr_lower, tr_row - 32, tr_row).astype(F32)
    trace_op = jnp.where(
        (tf == tr_f) & (ti < 5.0), jnp.where(tr_lower, parity_of(ti), 1.0), 0.0
    ).astype(BF16)
    l64 = lax.rem(iota((PAD, PAD), 1), 64)
    l32 = lax.rem(iota((PAD, PAD), 1), 32)
    expand_op = jnp.where(
        (rf == l32.astype(F32)) & (ri < 5.0), jnp.where(l64 < 32, parity_of(ri), 1.0), 0.0
    ).astype(BF16)

    vpad[...] = jnp.zeros_like(vpad)
    for d in range(3):
        vpad[d, 0:MODES, 0:MODES] = vol[d]
    ci, cf = divmod_const(iota((PAD, PAD), 1), 25)
    inside = (ri < 5.0) & (ci < 5.0)
    own_face = jnp.where(inside & (rf == cf), 1.0 + parity_of(ri) * parity_of(ci), 0.0)

    def build(v, carry):
        rows = pl.ds(pl.multiple_of(v * PAD, PAD), PAD)
        for w in range(NVAR):
            block = jnp.where(v == w, penalty[v], 0.0) * own_face
            for d in range(3):
                block = block - flux[v, d, w] * vpad[d]
            high, low = split(block)
            mhh[rows, w * PAD : (w + 1) * PAD] = high
            mhh[rows, WIDTH + w * PAD : WIDTH + (w + 1) * PAD] = high
            mlo[rows, w * PAD : (w + 1) * PAD] = low
        return carry

    lax.fori_loop(0, NVAR, build, 0)

    nearby = jnp.where(has_above, 1, 0) + jnp.where(has_below, 1, 0)
    pl.semaphore_wait(barrier, PEERS - 1 + nearby)

    def id_copy(r):
        return pltpu.make_async_remote_copy(
            src_ref=ids_row,
            dst_ref=ids_all.at[pl.ds(me, 1), :],
            send_sem=id_send.at[r],
            recv_sem=id_recv,
            device_id={"py": lax.rem(me + r, PEERS)},
            device_id_type=MESH,
        )

    def id_start(r, carry):
        id_copy(r).start()
        return carry

    lax.fori_loop(1, PEERS, id_start, 0, unroll=True)
    pltpu.make_async_copy(ids_row, ids_all.at[pl.ds(me, 1), :], id_recv).start()

    core = lax.rem(me, 2)
    px_in = lax.rem(me // 2, 4)
    py_in = me // 8
    sibling = me + 1 - 2 * core
    body1 = pltpu.make_async_remote_copy(
        src_ref=bown,
        dst_ref=bgot1,
        send_sem=b_send.at[0],
        recv_sem=b_recv.at[0],
        device_id={"py": sibling},
        device_id_type=MESH,
    )
    body1.start()

    load_state.wait()
    load_old.wait()
    load_mass.start()
    load_oper.start()

    def split_state(j, carry):
        cols = pl.ds(pl.multiple_of(j * 256, 256), 256)
        tcols = pl.ds(pl.multiple_of(j * 256 + 128, 128), 256)
        for v in range(NVAR):
            rows = pl.ds(v * PAD, PAD)
            u = pad_rows(st[v, :, cols])
            high, low = split(u)
            uhl[0, rows, cols] = high
            uhl[1, rows, cols] = low
            trx[v, :, tcols] = dot(trace_op, high) + dot(trace_op, low)
            high, low = split(u.T)
            across[0, cols, rows] = high
            across[1, cols, rows] = low
            high, low = split((u - pad_rows(so[v, :, cols])).T)
            across[2, cols, rows] = high
            across[3, cols, rows] = low
        return carry

    lax.fori_loop(0, 4, split_state, 0)
    rim_down = pltpu.make_async_remote_copy(
        src_ref=trx.at[:, 32:64, 128:256],
        dst_ref=trx.at[:, 32:64, 1152:1280],
        send_sem=rim_send.at[0],
        recv_sem=rim_recv.at[0],
        device_id={"px": below},
        device_id_type=MESH,
    )
    rim_up = pltpu.make_async_remote_copy(
        src_ref=trx.at[:, 0:32, 1024:1152],
        dst_ref=trx.at[:, 0:32, 0:128],
        send_sem=rim_send.at[1],
        recv_sem=rim_recv.at[1],
        device_id={"px": above},
        device_id_type=MESH,
    )

    @pl.when(has_below)
    def _():
        rim_down.start()

    @pl.when(has_above)
    def _():
        rim_up.start()


    body1.wait_recv()
    bsum1[...] = bown[...] + bgot1[...]
    body2 = []
    for r in range(1, 4):
        body2.append(
            pltpu.make_async_remote_copy(
                src_ref=bsum1,
                dst_ref=bgot2.at[r - 1],
                send_sem=b_send.at[r],
                recv_sem=b_recv.at[r],
                device_id={"py": py_in * 8 + lax.rem(px_in + r, 4) * 2 + core},
                device_id_type=MESH,
            )
        )
        body2[-1].start()

    pltpu.make_async_copy(ids_all, ids_all, id_recv).wait()
    asked = ids_all[...]
    lane = iota((PEERS, 128), 1)
    elem_lane = iota((PEERS, ELEM), 1)
    for k in range(2):
        wanted = jnp.sum(jnp.where(lane == me + k * PEERS, asked, 0), axis=1, keepdims=True)
        rows = slice(k * PEERS, (k + 1) * PEERS)
        onehot[rows, :] = jnp.where(wanted == elem_lane, 1.0, 0.0).astype(BF16)
    state_high = dot(onehot[...], across[0])
    state_low = dot(onehot[...], across[1])
    state_cols = state_high + state_low
    asking = onehot[0:SLOTS, :]
    change_cols = dot(asking, across[2]) + dot(asking, across[3])
    for k in range(2):
        rows = slice(k * PEERS, (k + 1) * PEERS)
        for v in range(NVAR):
            lanes = slice(v * PAD, (v + 1) * PAD)
            p2send[k * 10 + v] = change_cols[rows, lanes]
            p2send[k * 10 + 5 + v] = state_cols[rows, lanes]
    for v in range(NVAR):
        gbody[v] = state_cols[SLOTS:, v * PAD : (v + 1) * PAD]

    def p2_copy(r):
        peer = lax.rem(me + r, PEERS)
        return pltpu.make_async_remote_copy(
            src_ref=p2send.at[:, pl.ds(peer, 1), :],
            dst_ref=p2recv.at[:, pl.ds(me, 1), :],
            send_sem=p2_send.at[r],
            recv_sem=p2_recv,
            device_id={"py": peer},
            device_id_type=MESH,
        )

    def p2_start(r, carry):
        p2_copy(r).start()
        return carry

    lax.fori_loop(1, PEERS, p2_start, 0, unroll=True)
    pltpu.make_async_copy(
        p2send.at[:, pl.ds(me, 1), :], p2recv.at[:, pl.ds(me, 1), :], p2_recv
    ).start()

    mi, mrest = divmod_const(iota((MODES, 256), 0), 25)
    mj = jnp.floor((mrest + 0.5) * 0.2)
    mk = mrest - mj * 5.0
    mode_weight = 8.0 / ((2.0 * mi + 1.0) * (2.0 * mj + 1.0) * (2.0 * mk + 1.0))

    def volume(j, carry):
        base = pl.multiple_of(j * 256, 256)
        cols = pl.ds(base, 256)
        acc = dot(mhh[...], uhl[:, :, cols].reshape(2 * WIDTH, 256)) + dot(
            mlo[...], uhl[0, :, cols]
        )
        scale = mode_weight * jac[:, cols]
        for v in range(NVAR):
            change = st[v, :, cols] - so[v, :, cols]
            part[v, :, cols] = acc[v * PAD : v * PAD + MODES] + scale * change
        return carry

    lax.fori_loop(0, 4, volume, 0)

    for copy in body2:
        copy.wait_recv()
    bsum2[...] = bsum1[...] + bgot2[0] + bgot2[1] + bgot2[2]
    body3 = []
    for r in range(1, 4):
        body3.append(
            pltpu.make_async_remote_copy(
                src_ref=bsum2,
                dst_ref=bgot3.at[r - 1],
                send_sem=b_send.at[3 + r],
                recv_sem=b_recv.at[3 + r],
                device_id={"py": lax.rem(py_in + r, 4) * 8 + px_in * 2 + core},
                device_id_type=MESH,
            )
        )
        body3[-1].start()

    load_mass.wait()
    load_oper.wait()

    def split_cut(i, carry):
        rows = pl.ds(pl.multiple_of(i * (8 * CUTS), 8 * CUTS), 8 * CUTS)
        for t in range(2):
            high, low = split(pad_lanes(mats[t, pl.ds(i * 8, 8)].reshape(8 * CUTS, MODES)))
            cuth[rows, t * PAD : (t + 1) * PAD] = high
            cutl[rows, t * PAD : (t + 1) * PAD] = low
        return carry

    lax.fori_loop(0, MODES // 8, split_cut, 0)
    whole = MODES // 8 * 8
    for t in range(2):
        tail = pad_lanes(mats[t, whole:MODES].reshape((MODES - whole) * CUTS, MODES))
        zero = jnp.zeros(((PAD - MODES) * CUTS, PAD), F32)
        high, low = split(jnp.concatenate([tail, zero], axis=0))
        cuth[whole * CUTS :, t * PAD : (t + 1) * PAD] = high
        cutl[whole * CUTS :, t * PAD : (t + 1) * PAD] = low

    pltpu.make_async_copy(p2recv, p2recv, p2_recv).wait()
    xh[...] = jnp.zeros_like(xh)
    xl[...] = jnp.zeros_like(xl)
    take = jnp.where(slot_col == iota((CUTS, SLOTS), 1), 1.0, 0.0)
    take = jnp.concatenate([take, jnp.zeros((CPAD - CUTS, SLOTS), F32)], axis=0).astype(BF16)
    for t in range(2):
        for v in range(NVAR):
            got = jnp.concatenate([p2recv[t * 5 + v], p2recv[10 + t * 5 + v]], axis=0)
            high, low = split(-got if t else got)
            rows, lanes = slice(v * CPAD, (v + 1) * CPAD), slice(t * PAD, (t + 1) * PAD)
            xh[rows, lanes] = dot(take, high).astype(BF16)
            xl[rows, lanes] = dot(take, low).astype(BF16)

    _, block_lane = divmod_const(iota((CUTS, 256), 1), CPAD)
    diagonal = jnp.where(block_lane == iota((CUTS, 256), 0).astype(F32), 1.0, 0.0)

    for i in range(PAD // MBLOCK):
        rows = slice(i * MBLOCK * CUTS, (i + 1) * MBLOCK * CUTS)
        high, low = cuth[rows, :], cutl[rows, :]
        all_pairs = dot_nt(high, xh[...]) + (dot_nt(low, xh[...]) + dot_nt(high, xl[...]))
        kept = all_pairs.reshape(MBLOCK, CUTS, 256) * diagonal[None]
        tmode[i * MBLOCK : (i + 1) * MBLOCK, :] = jnp.sum(kept, axis=1)

    high, low = split(tmode[...])
    slotted = dot_nt(place[...], high) + dot_nt(place[...], low)
    p3send[...] = slotted.reshape(2 * NVAR, PEERS, PAD)

    def p3_copy(r):
        peer = lax.rem(me + r, PEERS)
        return pltpu.make_async_remote_copy(
            src_ref=p3send.at[:, pl.ds(peer, 1), :],
            dst_ref=p3recv.at[:, pl.ds(me, 1), :],
            send_sem=p3_send.at[r],
            recv_sem=p3_recv,
            device_id={"py": peer},
            device_id_type=MESH,
        )

    def p3_start(r, carry):
        p3_copy(r).start()
        return carry

    lax.fori_loop(1, PEERS, p3_start, 0, unroll=True)
    pltpu.make_async_copy(
        p3send.at[:, pl.ds(me, 1), :], p3recv.at[:, pl.ds(me, 1), :], p3_recv
    ).start()

    @pl.when(has_above)
    def _():
        rim_down.wait_recv()

    @pl.when(jnp.logical_not(has_above))
    def _():
        trx[:, 32:64, 1152:1280] = jnp.zeros((NVAR, 32, 128), F32)

    @pl.when(has_below)
    def _():
        rim_up.wait_recv()

    @pl.when(jnp.logical_not(has_below))
    def _():
        trx[:, 0:32, 0:128] = jnp.zeros((NVAR, 32, 128), F32)

    def neighbours(j, carry):
        base = pl.multiple_of(j * 256, 256)
        cols = pl.ds(base, 256)
        for v in range(NVAR):
            near = jnp.concatenate(
                [trx[v, 0:32, cols], trx[v, 32:64, pl.ds(pl.multiple_of(base + 256, 256), 256)]],
                axis=0,
            )
            high, low = split(near)
            faces = dot(expand_op, jnp.concatenate([high, low], axis=0))
            part[v, :, cols] = part[v, :, cols] - penalty[v] * faces[0:MODES]
        return carry

    lax.fori_loop(0, 4, neighbours, 0)

    for copy in body3:
        copy.wait_recv()
    bodies = bsum2[...] + bgot3[0] + bgot3[1] + bgot3[2]
    tables = []
    for d in range(3):
        x = bodies[d]
        table = [jnp.ones_like(x), x]
        for n in range(1, 4):
            table.append(((2.0 * n + 1.0) * x * table[n] - n * table[n - 1]) / (n + 1.0))
        tables.append(table)
    for i in range(5):
        for j in range(5):
            pair = tables[0][i] * tables[1][j]
            for k in range(5):
                basis[(i * 5 + j) * 5 + k] = pair * tables[2][k]
    for m in range(MODES, PAD):
        basis[m] = jnp.zeros((8, 128), F32)
    for b in range(BODIES):
        rows = slice(b * COVER, (b + 1) * COVER)
        bh, bl = split(basis[:, b, :])
        gh, gl = split(gbody[:, rows, :].reshape(NVAR * COVER, PAD))
        trace = (dot(gh, bh) + dot(gl, bh) + dot(gh, bl)).reshape(NVAR, COVER, 128)
        nx, ny, nz = bodies[3, b : b + 1], bodies[4, b : b + 1], bodies[5, b : b + 1]
        weight = bodies[6, b : b + 1]
        speed = nx * trace[1] + ny * trace[2] + nz * trace[3]
        wall = jnp.concatenate(
            [
                (speed + 0.5 * trace[0]) * weight,
                nx * trace[4] * weight,
                ny * trace[4] * weight,
                nz * trace[4] * weight,
                1.4 * speed * weight,
            ],
            axis=0,
        )
        wh, wl = split(wall)
        lifted = dot_nt(wh, bh) + dot_nt(wl, bh) + dot_nt(wh, bl)
        tbody[:, rows, :] = -lifted.reshape(NVAR, COVER, PAD)

    for v in range(NVAR):
        high, low = split(tbody[v].T)
        cover = onehot[SLOTS:, :]
        added = dot(high, cover) + dot(low, cover)
        part[v] = part[v] + added[0:MODES]

    def left_before(r, carry):
        id_copy(r).wait_send()
        p2_copy(r).wait_send()
        return carry

    lax.fori_loop(1, PEERS, left_before, 0)
    body1.wait_send()
    for copy in body2 + body3:
        copy.wait_send()

    @pl.when(has_below)
    def _():
        rim_down.wait_send()

    @pl.when(has_above)
    def _():
        rim_up.wait_send()

    asked_rows[...] = onehot[0:SLOTS, :]

    pltpu.make_async_copy(p3recv, p3recv, p3_recv).wait()
    returned[...] = p3recv[...]

    def left(r, carry):
        p3_copy(r).wait_send()
        return carry

    lax.fori_loop(1, PEERS, left, 0)


def add_cut_terms(part, got, asked_rows, out_hbm, total, out_sem):
    rows = jnp.concatenate([asked_rows[...], asked_rows[...]], axis=0)
    stores = []
    for v in range(NVAR):
        terms = jnp.concatenate([got[2 * v], got[2 * v + 1]], axis=0)
        added = dot(jnp.concatenate(split(terms.T), axis=1), rows)
        total[v] = part[v] + added[0:MODES]
        stores.append(pltpu.make_async_copy(total.at[v], out_hbm.at[v], out_sem.at[v]))
        stores[-1].start()
    for copy in stores:
        copy.wait()


def local(
    current_state,
    state_old,
    jacobian,
    volume_operator_list,
    flux_jacobian_list,
    penalty,
    cut_owner,
    cut_element,
    cut_mass,
    cut_operator,
    body_holder_index,
    body_points,
    body_normals,
    body_weights,
    covered,
):
    hbm = pl.BlockSpec(memory_space=pl.ANY)
    dma = pltpu.SemaphoreType.DMA
    vmem = pl.BlockSpec(memory_space=pltpu.VMEM)
    operands = (
        current_state,
        state_old,
        cut_mass.transpose(1, 0, 2),
        cut_operator.transpose(1, 0, 2),
        jacobian.reshape(1, ELEM),
        volume_operator_list,
        flux_jacobian_list.transpose(1, 0, 2),
        penalty,
        cut_owner.reshape(1, CUTS),
        cut_element.reshape(1, CUTS),
        body_holder_index,
        body_points,
        body_normals,
        body_weights,
        covered,
    )
    partial = pl.pallas_call(
        kernel,
        out_shape=(
            pltpu.VMEM((NVAR, MODES, ELEM), F32),
            pltpu.VMEM((2 * NVAR, PEERS, PAD), F32),
            pltpu.VMEM((SLOTS, ELEM), BF16),
        ),
        in_specs=[hbm] * 15,
        out_specs=(vmem, vmem, vmem),
        scratch_shapes=[
            pltpu.VMEM((1, ELEM), F32),
            pltpu.VMEM((3, MODES, MODES), F32),
            pltpu.SMEM((NVAR, 3, NVAR), F32),
            pltpu.SMEM((NVAR,), F32),
            pltpu.VMEM((1, CUTS), jnp.int32),
            pltpu.VMEM((1, CUTS), jnp.int32),
            pltpu.SMEM((BODIES,), jnp.int32),
            pltpu.VMEM((BODIES, 3, 128), F32),
            pltpu.VMEM((BODIES, 3, 128), F32),
            pltpu.VMEM((BODIES, 128), F32),
            pltpu.VMEM((BODIES, COVER), jnp.int32),
            pltpu.VMEM((NVAR, MODES, ELEM), F32),
            pltpu.VMEM((NVAR, MODES, ELEM), F32),
            pltpu.VMEM((2, MODES, CUTS, MODES), F32),
            pltpu.VMEM((2, WIDTH, ELEM), BF16),
            pltpu.VMEM((4, ELEM, WIDTH), BF16),
            pltpu.VMEM((3, PAD, PAD), F32),
            pltpu.VMEM((WIDTH, 2 * WIDTH), BF16),
            pltpu.VMEM((WIDTH, WIDTH), BF16),
            pltpu.VMEM((NVAR, 64, ELEM + 256), F32),
            pltpu.VMEM((PAD * CUTS, 256), BF16),
            pltpu.VMEM((PAD * CUTS, 256), BF16),
            pltpu.VMEM((1, 128), jnp.int32),
            pltpu.VMEM((PEERS, 128), jnp.int32),
            pltpu.VMEM((TERMS, ELEM), BF16),
            pltpu.VMEM((NVAR * SLOTS, 256), BF16),
            pltpu.VMEM((4 * NVAR, PEERS, PAD), F32),
            pltpu.VMEM((4 * NVAR, PEERS, PAD), F32),
            pltpu.VMEM((2 * NVAR, PEERS, PAD), F32),
            pltpu.VMEM((2 * NVAR, PEERS, PAD), F32),
            pltpu.VMEM((NVAR, BODIES * COVER, PAD), F32),
            pltpu.VMEM((256, 256), BF16),
            pltpu.VMEM((256, 256), BF16),
            pltpu.VMEM((PAD, 256), F32),
            pltpu.VMEM((7, 8, 128), F32),
            pltpu.VMEM((7, 8, 128), F32),
            pltpu.VMEM((7, 8, 128), F32),
            pltpu.VMEM((3, 7, 8, 128), F32),
            pltpu.VMEM((7, 8, 128), F32),
            pltpu.VMEM((3, 7, 8, 128), F32),
            pltpu.VMEM((PAD, 8, 128), F32),
            pltpu.VMEM((NVAR, BODIES * COVER, PAD), F32),
            dma((4,)),
            dma((11,)),
            dma((2,)),
            dma((2,)),
            dma((PEERS,)),
            dma,
            dma((PEERS,)),
            dma,
            dma((PEERS,)),
            dma,
            dma((7,)),
            dma((7,)),
        ],
        compiler_params=pltpu.CompilerParams(
            collective_id=0, has_side_effects=True, vmem_limit_bytes=44 * 1024 * 1024
        ),
        name="residual_step",
    )(
        *(pltpu.with_memory_space_constraint(x, pltpu.HBM) for x in operands)
    )
    return pl.pallas_call(
        add_cut_terms,
        out_shape=jax.ShapeDtypeStruct((NVAR, MODES, ELEM), F32),
        in_specs=[vmem] * 3,
        out_specs=hbm,
        scratch_shapes=[pltpu.VMEM((NVAR, MODES, ELEM), F32), dma((NVAR,))],
        compiler_params=pltpu.CompilerParams(vmem_limit_bytes=16 * 1024 * 1024),
        name="add_cut_terms",
    )(*partial)


def solution(mesh):
    in_specs = (
        P(None, None, ("px", "py")),
        P(None, None, ("px", "py")),
        P(("px", "py")),
        P(),
        P(),
        P(),
        P(("px", "py"), None),
        P(("px", "py")),
        P(("px", "py"), None, None),
        P(("px", "py"), None, None),
        P("px"),
        P(("px", "py"), None, None),
        P(("px", "py"), None, None),
        P(("px", "py"), None),
        P(("px", "py"), None),
    )
    out_specs = P(None, None, ("px", "py"))
    return jax.shard_map(local, mesh=mesh, in_specs=in_specs, out_specs=out_specs, check_vma=False)
```

```python
import functools

import jax
import jax.numpy as jnp
from jax import lax
from jax.experimental import pallas as pl
from jax.experimental.pallas import tpu as pltpu
from jax.sharding import PartitionSpec as P

F32 = jnp.float32
BF16 = jnp.bfloat16
MESH = pl.DeviceIdType.MESH
NVAR = 5
MODES = 125
PAD = 128
ELEM = 1024
PEERS = 32
CUTS = 40
CPAD = 48
SLOTS = 64
BODIES = 6
COVER = 16
TERMS = SLOTS + BODIES * COVER
WIDTH = NVAR * PAD
MBLOCK = 64


def split(value):
    high = value.astype(BF16)
    low = (value - high.astype(F32)).astype(BF16)
    return high, low


def dot(left, right):
    return jnp.dot(left, right, preferred_element_type=F32)


def dot_nt(left, right):
    return lax.dot_general(left, right, (((1,), (1,)), ((), ())), preferred_element_type=F32)


def iota(shape, dim):
    return lax.broadcasted_iota(jnp.int32, shape, dim)


def divmod_const(index, by):
    exact = index.astype(F32)
    whole = jnp.floor((exact + 0.5) * (1.0 / by))
    return whole, exact - whole * by


def parity_of(whole):
    return 1.0 - 2.0 * (whole - 2.0 * jnp.floor(whole * 0.5))


def pad_rows(value):
    zero = jnp.zeros((PAD - value.shape[0], value.shape[1]), value.dtype)
    return jnp.concatenate([value, zero], axis=0)


def pad_lanes(value):
    zero = jnp.zeros((value.shape[0], PAD - value.shape[1]), value.dtype)
    return jnp.concatenate([value, zero], axis=1)


def to_column(row, rows, lanes):
    spread = jnp.broadcast_to(row, (rows, lanes))
    pick = iota((rows, lanes), 0) == iota((rows, lanes), 1)
    return jnp.sum(jnp.where(pick, spread, 0), axis=1, keepdims=True)


def kernel(
    state_hbm,
    old_hbm,
    mass_hbm,
    oper_hbm,
    jac_hbm,
    vol_hbm,
    flux_hbm,
    penalty_hbm,
    owner_hbm,
    elem_hbm,
    holder_hbm,
    points_hbm,
    normals_hbm,
    weights_hbm,
    covered_hbm,
    part,
    returned,
    asked_rows,
    jac,
    vol,
    flux,
    penalty,
    owner,
    elem,
    holder,
    points,
    normals,
    weights,
    covered,
    st,
    so,
    mats,
    uhl,
    across,
    vpad,
    mhh,
    mlo,
    trx,
    cuth,
    cutl,
    ids_row,
    ids_all,
    onehot,
    place,
    p2send,
    p2recv,
    p3send,
    p3recv,
    gbody,
    xh,
    xl,
    tmode,
    bown,
    bgot1,
    bsum1,
    bgot2,
    bsum2,
    bgot3,
    basis,
    tbody,
    load_sem,
    small_sem,
    rim_send,
    rim_recv,
    id_send,
    id_recv,
    p2_send,
    p2_recv,
    p3_send,
    p3_recv,
    b_send,
    b_recv,
):
    me = lax.axis_index("py")
    pz = lax.axis_index("px")
    npx = lax.axis_size("px")

    barrier = pltpu.get_barrier_semaphore()
    above = lax.rem(pz + 1, npx)
    below = lax.rem(pz + npx - 1, npx)

    has_above = pz < npx - 1
    has_below = pz > 0

    @pl.when(has_above)
    def _():
        pl.semaphore_signal(barrier, inc=1, device_id={"px": above}, device_id_type=MESH)

    @pl.when(has_below)
    def _():
        pl.semaphore_signal(barrier, inc=1, device_id={"px": below}, device_id_type=MESH)

    def greet(r, carry):
        pl.semaphore_signal(
            barrier, inc=1, device_id={"py": lax.rem(me + r, PEERS)}, device_id_type=MESH
        )
        return carry

    lax.fori_loop(1, PEERS, greet, 0, unroll=True)

    load_state = pltpu.make_async_copy(state_hbm, st, load_sem.at[0])
    load_old = pltpu.make_async_copy(old_hbm, so, load_sem.at[1])
    load_mass = pltpu.make_async_copy(mass_hbm, mats.at[0], load_sem.at[2])
    load_oper = pltpu.make_async_copy(oper_hbm, mats.at[1], load_sem.at[3])
    pairs = (
        (owner_hbm, owner),
        (elem_hbm, elem),
        (covered_hbm, covered),
        (holder_hbm, holder),
        (points_hbm, points),
        (normals_hbm, normals),
        (weights_hbm, weights),
        (penalty_hbm, penalty),
        (flux_hbm, flux),
        (vol_hbm, vol),
        (jac_hbm, jac),
    )
    smalls = [
        pltpu.make_async_copy(source, target, small_sem.at[i])
        for i, (source, target) in enumerate(pairs)
    ]
    for copy in smalls:
        copy.start()
    for copy in smalls:
        copy.wait()
    load_state.start()
    load_old.start()

    own_row = jnp.broadcast_to(owner[...], (CUTS, CUTS))
    own_col = to_column(owner[...], CUTS, CUTS)
    elem_col = to_column(elem[...], CUTS, CUTS)
    same = own_row == own_col
    row_c, lane_c = iota((CUTS, CUTS), 0), iota((CUTS, CUTS), 1)
    pos_col = jnp.sum(jnp.where(same & (lane_c < row_c), 1, 0), axis=1, keepdims=True)
    pos_row = jnp.sum(jnp.where(same & (row_c < lane_c), 1, 0), axis=0, keepdims=True)
    slot_col = pos_col * PEERS + own_col
    slot_row = pos_row * PEERS + owner[...]
    placed = jnp.where(slot_col == iota((CUTS, PAD), 1), elem_col + 1, 0)
    ids_row[...] = jnp.sum(placed, axis=0, keepdims=True) - 1

    _, spread_lane = divmod_const(iota((CUTS, 256), 1), CPAD)
    spread = jnp.where(spread_lane == iota((CUTS, 256), 0).astype(F32), 1.0, 0.0)
    slots_f = jnp.sum(spread * slot_col.astype(F32), axis=0, keepdims=True)
    lane_v, lane_in = divmod_const(iota((1, 256), 1), CPAD)
    target = jnp.where((lane_in < CUTS) & (lane_v < NVAR), lane_v * SLOTS + slots_f, -1.0)
    place[...] = jnp.where(
        target == iota((NVAR * SLOTS, 256), 0).astype(F32), 1.0, 0.0
    ).astype(BF16)

    cover_lane = iota((COVER, ELEM), 1)
    for b in range(BODIES):
        wanted = to_column(covered[b : b + 1, :], COVER, COVER)
        start = SLOTS + b * COVER
        onehot[start : start + COVER, :] = jnp.where(wanted == cover_lane, 1.0, 0.0).astype(BF16)

    bown[...] = jnp.zeros_like(bown)
    body_row = iota((BODIES, 128), 0)
    held = jnp.zeros((BODIES, 128), jnp.int32)
    for b in range(BODIES):
        held = jnp.where(body_row == b, jnp.where(holder[b] == me, 1, 0), held)
    held = held == 1
    for d in range(3):
        bown[d, 0:BODIES, :] = jnp.where(held, points[:, d, :], 0.0)
        bown[3 + d, 0:BODIES, :] = jnp.where(held, normals[:, d, :], 0.0)
    bown[6, 0:BODIES, :] = jnp.where(held, weights[...], 0.0)

    ri, rf = divmod_const(iota((PAD, PAD), 0), 25)
    ti, tf = divmod_const(iota((64, PAD), 1), 25)
    tr_row = iota((64, PAD), 0)
    tr_lower = tr_row >= 32
    tr_f = jnp.where(tr_lower, tr_row - 32, tr_row).astype(F32)
    trace_op = jnp.where(
        (tf == tr_f) & (ti < 5.0), jnp.where(tr_lower, parity_of(ti), 1.0), 0.0
    ).astype(BF16)
    l64 = lax.rem(iota((PAD, PAD), 1), 64)
    l32 = lax.rem(iota((PAD, PAD), 1), 32)
    expand_op = jnp.where(
        (rf == l32.astype(F32)) & (ri < 5.0), jnp.where(l64 < 32, parity_of(ri), 1.0), 0.0
    ).astype(BF16)

    vpad[...] = jnp.zeros_like(vpad)
    for d in range(3):
        vpad[d, 0:MODES, 0:MODES] = vol[d]
    ci, cf = divmod_const(iota((PAD, PAD), 1), 25)
    inside = (ri < 5.0) & (ci < 5.0)
    own_face = jnp.where(inside & (rf == cf), 1.0 + parity_of(ri) * parity_of(ci), 0.0)

    def build(v, carry):
        rows = pl.ds(pl.multiple_of(v * PAD, PAD), PAD)
        for w in range(NVAR):
            block = jnp.where(v == w, penalty[v], 0.0) * own_face
            for d in range(3):
                block = block - flux[v, d, w] * vpad[d]
            high, low = split(block)
            mhh[rows, w * PAD : (w + 1) * PAD] = high
            mhh[rows, WIDTH + w * PAD : WIDTH + (w + 1) * PAD] = high
            mlo[rows, w * PAD : (w + 1) * PAD] = low
        return carry

    lax.fori_loop(0, NVAR, build, 0)

    nearby = jnp.where(has_above, 1, 0) + jnp.where(has_below, 1, 0)
    pl.semaphore_wait(barrier, PEERS - 1 + nearby)

    def id_copy(r):
        return pltpu.make_async_remote_copy(
            src_ref=ids_row,
            dst_ref=ids_all.at[pl.ds(me, 1), :],
            send_sem=id_send.at[r],
            recv_sem=id_recv,
            device_id={"py": lax.rem(me + r, PEERS)},
            device_id_type=MESH,
        )

    def id_start(r, carry):
        id_copy(r).start()
        return carry

    lax.fori_loop(1, PEERS, id_start, 0, unroll=True)
    pltpu.make_async_copy(ids_row, ids_all.at[pl.ds(me, 1), :], id_recv).start()

    core = lax.rem(me, 2)
    px_in = lax.rem(me // 2, 4)
    py_in = me // 8
    sibling = me + 1 - 2 * core
    body1 = pltpu.make_async_remote_copy(
        src_ref=bown,
        dst_ref=bgot1,
        send_sem=b_send.at[0],
        recv_sem=b_recv.at[0],
        device_id={"py": sibling},
        device_id_type=MESH,
    )
    body1.start()

    load_state.wait()
    load_old.wait()
    load_mass.start()
    load_oper.start()

    def split_state(j, carry):
        cols = pl.ds(pl.multiple_of(j * 256, 256), 256)
        tcols = pl.ds(pl.multiple_of(j * 256 + 128, 128), 256)
        for v in range(NVAR):
            rows = pl.ds(v * PAD, PAD)
            u = pad_rows(st[v, :, cols])
            high, low = split(u)
            uhl[0, rows, cols] = high
            uhl[1, rows, cols] = low
            trx[v, :, tcols] = dot(trace_op, high) + dot(trace_op, low)
            high, low = split(u.T)
            across[0, cols, rows] = high
            across[1, cols, rows] = low
            high, low = split((u - pad_rows(so[v, :, cols])).T)
            across[2, cols, rows] = high
            across[3, cols, rows] = low
        return carry

    lax.fori_loop(0, 4, split_state, 0)
    rim_down = pltpu.make_async_remote_copy(
        src_ref=trx.at[:, 32:64, 128:256],
        dst_ref=trx.at[:, 32:64, 1152:1280],
        send_sem=rim_send.at[0],
        recv_sem=rim_recv.at[0],
        device_id={"px": below},
        device_id_type=MESH,
    )
    rim_up = pltpu.make_async_remote_copy(
        src_ref=trx.at[:, 0:32, 1024:1152],
        dst_ref=trx.at[:, 0:32, 0:128],
        send_sem=rim_send.at[1],
        recv_sem=rim_recv.at[1],
        device_id={"px": above},
        device_id_type=MESH,
    )

    @pl.when(has_below)
    def _():
        rim_down.start()

    @pl.when(has_above)
    def _():
        rim_up.start()


    body1.wait_recv()
    bsum1[...] = bown[...] + bgot1[...]
    body2 = []
    for r in range(1, 4):
        body2.append(
            pltpu.make_async_remote_copy(
                src_ref=bsum1,
                dst_ref=bgot2.at[r - 1],
                send_sem=b_send.at[r],
                recv_sem=b_recv.at[r],
                device_id={"py": py_in * 8 + lax.rem(px_in + r, 4) * 2 + core},
                device_id_type=MESH,
            )
        )
        body2[-1].start()

    pltpu.make_async_copy(ids_all, ids_all, id_recv).wait()
    asked = ids_all[...]
    lane = iota((PEERS, 128), 1)
    elem_lane = iota((PEERS, ELEM), 1)
    for k in range(2):
        wanted = jnp.sum(jnp.where(lane == me + k * PEERS, asked, 0), axis=1, keepdims=True)
        rows = slice(k * PEERS, (k + 1) * PEERS)
        onehot[rows, :] = jnp.where(wanted == elem_lane, 1.0, 0.0).astype(BF16)
    state_high = dot(onehot[...], across[0])
    state_low = dot(onehot[...], across[1])
    state_cols = state_high + state_low
    asking = onehot[0:SLOTS, :]
    change_cols = dot(asking, across[2]) + dot(asking, across[3])
    for k in range(2):
        rows = slice(k * PEERS, (k + 1) * PEERS)
        for v in range(NVAR):
            lanes = slice(v * PAD, (v + 1) * PAD)
            p2send[k * 10 + v] = change_cols[rows, lanes]
            p2send[k * 10 + 5 + v] = state_cols[rows, lanes]
    for v in range(NVAR):
        gbody[v] = state_cols[SLOTS:, v * PAD : (v + 1) * PAD]

    def p2_copy(r):
        peer = lax.rem(me + r, PEERS)
        return pltpu.make_async_remote_copy(
            src_ref=p2send.at[:, pl.ds(peer, 1), :],
            dst_ref=p2recv.at[:, pl.ds(me, 1), :],
            send_sem=p2_send.at[r],
            recv_sem=p2_recv,
            device_id={"py": peer},
            device_id_type=MESH,
        )

    def p2_start(r, carry):
        p2_copy(r).start()
        return carry

    lax.fori_loop(1, PEERS, p2_start, 0, unroll=True)
    pltpu.make_async_copy(
        p2send.at[:, pl.ds(me, 1), :], p2recv.at[:, pl.ds(me, 1), :], p2_recv
    ).start()

    mi, mrest = divmod_const(iota((MODES, 256), 0), 25)
    mj = jnp.floor((mrest + 0.5) * 0.2)
    mk = mrest - mj * 5.0
    mode_weight = 8.0 / ((2.0 * mi + 1.0) * (2.0 * mj + 1.0) * (2.0 * mk + 1.0))

    def volume(j, carry):
        base = pl.multiple_of(j * 256, 256)
        cols = pl.ds(base, 256)
        acc = dot(mhh[...], uhl[:, :, cols].reshape(2 * WIDTH, 256)) + dot(
            mlo[...], uhl[0, :, cols]
        )
        scale = mode_weight * jac[:, cols]
        for v in range(NVAR):
            change = st[v, :, cols] - so[v, :, cols]
            part[v, :, cols] = acc[v * PAD : v * PAD + MODES] + scale * change
        return carry

    lax.fori_loop(0, 4, volume, 0)

    for copy in body2:
        copy.wait_recv()
    bsum2[...] = bsum1[...] + bgot2[0] + bgot2[1] + bgot2[2]
    body3 = []
    for r in range(1, 4):
        body3.append(
            pltpu.make_async_remote_copy(
                src_ref=bsum2,
                dst_ref=bgot3.at[r - 1],
                send_sem=b_send.at[3 + r],
                recv_sem=b_recv.at[3 + r],
                device_id={"py": lax.rem(py_in + r, 4) * 8 + px_in * 2 + core},
                device_id_type=MESH,
            )
        )
        body3[-1].start()

    load_mass.wait()
    load_oper.wait()

    def split_cut(i, carry):
        rows = pl.ds(pl.multiple_of(i * (8 * CUTS), 8 * CUTS), 8 * CUTS)
        for t in range(2):
            high, low = split(pad_lanes(mats[t, pl.ds(i * 8, 8)].reshape(8 * CUTS, MODES)))
            cuth[rows, t * PAD : (t + 1) * PAD] = high
            cutl[rows, t * PAD : (t + 1) * PAD] = low
        return carry

    lax.fori_loop(0, MODES // 8, split_cut, 0)
    whole = MODES // 8 * 8
    for t in range(2):
        tail = pad_lanes(mats[t, whole:MODES].reshape((MODES - whole) * CUTS, MODES))
        zero = jnp.zeros(((PAD - MODES) * CUTS, PAD), F32)
        high, low = split(jnp.concatenate([tail, zero], axis=0))
        cuth[whole * CUTS :, t * PAD : (t + 1) * PAD] = high
        cutl[whole * CUTS :, t * PAD : (t + 1) * PAD] = low

    pltpu.make_async_copy(p2recv, p2recv, p2_recv).wait()
    xh[...] = jnp.zeros_like(xh)
    xl[...] = jnp.zeros_like(xl)
    take = jnp.where(slot_col == iota((CUTS, SLOTS), 1), 1.0, 0.0)
    take = jnp.concatenate([take, jnp.zeros((CPAD - CUTS, SLOTS), F32)], axis=0).astype(BF16)
    for t in range(2):
        for v in range(NVAR):
            got = jnp.concatenate([p2recv[t * 5 + v], p2recv[10 + t * 5 + v]], axis=0)
            high, low = split(-got if t else got)
            rows, lanes = slice(v * CPAD, (v + 1) * CPAD), slice(t * PAD, (t + 1) * PAD)
            xh[rows, lanes] = dot(take, high).astype(BF16)
            xl[rows, lanes] = dot(take, low).astype(BF16)

    _, block_lane = divmod_const(iota((CUTS, 256), 1), CPAD)
    diagonal = jnp.where(block_lane == iota((CUTS, 256), 0).astype(F32), 1.0, 0.0)

    for i in range(PAD // MBLOCK):
        rows = slice(i * MBLOCK * CUTS, (i + 1) * MBLOCK * CUTS)
        high, low = cuth[rows, :], cutl[rows, :]
        all_pairs = dot_nt(high, xh[...]) + (dot_nt(low, xh[...]) + dot_nt(high, xl[...]))
        kept = all_pairs.reshape(MBLOCK, CUTS, 256) * diagonal[None]
        tmode[i * MBLOCK : (i + 1) * MBLOCK, :] = jnp.sum(kept, axis=1)

    high, low = split(tmode[...])
    slotted = dot_nt(place[...], high) + dot_nt(place[...], low)
    p3send[...] = slotted.reshape(2 * NVAR, PEERS, PAD)

    def p3_copy(r):
        peer = lax.rem(me + r, PEERS)
        return pltpu.make_async_remote_copy(
            src_ref=p3send.at[:, pl.ds(peer, 1), :],
            dst_ref=p3recv.at[:, pl.ds(me, 1), :],
            send_sem=p3_send.at[r],
            recv_sem=p3_recv,
            device_id={"py": peer},
            device_id_type=MESH,
        )

    def p3_start(r, carry):
        p3_copy(r).start()
        return carry

    lax.fori_loop(1, PEERS, p3_start, 0, unroll=True)
    pltpu.make_async_copy(
        p3send.at[:, pl.ds(me, 1), :], p3recv.at[:, pl.ds(me, 1), :], p3_recv
    ).start()

    @pl.when(has_above)
    def _():
        rim_down.wait_recv()

    @pl.when(jnp.logical_not(has_above))
    def _():
        trx[:, 32:64, 1152:1280] = jnp.zeros((NVAR, 32, 128), F32)

    @pl.when(has_below)
    def _():
        rim_up.wait_recv()

    @pl.when(jnp.logical_not(has_below))
    def _():
        trx[:, 0:32, 0:128] = jnp.zeros((NVAR, 32, 128), F32)

    def neighbours(j, carry):
        base = pl.multiple_of(j * 256, 256)
        cols = pl.ds(base, 256)
        for v in range(NVAR):
            near = jnp.concatenate(
                [trx[v, 0:32, cols], trx[v, 32:64, pl.ds(pl.multiple_of(base + 256, 256), 256)]],
                axis=0,
            )
            high, low = split(near)
            faces = dot(expand_op, jnp.concatenate([high, low], axis=0))
            part[v, :, cols] = part[v, :, cols] - penalty[v] * faces[0:MODES]
        return carry

    lax.fori_loop(0, 4, neighbours, 0)

    for copy in body3:
        copy.wait_recv()
    bodies = bsum2[...] + bgot3[0] + bgot3[1] + bgot3[2]
    tables = []
    for d in range(3):
        x = bodies[d]
        table = [jnp.ones_like(x), x]
        for n in range(1, 4):
            table.append(((2.0 * n + 1.0) * x * table[n] - n * table[n - 1]) / (n + 1.0))
        tables.append(table)
    for i in range(5):
        for j in range(5):
            pair = tables[0][i] * tables[1][j]
            for k in range(5):
                basis[(i * 5 + j) * 5 + k] = pair * tables[2][k]
    for m in range(MODES, PAD):
        basis[m] = jnp.zeros((8, 128), F32)
    for b in range(BODIES):
        rows = slice(b * COVER, (b + 1) * COVER)
        bh, bl = split(basis[:, b, :])
        gh, gl = split(gbody[:, rows, :].reshape(NVAR * COVER, PAD))
        trace = (dot(gh, bh) + dot(gl, bh) + dot(gh, bl)).reshape(NVAR, COVER, 128)
        nx, ny, nz = bodies[3, b : b + 1], bodies[4, b : b + 1], bodies[5, b : b + 1]
        weight = bodies[6, b : b + 1]
        speed = nx * trace[1] + ny * trace[2] + nz * trace[3]
        wall = jnp.concatenate(
            [
                (speed + 0.5 * trace[0]) * weight,
                nx * trace[4] * weight,
                ny * trace[4] * weight,
                nz * trace[4] * weight,
                1.4 * speed * weight,
            ],
            axis=0,
        )
        wh, wl = split(wall)
        lifted = dot_nt(wh, bh) + dot_nt(wl, bh) + dot_nt(wh, bl)
        tbody[:, rows, :] = -lifted.reshape(NVAR, COVER, PAD)

    for v in range(NVAR):
        high, low = split(tbody[v].T)
        cover = onehot[SLOTS:, :]
        added = dot(high, cover) + dot(low, cover)
        part[v] = part[v] + added[0:MODES]

    def left_before(r, carry):
        id_copy(r).wait_send()
        p2_copy(r).wait_send()
        return carry

    lax.fori_loop(1, PEERS, left_before, 0)
    body1.wait_send()
    for copy in body2 + body3:
        copy.wait_send()

    @pl.when(has_below)
    def _():
        rim_down.wait_send()

    @pl.when(has_above)
    def _():
        rim_up.wait_send()

    asked_rows[...] = onehot[0:SLOTS, :]

    pltpu.make_async_copy(p3recv, p3recv, p3_recv).wait()
    returned[...] = p3recv[...]

    def left(r, carry):
        p3_copy(r).wait_send()
        return carry

    lax.fori_loop(1, PEERS, left, 0, unroll=True)


def add_cut_terms(part, got, asked_rows, out_hbm, total, out_sem):
    rows = jnp.concatenate([asked_rows[...], asked_rows[...]], axis=0)
    stores = []
    for v in range(NVAR):
        terms = jnp.concatenate([got[2 * v], got[2 * v + 1]], axis=0)
        added = dot(jnp.concatenate(split(terms.T), axis=1), rows)
        total[v] = part[v] + added[0:MODES]
        stores.append(pltpu.make_async_copy(total.at[v], out_hbm.at[v], out_sem.at[v]))
        stores[-1].start()
    for copy in stores:
        copy.wait()


def local(
    current_state,
    state_old,
    jacobian,
    volume_operator_list,
    flux_jacobian_list,
    penalty,
    cut_owner,
    cut_element,
    cut_mass,
    cut_operator,
    body_holder_index,
    body_points,
    body_normals,
    body_weights,
    covered,
):
    hbm = pl.BlockSpec(memory_space=pl.ANY)
    dma = pltpu.SemaphoreType.DMA
    vmem = pl.BlockSpec(memory_space=pltpu.VMEM)
    operands = (
        current_state,
        state_old,
        cut_mass.transpose(1, 0, 2),
        cut_operator.transpose(1, 0, 2),
        jacobian.reshape(1, ELEM),
        volume_operator_list,
        flux_jacobian_list.transpose(1, 0, 2),
        penalty,
        cut_owner.reshape(1, CUTS),
        cut_element.reshape(1, CUTS),
        body_holder_index,
        body_points,
        body_normals,
        body_weights,
        covered,
    )
    partial = pl.pallas_call(
        kernel,
        out_shape=(
            pltpu.VMEM((NVAR, MODES, ELEM), F32),
            pltpu.VMEM((2 * NVAR, PEERS, PAD), F32),
            pltpu.VMEM((SLOTS, ELEM), BF16),
        ),
        in_specs=[hbm] * 15,
        out_specs=(vmem, vmem, vmem),
        scratch_shapes=[
            pltpu.VMEM((1, ELEM), F32),
            pltpu.VMEM((3, MODES, MODES), F32),
            pltpu.SMEM((NVAR, 3, NVAR), F32),
            pltpu.SMEM((NVAR,), F32),
            pltpu.VMEM((1, CUTS), jnp.int32),
            pltpu.VMEM((1, CUTS), jnp.int32),
            pltpu.SMEM((BODIES,), jnp.int32),
            pltpu.VMEM((BODIES, 3, 128), F32),
            pltpu.VMEM((BODIES, 3, 128), F32),
            pltpu.VMEM((BODIES, 128), F32),
            pltpu.VMEM((BODIES, COVER), jnp.int32),
            pltpu.VMEM((NVAR, MODES, ELEM), F32),
            pltpu.VMEM((NVAR, MODES, ELEM), F32),
            pltpu.VMEM((2, MODES, CUTS, MODES), F32),
            pltpu.VMEM((2, WIDTH, ELEM), BF16),
            pltpu.VMEM((4, ELEM, WIDTH), BF16),
            pltpu.VMEM((3, PAD, PAD), F32),
            pltpu.VMEM((WIDTH, 2 * WIDTH), BF16),
            pltpu.VMEM((WIDTH, WIDTH), BF16),
            pltpu.VMEM((NVAR, 64, ELEM + 256), F32),
            pltpu.VMEM((PAD * CUTS, 256), BF16),
            pltpu.VMEM((PAD * CUTS, 256), BF16),
            pltpu.VMEM((1, 128), jnp.int32),
            pltpu.VMEM((PEERS, 128), jnp.int32),
            pltpu.VMEM((TERMS, ELEM), BF16),
            pltpu.VMEM((NVAR * SLOTS, 256), BF16),
            pltpu.VMEM((4 * NVAR, PEERS, PAD), F32),
            pltpu.VMEM((4 * NVAR, PEERS, PAD), F32),
            pltpu.VMEM((2 * NVAR, PEERS, PAD), F32),
            pltpu.VMEM((2 * NVAR, PEERS, PAD), F32),
            pltpu.VMEM((NVAR, BODIES * COVER, PAD), F32),
            pltpu.VMEM((256, 256), BF16),
            pltpu.VMEM((256, 256), BF16),
            pltpu.VMEM((PAD, 256), F32),
            pltpu.VMEM((7, 8, 128), F32),
            pltpu.VMEM((7, 8, 128), F32),
            pltpu.VMEM((7, 8, 128), F32),
            pltpu.VMEM((3, 7, 8, 128), F32),
            pltpu.VMEM((7, 8, 128), F32),
            pltpu.VMEM((3, 7, 8, 128), F32),
            pltpu.VMEM((PAD, 8, 128), F32),
            pltpu.VMEM((NVAR, BODIES * COVER, PAD), F32),
            dma((4,)),
            dma((11,)),
            dma((2,)),
            dma((2,)),
            dma((PEERS,)),
            dma,
            dma((PEERS,)),
            dma,
            dma((PEERS,)),
            dma,
            dma((7,)),
            dma((7,)),
        ],
        compiler_params=pltpu.CompilerParams(
            collective_id=0, has_side_effects=True, vmem_limit_bytes=44 * 1024 * 1024
        ),
        name="residual_step",
    )(
        *(pltpu.with_memory_space_constraint(x, pltpu.HBM) for x in operands)
    )
    return pl.pallas_call(
        add_cut_terms,
        out_shape=jax.ShapeDtypeStruct((NVAR, MODES, ELEM), F32),
        in_specs=[vmem] * 3,
        out_specs=hbm,
        scratch_shapes=[pltpu.VMEM((NVAR, MODES, ELEM), F32), dma((NVAR,))],
        compiler_params=pltpu.CompilerParams(vmem_limit_bytes=16 * 1024 * 1024),
        name="add_cut_terms",
    )(*partial)


def solution(mesh):
    in_specs = (
        P(None, None, ("px", "py")),
        P(None, None, ("px", "py")),
        P(("px", "py")),
        P(),
        P(),
        P(),
        P(("px", "py"), None),
        P(("px", "py")),
        P(("px", "py"), None, None),
        P(("px", "py"), None, None),
        P("px"),
        P(("px", "py"), None, None),
        P(("px", "py"), None, None),
        P(("px", "py"), None),
        P(("px", "py"), None),
    )
    out_specs = P(None, None, ("px", "py"))
    return jax.shard_map(local, mesh=mesh, in_specs=in_specs, out_specs=out_specs, check_vma=False)
```
